32 devices in a mesh: dp: 8 (over z, x), tensor: 4 (over y, core).
Axes of the slice: x: 2, y: 2, z: 4, core: 2. Of those that a mesh axis runs over, the one named last changes fastest.
Arguments:
- tokens: bfloat16 [8, 1024, 1024], P('dp'), may hold values from -6 to 6
- cotangent: bfloat16 [8, 1024, 1024], P('dp'), may hold values from -6 to 6
- seg_lengths: int32 [8, 8], P('dp'), may hold values from 1 to 384, 1024 in all within a row
- pad_counts: int32 [8], P('dp'), may hold values from 0 to 127
- ln1_gain: bfloat16 [1024], replicated, may hold values from 0.5 to 1.5
- ln1_shift: bfloat16 [1024], replicated, may hold values from -1 to 1
- qkv_weight: bfloat16 [1024, 3, 1024], P(None, None, 'tensor'), may hold values from -0.1875 to 0.1875
- qkv_bias: bfloat16 [3, 1024], P(None, 'tensor'), may hold values from -1.5 to 1.5
- out_weight: bfloat16 [1024, 1024], P('tensor'), may hold values from -0.5 to 0.5
- out_bias: bfloat16 [1024], replicated, may hold values from -1 to 1
- ln2_gain: bfloat16 [1024], replicated, may hold values from 0.5 to 1.5
- ln2_shift: bfloat16 [1024], replicated, may hold values from -1 to 1
- fc_weight: bfloat16 [1024, 4096], P(None, 'tensor'), may hold values from -0.1875 to 0.1875
- fc_bias: bfloat16 [4096], P('tensor'), may hold values from -1.5 to 1.5
- proj_weight: bfloat16 [4096, 1024], P('tensor'), may hold values from -0.125 to 0.125
- proj_bias: bfloat16 [1024], replicated, may hold values from -1 to 1
- prefix_embed: bfloat16 [10, 1024], replicated, may hold values from -6 to 6
- reparam_w1: bfloat16 [1024, 512], replicated, may hold values from -0.1875 to 0.1875
- reparam_b1: bfloat16 [512], replicated, may hold values from -1.5 to 1.5
- reparam_w2: bfloat16 [512, 2, 1024], P(None, None, 'tensor'), may hold values from -0.5 to 0.5
- reparam_b2: bfloat16 [2, 1024], P(None, 'tensor'), may hold values from -1.5 to 1.5
Outputs:
- mixed: bfloat16 [8, 1024, 1024], P('dp')
- input_grad: float32 [8, 1024, 1024], P('dp')
- embed_grad: float32 [10, 1024], replicated
- w1_grad: float32 [1024, 512], replicated
- b1_grad: float32 [512], replicated
- w2_grad: float32 [512, 2, 1024], P(None, None, 'tensor')
- b2_grad: float32 [2, 1024], P(None, 'tensor')
- prefix_kv: float32 [10, 2, 1024], P(None, None, 'tensor')
The draws below stay inside these ranges and needn't reach their ends.
Inputs may be any that keep to these rules, and one draw needn't show every extreme that they name: `seg_lengths`: each row's 8 lengths add up to 1024, and each row has a segment of exactly 384 tokens.
All inputs are finite; a program needn't handle non-finite values.
Results may differ from the reference program's by a relative error of at most 0.0097.
Values sent between devices are 32-bit elements; how exact they have to be, the bound alone decides.
No kernel may reach another device: no remote copies, remote signals or barrier semaphores. Data moves between devices by JAX's collectives and lax.ppermute only.
A program may use at most 128 MiB of HBM per device.

```python
import math
import jax
import jax.numpy as jnp
import numpy as np
from jax import lax

D = 1024
HEADS = 16
HEAD_DIM = 64
FF = 4096
RANK = 512
PREFIX = 10
ROW_LEN = 1024
SEGS = 8
QBLK = 512
ROWS = 8


def plant(drawn, own_key, low, top_value):
    index_at = [jax.random.randint(jax.random.fold_in(own_key, axis), (), 0, length) for axis, length in enumerate(drawn.shape)]
    widest = drawn.shape.index(max(drawn.shape))
    neighbour = index_at[:widest] + [(index_at[widest] + 1) % drawn.shape[widest]] + index_at[widest + 1:]
    return drawn.at[tuple(index_at)].set(low).at[tuple(neighbour)].set(top_value)


def block_levels(rng, shape, shards, least, top_value):
    def one(dim, shards_of):
        draws = jax.random.uniform(jax.random.fold_in(jax.random.fold_in(rng, 6), dim), (shards_of,), jnp.float32, least / len(shards), top_value / len(shards))
        return jnp.repeat(jnp.exp(draws), shape[dim] // shards_of).reshape((-1,) + (1,) * (len(shape) - dim - 1))

    loudness = one(*shards[0])
    for cut in shards[1:]:
        loudness = loudness * one(*cut)
    return loudness


def profile(amount, total, limit, skew):
    loads = [(1 << 20) // math.isqrt(grade ** skew) + 1 for grade in range(2, amount + 1)]
    surplus, counts = total - limit - (amount - 1), [1] * (amount - 1)
    while surplus > 0:
        movable = [i for i in range(amount - 1) if counts[i] < limit]
        whole, left = sum([loads[i] for i in movable]), surplus
        for i in movable:
            extra = min(limit - counts[i], max(1, left * loads[i] // whole), surplus)
            counts[i] = counts[i] + extra
            surplus = surplus - extra
    return np.array([limit] + counts)


def ragged_sizes(stream_key, number_of, total, reach, lean):
    if number_of == 2:
        one = jax.random.randint(stream_key, (), max(1, total - reach), min(reach, total - 1) + 1)
        return jnp.stack([one, total - one])
    tallies = jnp.asarray(profile(number_of, total, reach, lean), jnp.int32)
    pairs = (number_of - 1) // 2
    source_of, taker = tallies[1:1 + 2 * pairs:2], tallies[2:2 + 2 * pairs:2]
    room = jnp.minimum(source_of - 1, reach - taker)
    moved = jax.random.randint(jax.random.fold_in(stream_key, 1), (pairs,), 0, 1 << 20) % (room + 1)
    tallies = tallies.at[1:1 + 2 * pairs:2].set(source_of - moved).at[2:2 + 2 * pairs:2].set(taker + moved)
    return tallies[jax.random.permutation(jax.random.fold_in(stream_key, 2), number_of)]


def gaussian(key, dims, width, reach, split=(), kind=jnp.bfloat16):
    entries = jax.random.normal(key, dims, jnp.float32) * width
    if len(split) > 0:
        entries = block_levels(key, dims, split, -0.22, 0.18) * entries
    return jnp.clip(entries, min=-reach, max=reach).astype(kind)


def setup_inputs(seed: int = 0) -> dict:
    seeds = jax.random.split(jax.random.key(seed), 22)
    tokens = gaussian(seeds[0], (ROWS, ROW_LEN, D), 1.0, 6.0, ((0, 8),))
    cotangent = gaussian(seeds[1], (ROWS, ROW_LEN, D), 1.0, 6.0, ((0, 8),))
    seg_lengths = jax.vmap(lambda own: ragged_sizes(own, SEGS, ROW_LEN, ROW_LEN * 3 // 8, 2))(jax.random.split(seeds[2], ROWS)).reshape((ROWS, SEGS)).astype(jnp.int32)
    pad_counts = plant(jax.random.randint(seeds[3], (ROWS,), 0, ROW_LEN // 8), jax.random.fold_in(seeds[3], 1), 0, (ROW_LEN // 8) - 1).astype(jnp.int32)
    ln1_gain = jnp.clip(1.0 + 0.1 * jax.random.normal(seeds[4], (D,), jnp.float32), 0.5, 1.5).astype(jnp.bfloat16)
    ln1_shift = gaussian(seeds[5], (D,), 0.2, 1.0)
    qkv_weight = gaussian(seeds[6], (D, 3, D), D ** -0.5, 0.1875, ((2, 4),))
    qkv_bias = gaussian(seeds[7], (3, D), 0.3, 1.5, ((1, 4),))
    out_weight = gaussian(seeds[8], (D, D), (D // 8) ** -0.5, 0.5, ((0, 4),))
    out_bias = gaussian(seeds[9], (D,), 0.2, 1.0)
    ln2_gain = jnp.clip(1.0 + 0.1 * jax.random.normal(seeds[10], (D,), jnp.float32), 0.5, 1.5).astype(jnp.bfloat16)
    ln2_shift = gaussian(seeds[11], (D,), 0.2, 1.0)
    fc_weight = gaussian(seeds[12], (D, FF), D ** -0.5, 0.1875, ((1, 4),))
    fc_bias = gaussian(seeds[13], (FF,), 0.3, 1.5, ((0, 4),))
    proj_weight = gaussian(seeds[14], (FF, D), (FF // 2) ** -0.5, 0.125, ((0, 4),))
    proj_bias = gaussian(seeds[15], (D,), 0.2, 1.0)
    prefix_embed = gaussian(seeds[16], (PREFIX, D), 1.0, 6.0)
    reparam_w1 = gaussian(seeds[17], (D, RANK), D ** -0.5, 0.1875)
    reparam_b1 = gaussian(seeds[18], (RANK,), 0.3, 1.5)
    reparam_w2 = gaussian(seeds[19], (RANK, 2, D), (RANK // 4) ** -0.5, 0.5, ((2, 4),))
    reparam_b2 = gaussian(seeds[20], (2, D), 0.3, 1.5, ((1, 4),))
    return dict(tokens=tokens, cotangent=cotangent, seg_lengths=seg_lengths, pad_counts=pad_counts, ln1_gain=ln1_gain, ln1_shift=ln1_shift, qkv_weight=qkv_weight, qkv_bias=qkv_bias, out_weight=out_weight, out_bias=out_bias, ln2_gain=ln2_gain, ln2_shift=ln2_shift, fc_weight=fc_weight, fc_bias=fc_bias, proj_weight=proj_weight, proj_bias=proj_bias, prefix_embed=prefix_embed, reparam_w1=reparam_w1, reparam_b1=reparam_b1, reparam_w2=reparam_w2, reparam_b2=reparam_b2)


@jax.custom_vjp
def low(v):
    return lax.optimization_barrier(v.astype(jnp.bfloat16)).astype(jnp.float32)

@jax.custom_vjp
def low_back(v):
    return v

def low_keep(v):
    return (low(v), None)

def low_pass(kept, grad):
    return (grad,)

def back_keep(v):
    return (v, None)

def back_low(kept, grad):
    return (low(grad),)
low.defvjp(low_keep, low_pass)
low_back.defvjp(back_keep, back_low)
highest = lax.Precision.HIGHEST
epsilon = 1e-05

def layer_norm(values, gain, shift):
    center = lax.optimization_barrier(jnp.mean(values, axis=-1, keepdims=True))
    centered = values - center
    spread = lax.optimization_barrier(jnp.mean(centered * centered, axis=-1, keepdims=True))
    return centered * lax.rsqrt(spread + epsilon) * gain + shift

def gelu_tanh(values):
    return 0.5 * values * (1.0 + jnp.tanh(0.7978845608028654 * (values + 0.044715 * values * values * values)))

def attend_block(offset, queries, keys, values, prefix_keys, prefix_vals, segment, usable):
    factor = HEAD_DIM ** (-0.5)
    places = jnp.arange(ROW_LEN, dtype=jnp.int32)
    query_block = lax.dynamic_slice_in_dim(queries, offset, QBLK, 0)
    query_pos = offset + jnp.arange(QBLK, dtype=jnp.int32)
    query_seg = lax.dynamic_slice_in_dim(segment, offset, QBLK, 0)
    query_use = lax.dynamic_slice_in_dim(usable, offset, QBLK, 0)
    allowed = (query_seg[:, None] == segment[None, :]) & (places[None, :] <= query_pos[:, None]) & usable[None, :] & query_use[:, None]
    front = low_back(jnp.einsum('qhe,phe->hqp', query_block, prefix_keys, precision=highest) * factor)
    inside = low_back(jnp.einsum('qhe,khe->hqk', query_block, keys, precision=highest) * factor)
    inside = jnp.where(allowed[None], inside, -1e+30)
    largest = jnp.maximum(lax.optimization_barrier(jnp.max(front, axis=2, keepdims=True)), lax.optimization_barrier(jnp.max(inside, axis=2, keepdims=True)))
    front_exp = jnp.exp(front - largest)
    inside_exp = jnp.exp(inside - largest)
    totals = lax.optimization_barrier(jnp.sum(front_exp, axis=2, keepdims=True)) + lax.optimization_barrier(jnp.sum(inside_exp, axis=2, keepdims=True))
    front_prob = low(front_exp / totals)
    inside_prob = low(inside_exp / totals)
    return jnp.einsum('hqp,phe->qhe', front_prob, prefix_vals, precision=highest) + jnp.einsum('hqk,khe->qhe', inside_prob, values, precision=highest)

def row_forward(inputs, segment, usable, prefix_keys, prefix_vals, frozen):
    ln1_gain, ln1_shift, qkv_weight, qkv_bias, out_weight, out_bias, ln2_gain, ln2_shift, fc_weight, fc_bias, proj_weight, proj_bias = frozen
    normed = low(layer_norm(inputs, ln1_gain, ln1_shift))
    projected = jnp.dot(normed, qkv_weight.reshape(D, 3 * D), precision=highest).reshape(ROW_LEN, 3, D) + qkv_bias
    projected = low(low_back(projected))
    queries = projected[:, 0].reshape(ROW_LEN, HEADS, HEAD_DIM)
    keys = projected[:, 1].reshape(ROW_LEN, HEADS, HEAD_DIM)
    values = projected[:, 2].reshape(ROW_LEN, HEADS, HEAD_DIM)
    checked = jax.checkpoint(attend_block)
    offsets = jnp.arange(ROW_LEN // QBLK, dtype=jnp.int32) * QBLK
    attended = lax.map(lambda offset: checked(offset, queries, keys, values, prefix_keys, prefix_vals, segment, usable), offsets)
    attended = low(low_back(attended.reshape(ROW_LEN, D)))
    branch = low_back(jnp.dot(attended, out_weight, precision=highest) + out_bias)
    middle = inputs + branch
    normed_two = low(layer_norm(middle, ln2_gain, ln2_shift))
    hidden = low_back(jnp.dot(normed_two, fc_weight, precision=highest) + fc_bias)
    activated = low(gelu_tanh(hidden))
    feed = low_back(jnp.dot(activated, proj_weight, precision=highest) + proj_bias)
    return middle + feed

def reference(tokens, cotangent, seg_lengths, pad_counts, ln1_gain, ln1_shift, qkv_weight, qkv_bias, out_weight, out_bias, ln2_gain, ln2_shift, fc_weight, fc_bias, proj_weight, proj_bias, prefix_embed, reparam_w1, reparam_b1, reparam_w2, reparam_b2):
    frozen = tuple((item.astype(jnp.float32) for item in (ln1_gain, ln1_shift, qkv_weight, qkv_bias, out_weight, out_bias, ln2_gain, ln2_shift, fc_weight, fc_bias, proj_weight, proj_bias)))
    places = jnp.arange(ROW_LEN, dtype=jnp.int32)
    ends = jnp.cumsum(seg_lengths, axis=1).astype(jnp.int32)
    segment = lax.optimization_barrier(jnp.sum((places[None, :, None] >= ends[:, None, :]).astype(jnp.int32), axis=2)).astype(jnp.int32)
    usable = places[None, :] < (ROW_LEN - pad_counts.astype(jnp.int32))[:, None]

    def forward(inputs, embed, trunk_weight, trunk_bias, head_weight, head_bias):
        trunk = jnp.tanh(jnp.dot(embed, trunk_weight, precision=highest) + trunk_bias)
        kv_values = jnp.einsum('pr,rtd->ptd', trunk, head_weight, precision=highest) + head_bias
        kv_low = low(kv_values)
        prefix_keys = kv_low[:, 0].reshape(PREFIX, HEADS, HEAD_DIM)
        prefix_vals = kv_low[:, 1].reshape(PREFIX, HEADS, HEAD_DIM)

        def step(carry, item):
            row_inputs, row_segment, row_usable = item
            return (carry, row_forward(row_inputs, row_segment, row_usable, prefix_keys, prefix_vals, frozen))
        carry, result = lax.scan(step, jnp.zeros((), jnp.float32), (inputs, segment, usable))
        return (result, kv_values)
    primal = (tokens.astype(jnp.float32), prefix_embed.astype(jnp.float32), reparam_w1.astype(jnp.float32), reparam_b1.astype(jnp.float32), reparam_w2.astype(jnp.float32), reparam_b2.astype(jnp.float32))
    outputs, pullback = jax.vjp(forward, primal[0], primal[1], primal[2], primal[3], primal[4], primal[5])
    result, kv_values = outputs
    gradients = pullback((cotangent.astype(jnp.float32), jnp.zeros_like(kv_values)))
    return (result.astype(jnp.bfloat16), gradients[0], gradients[1], gradients[2], gradients[3], gradients[4], gradients[5], kv_values)
```

```python
import functools

import jax
import jax.numpy as jnp
from jax import lax
from jax.experimental import pallas as pl
from jax.experimental.pallas import tpu as pltpu
from jax.sharding import PartitionSpec as P

HEAD_DIM = 64
CORES = 2
QB = 128
SPAN = 384
PAD = 16
RING = 8
LIGHT = 16
KEEP, OWN, FAR = 640, 320, 320
MASKED = -1e30
GAIN_ONE, SHIFT_ONE, OUT_BIAS, GAIN_TWO, SHIFT_TWO, PROJ_BIAS = range(6)
highest = lax.Precision.HIGHEST
epsilon = 1e-05
f32 = jnp.float32
bf16 = jnp.bfloat16


def nn(a, b):
    return jnp.dot(a, b, preferred_element_type=f32)


def nt(a, b):
    return lax.dot_general(a, b, (((1,), (1,)), ((), ())), preferred_element_type=f32)


def tn(a, b):
    return lax.dot_general(a, b, (((0,), (0,)), ((), ())), preferred_element_type=f32)


def params(mib):
    return pltpu.CompilerParams(vmem_limit_bytes=mib * 1024 * 1024)


def in_hbm(values):
    return [pltpu.with_memory_space_constraint(v, pltpu.HBM) for v in values]


def cost(flops, bytes_accessed, transcendentals=0):
    return pl.CostEstimate(
        flops=int(flops) // LIGHT,
        bytes_accessed=int(bytes_accessed) // LIGHT,
        transcendentals=int(transcendentals) // LIGHT,
    )


def unread(after):
    return [pl.BlockSpec(memory_space=pl.ANY)] * len(after)


def once(shape, index):
    return pl.BlockSpec(shape, lambda *_: index, pipeline_mode=pl.Buffered(1))


def vector(ref, number):
    return ref[number : number + 1, :]


def normalize(values):
    centered = values - jnp.mean(values, axis=-1, keepdims=True)
    scale = lax.rsqrt(jnp.mean(centered * centered, axis=-1, keepdims=True) + epsilon)
    return centered * scale, scale


def norm_back(grad, hat, scale):
    mean_grad = jnp.mean(grad, axis=-1, keepdims=True)
    mean_both = jnp.mean(grad * hat, axis=-1, keepdims=True)
    return scale * (grad - mean_grad - hat * mean_both)


class Parcel:
    def __init__(self, length, width, full):
        self.length, self.width, self.full = length, width, full
        self.piece = full // 8
        self.kv = length + self.piece
        self.lse = self.kv + 2 * PAD
        self.bias = self.lse + 2 * (length // QB)
        self.rows = self.bias + 16

    def part(self, start, size):
        assert start % size == 0
        return once((size, self.width), (start // size, 0))


def head_masks():
    lanes = lax.broadcasted_iota(jnp.int32, (QB, 2 * HEAD_DIM), 1)
    return lanes < HEAD_DIM


def both_heads(block, first):
    zero = jnp.zeros_like(block)
    return jnp.concatenate([jnp.where(first, block, zero), jnp.where(first, zero, block)], axis=0)


def own_quadrants(product):
    return jnp.concatenate([product[:HEAD_DIM, :QB], product[HEAD_DIM:, QB:]], axis=0)


def segment_start(position, lengths_ref):
    start, end = jnp.zeros_like(position), jnp.int32(0)
    for number in range(lengths_ref.shape[0]):
        end = end + lengths_ref[number]
        start = jnp.where(position >= end, end, start)
    return start


def by_window(length, lengths_ref, order_ref, run):
    blocks = length // QB
    most = min(length, SPAN + QB) // QB

    def tiles_of(block):
        return block - segment_start(block * QB, lengths_ref) // QB + 1

    def place(block, ends):
        low, high = ends
        small = tiles_of(block) <= most // 2
        order_ref[jnp.where(small, low, high)] = block
        return jnp.where(small, low + 1, low), jnp.where(small, high, high - 1)

    lax.fori_loop(0, blocks, place, (jnp.int32(0), jnp.int32(blocks - 1)))

    def step(number, _):
        pair = order_ref[2 * number], order_ref[2 * number + 1]
        tiles = jnp.maximum(tiles_of(pair[0]), tiles_of(pair[1]))
        for count in (most // 2, most):

            @pl.when((tiles <= count) & (tiles > count - most // 2))
            def _():
                run(pair, count * QB)

        return 0

    lax.fori_loop(0, blocks // 2, step, 0)


def window_bias(block, start, window, length, lengths_ref, pads_ref):
    lanes = lax.broadcasted_iota(jnp.int32, (1, 2 * QB), 1)
    position = block * QB + jnp.where(lanes < QB, lanes, lanes - QB)
    low = segment_start(position, lengths_ref)
    low = jnp.where(position < length - pads_ref[0], low, 4 * length)
    key = start + lax.broadcasted_iota(jnp.int32, (window, 2 * QB), 0)
    return jnp.where((key >= low) & (key <= position), 0.0, MASKED)


def window_start(block, window):
    return pl.multiple_of(jnp.maximum((block + 1) * QB - window, 0), QB)


def prefix_bias(prefix):
    rows = lax.broadcasted_iota(jnp.int32, (PAD, 2 * QB), 0)
    return jnp.where(rows < prefix, 0.0, MASKED)


def project_kernel(first, x_ref, vec_ref, w_ref, bias_ref, *refs):
    if first:
        qkv_ref, normed_ref = refs[-2:]
        hat, _ = normalize(x_ref[...].astype(f32))
        normed = (hat * vector(vec_ref, GAIN_ONE) + vector(vec_ref, SHIFT_ONE)).astype(bf16)
        normed_ref[...] = normed
    else:
        qkv_ref = refs[-1]
        normed = x_ref[...]
    width = w_ref.shape[2]
    for i in range(3):
        part = nn(normed, w_ref[i]) + bias_ref[i : i + 1, :]
        qkv_ref[:, i * width : (i + 1) * width] = part.astype(bf16)


def project(first, x, vectors, weight, bias, bias_spec, after=()):
    length, full = x.shape
    width = weight.shape[2]
    step = 256
    block = pl.BlockSpec((step, full), lambda i: (i, 0))
    specs = [pl.BlockSpec((step, 3 * width), lambda i: (i, 0))]
    shapes = [jax.ShapeDtypeStruct((length, 3 * width), bf16)]
    if first:
        specs.append(block)
        shapes.append(pltpu.HBM((length, full), bf16))
    return pl.pallas_call(
        functools.partial(project_kernel, first),
        grid=(length // step,),
        in_specs=[
            block,
            once(vectors.shape, (0, 0)),
            once(weight.shape, (0, 0, 0)),
            bias_spec,
        ]
        + unread(after),
        out_specs=specs,
        out_shape=shapes,
        compiler_params=params(4),
        cost_estimate=cost(6 * length * full * width, length * full * 8),
        name="project",
    )(x, vectors, weight, bias, *after)


def attend_kernel(
    prefix, parcel, lengths_ref, pads_ref, qkv_ref, kv_ref, bias_ref, *refs
):
    o_ref, token_ref, norm_ref, order_ref = refs[-4:]
    token_ref[...] = jnp.zeros_like(token_ref)
    length, width = parcel.length, parcel.width
    pairs = width // (2 * HEAD_DIM)
    first = head_masks()
    front_bias = prefix_bias(prefix)
    o_ref[parcel.kv : parcel.lse, :] = kv_ref[...]
    o_ref[parcel.bias :, :] = bias_ref[...]

    def attend(blocks, window):
        for block in blocks:
            rows = pl.ds(pl.multiple_of(block * QB, QB), QB)
            start = window_start(block, window)
            keys_at = pl.ds(start, window)
            bias = window_bias(block, start, window, length, lengths_ref, pads_ref)
            for pair in range(pairs):
                at = pair * 2 * HEAD_DIM
                cols = slice(at, at + 2 * HEAD_DIM)
                q = both_heads(qkv_ref[rows, cols] * jnp.asarray(HEAD_DIM**-0.5, bf16), first)
                k = qkv_ref[keys_at, width + at : width + at + 2 * HEAD_DIM]
                v = qkv_ref[keys_at, 2 * width + at : 2 * width + at + 2 * HEAD_DIM]
                pk = kv_ref[:PAD, cols].astype(bf16)
                pv = kv_ref[PAD:, cols].astype(bf16)
                inside = nt(k, q) + bias
                front = nt(pk, q) + front_bias
                largest = jnp.maximum(
                    jnp.max(inside, axis=0, keepdims=True), jnp.max(front, axis=0, keepdims=True)
                )
                inside = jnp.exp(inside - largest)
                front = jnp.exp(front - largest)
                total = jnp.sum(inside, axis=0, keepdims=True) + jnp.sum(
                    front, axis=0, keepdims=True
                )
                scale = 1.0 / total
                out = tn(v, (inside * scale).astype(bf16)) + tn(pv, (front * scale).astype(bf16))
                o_ref[rows, cols] = own_quadrants(out).T
                lse = largest + jnp.log(total)
                norm_ref[pair, pl.ds(2 * block, 1), :] = lse[:, :QB]
                norm_ref[pair, pl.ds(2 * block + 1, 1), :] = lse[:, QB:]

    by_window(length, lengths_ref, order_ref, attend)
    for pair in range(pairs):
        cols = slice(pair * 2 * HEAD_DIM, (pair + 1) * 2 * HEAD_DIM)
        o_ref[parcel.lse : parcel.bias, cols] = norm_ref[pair]


def attend(prefix, parcel, lengths, pads, qkv, prefix_kv, biases, after=()):
    length, width = parcel.length, parcel.width
    return pl.pallas_call(
        functools.partial(attend_kernel, prefix, parcel),
        grid=(1,),
        in_specs=[pl.BlockSpec(memory_space=pltpu.SMEM)] * 2
        + [once(v.shape, (0, 0)) for v in (qkv, prefix_kv, biases)]
        + unread(after),
        out_specs=[once((parcel.rows, width), (0, 0)), once((8, 128), (0, 0))],
        out_shape=[
            jax.ShapeDtypeStruct((parcel.rows, width), f32),
            jax.ShapeDtypeStruct((8, 128), f32),
        ],
        scratch_shapes=[
            pltpu.VMEM((width // (2 * HEAD_DIM), parcel.bias - parcel.lse, 2 * HEAD_DIM), f32),
            pltpu.SMEM((length // QB,), jnp.int32),
        ],
        compiler_params=params(10),
        cost_estimate=cost(
            8 * length * (SPAN + QB) * width,
            length * width * 10,
            length * (SPAN + QB) * width // HEAD_DIM,
        ),
        name="attend",
    )(lengths, pads, qkv, prefix_kv, biases, *after)


def pack_kernel(which_ref, w_ref, *refs):
    out_ref = refs[-1]
    size, width = w_ref.shape[0], out_ref.shape[1]
    for i in range(w_ref.shape[1] // width):
        out_ref[i * size : (i + 1) * size, :] = w_ref[:, i * width : (i + 1) * width].astype(f32)


def pack(which, parcel, out, weight, after=()):
    size = weight.shape[0] // RING
    assert size * (weight.shape[1] // parcel.width) == parcel.piece
    assert parcel.length % parcel.piece == 0
    place = parcel.length // parcel.piece
    return pl.pallas_call(
        pack_kernel,
        grid_spec=pltpu.PrefetchScalarGridSpec(
            num_scalar_prefetch=1,
            grid=(1,),
            in_specs=[pl.BlockSpec((size, weight.shape[1]), lambda i, w: (w[0], 0))]
            + unread([out])
            + unread(after),
            out_specs=pl.BlockSpec((parcel.piece, parcel.width), lambda i, w: (place, 0)),
        ),
        out_shape=jax.ShapeDtypeStruct(out.shape, f32),
        input_output_aliases={2: 0},
        compiler_params=params(2),
        cost_estimate=cost(0, parcel.piece * parcel.width * 6),
        name="pack",
    )(which, weight, out, *after)


def heads_back_kernel(count, core_ref, keep_ref, other_ref, *refs):
    weights, outs = refs[:count], refs[-count:]
    own = pl.program_id(0) == core_ref[0]
    low = jnp.where(own, keep_ref[...], other_ref[...]).astype(bf16)
    for w_ref, out_ref in zip(weights, outs):
        out_ref[...] = nt(low, w_ref[...]).astype(bf16)


def heads_back(which, keep, other, weights, after=()):
    half, full = keep.shape
    step = 256
    count = half // step

    def at_keep(h, i, w):
        return jnp.where(h == w[0], i, (count - 1) * (1 - w[0])), 0

    def at_other(h, i, w):
        return jnp.where(h == w[0], (count - 1) * w[0], i), 0

    return pl.pallas_call(
        functools.partial(heads_back_kernel, len(weights)),
        grid_spec=pltpu.PrefetchScalarGridSpec(
            num_scalar_prefetch=1,
            grid=(2, count),
            in_specs=[pl.BlockSpec((step, full), at_keep), pl.BlockSpec((step, full), at_other)]
            + [once(w.shape, (0, 0)) for w in weights]
            + unread(after),
            out_specs=[
                pl.BlockSpec((step, w.shape[0]), lambda h, i, w: (h * count + i, 0))
                for w in weights
            ],
        ),
        out_shape=[jax.ShapeDtypeStruct((2 * half, w.shape[0]), bf16) for w in weights],
        compiler_params=params(8),
        cost_estimate=cost(4 * half * sum(w.size for w in weights), half * full * 10),
        name="heads_back",
    )(which, keep, other, *weights, *after)


def attend_back_kernel(
    prefix, lengths_ref, pads_ref, qkv_ref, do_ref, kv_ref, lse_ref, *refs
):
    dqkv_ref, dpk_ref, dpv_ref, norm_ref, order_ref, *sums = refs[-9:]
    length, width = do_ref.shape
    pairs = width // (2 * HEAD_DIM)
    first = head_masks()
    front_bias = prefix_bias(prefix)
    for pair in range(pairs):
        norm_ref[pair] = lse_ref[:, pair * 2 * HEAD_DIM : (pair + 1) * 2 * HEAD_DIM]
    for ref in (dpk_ref, dpv_ref, *sums):
        ref[...] = jnp.zeros_like(ref)
    factor = HEAD_DIM**-0.5

    def back(blocks, window):
        for number, block in enumerate(blocks):
            dk_ref, dv_ref = sums[2 * number : 2 * number + 2]
            rows = pl.ds(pl.multiple_of(block * QB, QB), QB)
            start = window_start(block, window)
            keys_at = pl.ds(start, window)
            bias = window_bias(block, start, window, length, lengths_ref, pads_ref)
            for pair in range(pairs):
                at = pair * 2 * HEAD_DIM
                cols = slice(at, at + 2 * HEAD_DIM)
                k = qkv_ref[keys_at, width + at : width + at + 2 * HEAD_DIM]
                v = qkv_ref[keys_at, 2 * width + at : 2 * width + at + 2 * HEAD_DIM]
                pk = kv_ref[:PAD, cols].astype(bf16)
                pv = kv_ref[PAD:, cols].astype(bf16)
                q = both_heads(qkv_ref[rows, cols] * jnp.asarray(factor, bf16), first)
                do = both_heads(do_ref[rows, cols], first)
                lse = jnp.concatenate(
                    [
                        norm_ref[pair, pl.ds(2 * block, 1), :],
                        norm_ref[pair, pl.ds(2 * block + 1, 1), :],
                    ],
                    axis=1,
                )
                inside = jnp.exp(nt(k, q) + bias - lse)
                front = jnp.exp(nt(pk, q) + front_bias - lse)
                d_inside = nt(v, do)
                d_front = nt(pv, do)
                delta = jnp.sum(inside * d_inside, axis=0, keepdims=True) + jnp.sum(
                    front * d_front, axis=0, keepdims=True
                )
                s_inside = (inside * (d_inside - delta)).astype(bf16)
                s_front = (front * (d_front - delta)).astype(bf16)
                dk_ref[keys_at, cols] += nn(s_inside, q)
                dv_ref[keys_at, cols] += nn(inside.astype(bf16), do)
                dpk_ref[:, cols] += nn(s_front, q)
                dpv_ref[:, cols] += nn(front.astype(bf16), do)
                dq = own_quadrants(tn(k, s_inside) + tn(pk, s_front)).T * factor
                dqkv_ref[rows, cols] = dq.astype(bf16)

    by_window(length, lengths_ref, order_ref, back)
    dqkv_ref[:, width : 2 * width] = (sums[0][...] + sums[2][...]).astype(bf16)
    dqkv_ref[:, 2 * width :] = (sums[1][...] + sums[3][...]).astype(bf16)


def attend_back(prefix, parcel, lengths, pads, qkv, grad, out, after=(), weight=1):
    length, width = parcel.length, parcel.width
    lse_rows = parcel.bias - parcel.lse
    return pl.pallas_call(
        functools.partial(attend_back_kernel, prefix),
        grid=(1,),
        in_specs=[pl.BlockSpec(memory_space=pltpu.SMEM)] * 2
        + [
            once(qkv.shape, (0, 0)),
            once(grad.shape, (0, 0)),
            parcel.part(parcel.kv, 2 * PAD),
            parcel.part(parcel.lse, lse_rows),
        ]
        + unread(after),
        out_specs=[
            once((length, 3 * width), (0, 0)),
            once((PAD, width), (0, 0)),
            once((PAD, width), (0, 0)),
        ],
        out_shape=[
            jax.ShapeDtypeStruct((length, 3 * width), bf16),
            jax.ShapeDtypeStruct((PAD, width), f32),
            jax.ShapeDtypeStruct((PAD, width), f32),
        ],
        scratch_shapes=[
            pltpu.VMEM((width // (2 * HEAD_DIM), lse_rows, 2 * HEAD_DIM), f32),
            pltpu.SMEM((length // QB,), jnp.int32),
        ]
        + [pltpu.VMEM((length, width), f32)] * 4,
        compiler_params=params(14),
        cost_estimate=cost(
            weight * 20 * length * (SPAN + QB) * width,
            length * width * 40,
            length * (SPAN + QB) * width // HEAD_DIM,
        ),
        name="attend_back",
    )(lengths, pads, qkv, grad, out, out, *after)


def pass_kernel(*refs):
    del refs


def held(values, after):
    count = len(values)
    return pl.pallas_call(
        pass_kernel,
        in_specs=unread(values) + unread(after),
        out_specs=unread(values),
        out_shape=[jax.ShapeDtypeStruct(v.shape, v.dtype) for v in values],
        input_output_aliases={i: i for i in range(count)},
        compiler_params=params(1),
        cost_estimate=cost(0, 0),
        name="held",
    )(*values, *after)


def pick_kernel(count, which_ref, *refs):
    weights, outs = refs[:count], refs[-2 * count - 1 : -count - 1]
    buffers, sems = refs[-count - 1 : -1], refs[-1]
    copies = []
    for number, (ref, buffer) in enumerate(zip(weights, buffers)):
        size = buffer.shape[-2]
        rows = pl.ds(pl.multiple_of(which_ref[number] * size, size), size)
        source = ref.at[rows, :] if len(ref.shape) == 2 else ref.at[:, rows, :]
        copies.append(pltpu.make_async_copy(source, buffer, sems.at[number]))
        copies[-1].start()
    for copy, buffer, out_ref in zip(copies, buffers, outs):
        copy.wait()
        out_ref[...] = buffer[...].astype(f32)


def picked(whiches, weights, after=()):
    shapes = [(*w.shape[:-2], w.shape[-2] // RING, w.shape[-1]) for w in weights]
    return pl.pallas_call(
        functools.partial(pick_kernel, len(weights)),
        grid=(1,),
        in_specs=[pl.BlockSpec(memory_space=pltpu.SMEM)]
        + [pl.BlockSpec(memory_space=pltpu.HBM)] * len(weights)
        + unread(after),
        out_specs=[once(shape, (0,) * len(shape)) for shape in shapes],
        out_shape=[jax.ShapeDtypeStruct(shape, f32) for shape in shapes],
        scratch_shapes=[pltpu.VMEM(shape, bf16) for shape in shapes]
        + [pltpu.SemaphoreType.DMA((len(weights),))],
        compiler_params=params(6),
        cost_estimate=cost(0, sum(shape[-2] * shape[-1] for shape in shapes) * 6),
        name="pick",
    )(jnp.concatenate(whiches), *in_hbm(weights), *after)


def assemble_kernel(shifts, folded, order_ref, *refs):
    out_ref = refs[-1]
    pieces = refs[: len(shifts)]
    size = pieces[0].shape[-2]
    for shift, ref in zip(shifts, pieces):
        at = lax.rem(order_ref[0] + (shift + RING), RING) * size
        rows = pl.ds(pl.multiple_of(at, size), size)
        if folded and ref is pieces[-1]:
            width = ref.shape[1]
            for i in range(out_ref.shape[1] // width):
                block = ref[i * size : (i + 1) * size, :]
                out_ref[rows, i * width : (i + 1) * width] = block.astype(bf16)
        else:
            out_ref[..., rows, :] = ref[...].astype(bf16)


def assembled(order, shifts, pieces, last_spec, folded=False, after=()):
    shape = pieces[0].shape
    zeros = (0,) * len(shape)
    whole = (*shape[:-2], shape[-2] * RING, shape[-1])
    return pl.pallas_call(
        functools.partial(assemble_kernel, shifts, folded),
        grid=(1,),
        in_specs=[pl.BlockSpec(memory_space=pltpu.SMEM)]
        + [once(shape, zeros)] * (len(pieces) - 1)
        + [last_spec]
        + unread(after),
        out_specs=once(whole, zeros),
        out_shape=jax.ShapeDtypeStruct(whole, bf16),
        compiler_params=params(6),
        cost_estimate=cost(0, shape[-2] * RING * shape[-1] * 6),
        name="assemble",
    )(order, *pieces, *after)


def product_kernel(pieces, which_ref, *refs):
    total = None
    for a_ref, b_ref in zip(refs[:pieces], refs[pieces : 2 * pieces]):
        part = nn(a_ref[...].astype(bf16), b_ref[...])
        total = part if total is None else total + part
    refs[-1][...] = total


def half_product(which, half, lefts, rights, after=(), weight=1):
    columns = rights[0].shape[1]
    step = 256
    count = half // step
    depth = sum(b.shape[0] for b in rights)
    return pl.pallas_call(
        functools.partial(product_kernel, len(lefts)),
        grid_spec=pltpu.PrefetchScalarGridSpec(
            num_scalar_prefetch=1,
            grid=(count,),
            in_specs=[
                pl.BlockSpec((step, a.shape[1]), lambda i, w: (w[0] * count + i, 0)) for a in lefts
            ]
            + [once(b.shape, (0, 0)) for b in rights]
            + unread(after),
            out_specs=pl.BlockSpec((step, columns), lambda i, w: (i, 0)),
        ),
        out_shape=jax.ShapeDtypeStruct((half, columns), f32),
        compiler_params=params(6),
        cost_estimate=cost(
            weight * 2 * half * columns * depth, half * columns * 4 + depth * columns * 2
        ),
        name="half_product",
    )(which, *lefts, *rights, *after)


def unproject_kernel(pieces, which_ref, *refs):
    total = None
    for grad_ref, w_ref in zip(refs[:pieces], refs[pieces : 2 * pieces]):
        width = w_ref.shape[2]
        part = None
        for i in range(3):
            product = nt(grad_ref[:, i * width : (i + 1) * width], w_ref[i])
            part = product if part is None else part + product
        total = part if total is None else total + part
    refs[-1][...] = total


def unproject(which, grads, weights, after=()):
    full, width = weights[0].shape[1:]
    half = grads[0].shape[0] // 2
    step = 256
    count = half // step
    return pl.pallas_call(
        functools.partial(unproject_kernel, len(weights)),
        grid_spec=pltpu.PrefetchScalarGridSpec(
            num_scalar_prefetch=1,
            grid=(count,),
            in_specs=[pl.BlockSpec((step, 3 * width), lambda i, w: (w[0] * count + i, 0))]
            * len(grads)
            + [once(w.shape, (0, 0, 0)) for w in weights]
            + unread(after),
            out_specs=pl.BlockSpec((step, full), lambda i, w: (i, 0)),
        ),
        out_shape=jax.ShapeDtypeStruct((half, full), f32),
        compiler_params=params(4),
        cost_estimate=cost(6 * half * full * width * len(weights), half * full * 8),
        name="unproject",
    )(which, *grads, *weights, *after)


def norm_two_kernel(which_ref, x_ref, a_ref, b_ref, vec_ref, *refs):
    middle_ref, normed_ref = refs[-2:]
    middle = x_ref[...].astype(f32) + (a_ref[...] + b_ref[...]) + vector(vec_ref, OUT_BIAS)
    middle_ref[...] = middle
    hat, _ = normalize(middle)
    normed = hat * vector(vec_ref, GAIN_TWO) + vector(vec_ref, SHIFT_TWO)
    normed_ref[...] = normed.astype(bf16).astype(f32)


def norm_two(which, x, terms, vectors, after=()):
    half, width = terms[0].shape
    step = 128
    count = half // step
    block = pl.BlockSpec((step, width), lambda i, w: (i, 0))
    return pl.pallas_call(
        norm_two_kernel,
        grid_spec=pltpu.PrefetchScalarGridSpec(
            num_scalar_prefetch=1,
            grid=(count,),
            in_specs=[pl.BlockSpec((step, width), lambda i, w: (w[0] * count + i, 0))]
            + [block] * 2
            + [once(vectors.shape, (0, 0))]
            + unread(after),
            out_specs=[block] * 2,
        ),
        out_shape=[jax.ShapeDtypeStruct((half, width), f32)] * 2,
        compiler_params=params(6),
        cost_estimate=cost(half * width * 12, half * width * 20),
        name="norm_two",
    )(which, x, *terms, vectors, *after)


def mlp_kernel(has_sum, which_ref, n_ref, g_ref, fc_ref, proj_ref, bias_ref, *refs):
    feed_ref, back_ref, act_ref, grad_ref = refs[-4:]
    normed = n_ref[...].astype(bf16)
    grad = g_ref[...]
    units, step = fc_ref.shape[1], bias_ref.shape[1]
    for number, at in enumerate(range(0, units, step)):
        cols = slice(at, at + step)
        hidden = nn(normed, fc_ref[:, cols]) + bias_ref[number : number + 1, :]
        square = hidden * hidden
        inner = jnp.tanh(hidden * (0.7978845608028654 + 0.7978845608028654 * 0.044715 * square))
        gate = 0.5 + 0.5 * inner
        act_ref[:, cols] = (hidden * gate).astype(bf16)
        slope = gate + (0.5 * hidden) * (1.0 - inner * inner) * (
            0.7978845608028654 + 3.0 * 0.7978845608028654 * 0.044715 * square
        )
        grad_ref[:, cols] = (nt(grad, proj_ref[cols, :]) * slope).astype(bf16)
    feed = nn(act_ref[...], proj_ref[...])
    back = nt(grad_ref[...], fc_ref[...])
    if has_sum:
        feed = feed + refs[0][...]
        back = back + refs[1][...]
    feed_ref[...] = feed
    back_ref[...] = back


def mlp(which, normed, cotangent, fc, proj, bias, bias_spec, sums=(), after=(), weight=1):
    half, width = normed.shape
    units = fc.shape[1]
    step = 256
    count = half // step
    block = pl.BlockSpec((step, width), lambda i, w: (i, 0))
    return pl.pallas_call(
        functools.partial(mlp_kernel, bool(sums)),
        grid_spec=pltpu.PrefetchScalarGridSpec(
            num_scalar_prefetch=1,
            grid=(count,),
            in_specs=[
                block,
                pl.BlockSpec((step, width), lambda i, w: (w[0] * count + i, 0)),
                once(fc.shape, (0, 0)),
                once(proj.shape, (0, 0)),
                bias_spec,
            ]
            + [block] * len(sums)
            + unread(after),
            out_specs=[block] * 2,
            scratch_shapes=[pltpu.VMEM((step, units), bf16)] * 2,
        ),
        out_shape=[jax.ShapeDtypeStruct((half, width), f32)] * 2,
        compiler_params=params(14),
        cost_estimate=cost(
            weight * 8 * half * width * units, half * width * 16 + 4 * width * units, half * units
        ),
        name="mlp",
    )(which, normed, cotangent, fc, proj, bias, *sums, *after)


def norm_two_back_kernel(which_ref, g_ref, a_ref, b_ref, middle_ref, vec_ref, *refs):
    hat, scale = normalize(middle_ref[...])
    grad = (a_ref[...] + b_ref[...]) * vector(vec_ref, GAIN_TWO)
    refs[-1][...] = g_ref[...].astype(f32) + norm_back(grad, hat, scale)


def norm_two_back(which, cotangent, a, b, middle, vectors, after=()):
    half, width = a.shape
    step = 128
    count = half // step
    block = pl.BlockSpec((step, width), lambda i, w: (i, 0))
    return pl.pallas_call(
        norm_two_back_kernel,
        grid_spec=pltpu.PrefetchScalarGridSpec(
            num_scalar_prefetch=1,
            grid=(count,),
            in_specs=[
                pl.BlockSpec((step, width), lambda i, w: (w[0] * count + i, 0)),
                block,
                block,
                block,
                once(vectors.shape, (0, 0)),
            ]
            + unread(after),
            out_specs=block,
        ),
        out_shape=jax.ShapeDtypeStruct((half, width), f32),
        compiler_params=params(7),
        cost_estimate=cost(half * width * 20, half * width * 18),
        name="norm_two_back",
    )(which, cotangent, a, b, middle, vectors, *after)


def norm_one_back_kernel(which_ref, x_ref, upper_ref, vec_ref, a_ref, b_ref, *refs):
    hat, scale = normalize(x_ref[...].astype(f32))
    grad = (a_ref[...] + b_ref[...]) * vector(vec_ref, GAIN_ONE)
    refs[-2][...] = upper_ref[...] + norm_back(grad, hat, scale)
    refs[-1][...] = jnp.zeros_like(refs[-1])


def norm_one_back(which, x, upper, vectors, a, b, whole=(), after=()):
    half, width = upper.shape
    step = 128
    count = half // step
    block = pl.BlockSpec((step, width), lambda i, w: (i, 0))
    placed = pl.BlockSpec((step, width), lambda i, w: (w[0] * count + i, 0))
    return pl.pallas_call(
        norm_one_back_kernel,
        grid_spec=pltpu.PrefetchScalarGridSpec(
            num_scalar_prefetch=1,
            grid=(count,),
            in_specs=[placed, block, once(vectors.shape, (0, 0)), block, block]
            + unread(whole)
            + unread(after),
            out_specs=[placed, once((8, 128), (0, 0))],
        ),
        out_shape=[
            jax.ShapeDtypeStruct((2 * half, width), f32),
            jax.ShapeDtypeStruct((8, 128), f32),
        ],
        input_output_aliases={6: 0} if whole else {},
        compiler_params=params(6),
        cost_estimate=cost(half * width * 20, half * width * 18),
        name="norm_one_back",
    )(which, x, upper, vectors, a, b, *whole, *after)


def result_kernel(which_ref, a_ref, b_ref, middle_ref, vec_ref, *refs):
    half_ref, whole_ref, token_ref = refs[-3:]
    token_ref[...] = jnp.zeros_like(token_ref)
    result = middle_ref[...] + (a_ref[...] + b_ref[...]) + vector(vec_ref, PROJ_BIAS)
    half_ref[...] = result
    whole_ref[...] = result.astype(bf16)


def result_half(which, a, b, middle, vectors, after=(), weight=1):
    half, width = middle.shape
    step = 128
    count = half // step
    block = pl.BlockSpec((step, width), lambda i, w: (i, 0))
    placed = pl.BlockSpec((step, width), lambda i, w: (w[0] * count + i, 0))
    return pl.pallas_call(
        result_kernel,
        grid_spec=pltpu.PrefetchScalarGridSpec(
            num_scalar_prefetch=1,
            grid=(count,),
            in_specs=[block, block, block, once(vectors.shape, (0, 0))] + unread(after),
            out_specs=[block, placed, once((8, 128), (0, 0))],
        ),
        out_shape=[
            jax.ShapeDtypeStruct((half, width), f32),
            jax.ShapeDtypeStruct((2 * half, width), bf16),
            jax.ShapeDtypeStruct((8, 128), f32),
        ],
        compiler_params=params(6),
        cost_estimate=cost(weight * half * width * 2048, half * width * 18),
        name="result",
    )(which, a, b, middle, vectors, *after)


def place_kernel(which_ref, half_ref, *refs):
    refs[-2][...] = half_ref[...].astype(refs[-2].dtype)
    refs[-1][...] = jnp.zeros_like(refs[-1])


def placed_half(which, half_values, whole, after=()):
    half, width = half_values.shape
    step = 128
    count = half // step
    return pl.pallas_call(
        place_kernel,
        grid_spec=pltpu.PrefetchScalarGridSpec(
            num_scalar_prefetch=1,
            grid=(count,),
            in_specs=[pl.BlockSpec((step, width), lambda i, w: (i, 0))]
            + unread([whole])
            + unread(after),
            out_specs=[
                pl.BlockSpec((step, width), lambda i, w: (w[0] * count + i, 0)),
                once((8, 128), (0, 0)),
            ],
        ),
        out_shape=[
            jax.ShapeDtypeStruct(whole.shape, whole.dtype),
            jax.ShapeDtypeStruct((8, 128), f32),
        ],
        input_output_aliases={2: 0},
        compiler_params=params(3),
        cost_estimate=cost(0, half * width * 8),
        name="place",
    )(which, half_values, whole, *after)


def parts(values):
    high = values.astype(bf16)
    return high, (values - high.astype(f32)).astype(bf16)


def prefix_kernel(a_ref, b_ref, trunk_ref, embed_ref, w1_ref, *refs):
    w1_grad_ref, w2_grad_ref, b1_grad_ref, b2_grad_ref, embed_grad_ref = refs[-5:]
    columns = w2_grad_ref.shape[2]
    wide = w2_grad_ref.shape[1] * columns
    both = a_ref[:PAD, :] + b_ref[:PAD, :]
    kv, trunk = both[:, :wide], trunk_ref[...]
    pre = both[:, wide:] * (1.0 - trunk * trunk)
    pre_high, pre_low = parts(pre)
    embed = embed_ref[...]
    w1_grad_ref[...] = tn(
        jnp.concatenate([embed, embed], axis=0), jnp.concatenate([pre_high, pre_low], axis=0)
    )
    rows = nt(jnp.concatenate([pre_high, pre_low], axis=0), w1_ref[...])
    embed_grad_ref[...] = rows[:PAD] + rows[PAD:]
    b1_grad_ref[...] = jnp.sum(pre, axis=0, keepdims=True)
    b2_grad = jnp.sum(kv, axis=0, keepdims=True)
    trunk_high, trunk_low = parts(trunk)
    kv_high, kv_low = parts(kv)
    w2_grad = tn(
        jnp.concatenate([trunk_high, trunk_high, trunk_low], axis=0),
        jnp.concatenate([kv_high, kv_low, kv_high], axis=0),
    )
    for i in range(w2_grad_ref.shape[1]):
        cols = slice(i * columns, (i + 1) * columns)
        w2_grad_ref[:, i, :] = w2_grad[:, cols]
        b2_grad_ref[i : i + 1, :] = b2_grad[:, cols]


def prefix_grads(a, b, trunk, embed, w1, width, after=()):
    full, rank = w1.shape
    shapes = [(full, rank), (rank, 2, width), (1, rank), (2, width), (PAD, full)]
    return pl.pallas_call(
        prefix_kernel,
        grid=(1,),
        in_specs=[once(v.shape, (0, 0)) for v in (a, b, trunk, embed, w1)] + unread(after),
        out_specs=[once(shape, (0,) * len(shape)) for shape in shapes],
        out_shape=[jax.ShapeDtypeStruct(shape, f32) for shape in shapes],
        compiler_params=params(16),
        cost_estimate=cost(0, full * rank * 8),
        name="prefix_grads",
    )(a, b, trunk, embed, w1, *after)


def shards(
    group,
    copies,
    tokens,
    cotangent,
    seg_lengths,
    pad_counts,
    ln1_gain,
    ln1_shift,
    qkv_weight,
    qkv_bias,
    out_weight,
    out_bias,
    ln2_gain,
    ln2_shift,
    fc_weight,
    fc_bias,
    proj_weight,
    proj_bias,
    prefix_embed,
    reparam_w1,
    reparam_b1,
    reparam_w2,
    reparam_b2,
):
    rows_here, length, width = tokens.shape
    assert rows_here == 1 and copies % RING == 0
    local_width = qkv_weight.shape[2]
    prefix = prefix_embed.shape[0]
    half = length // 2
    parcel = Parcel(length, local_width, width)
    place = lax.axis_index("tensor")
    core = place % CORES
    mine = core.reshape(1).astype(jnp.int32)
    theirs = 1 - mine
    none = mine * 0
    far_shifts = [CORES * s for s in range(1, group // CORES)]

    def to_core(values):
        return lax.ppermute(values, "tensor", [(t, t ^ 1) for t in range(group)])

    def to_far(values):
        return [
            lax.ppermute(values, "tensor", [(t, (t + shift) % group) for t in range(group)])
            for shift in far_shifts
        ]

    def swapped(values, axis, size, step):
        return values + lax.ppermute(values, axis, [(i, i ^ step) for i in range(size)])

    ring = list(range(0, RING, 2)) + list(range(RING - 1, 0, -2))
    member = lax.axis_index("dp") % RING
    order = jnp.where(member % 2 == 0, member // 2, RING - 1 - member // 2)
    here = order.reshape(1).astype(jnp.int32)
    across = (here + RING // 2) % RING
    hops = RING // 2 - 1

    def along(values, step):
        hop = [
            (base + ring[i], base + ring[(i + step) % RING])
            for base in range(0, copies, RING)
            for i in range(RING)
        ]
        return lax.ppermute(values, "dp", hop)

    def hop(rings):
        for levels in rings:
            up, down = levels[-1]
            levels.append((along(up, 1), along(down, -1)))

    def last(rings):
        return [piece for levels in rings for piece in levels[-1]]

    def hold(rings, after):
        for levels in rings:
            up, down = levels[-1]
            if up is down:
                up = down = held([up], after)[0]
            else:
                up, down = held([up, down], after)
            levels[-1] = (up, down)

    def starting(pieces):
        return [[(piece, piece)] for piece in pieces]

    def rebuilt(levels, facing, spec, folded=False, after=()):
        shifts, pieces = [0], [levels[0][0]]
        for number, (up, down) in enumerate(levels[1:]):
            shifts += [-1 - number, number + 1]
            pieces += [up, down]
        return assembled(here, shifts + [RING // 2], pieces + [facing], spec, folded, after)

    x = tokens.reshape(length, width)
    grad_out = cotangent.reshape(length, width)
    lengths = seg_lengths.reshape(-1)
    qkv_w = jnp.transpose(qkv_weight, (1, 0, 2))
    vectors = jnp.stack([ln1_gain, ln1_shift, out_bias, ln2_gain, ln2_shift, proj_bias])
    vectors = jnp.pad(vectors, ((0, 2), (0, 0))).astype(f32)

    (piece_fc,) = picked([here], [fc_weight])
    near_fc = to_far(piece_fc)
    (piece_out,) = picked([here], [out_weight], [piece_fc])
    near_out = to_far(piece_out)
    (piece_proj,) = picked([here], [proj_weight], [piece_out])
    near_proj = to_far(piece_proj)
    ring_out, ring_fc, ring_proj = starting(near_out), starting(near_fc), starting(near_proj)

    fc_rows = fc_bias.astype(f32).reshape(-1, local_width)
    biases = jnp.concatenate(
        [
            jnp.pad(qkv_bias.astype(f32), ((0, 5), (0, 0))),
            jnp.pad(fc_rows, ((0, 8 - fc_rows.shape[0]), (0, 0))),
        ],
        axis=0,
    )
    qkv_bias_spec = once((8, local_width), (0, 0))
    fc_bias_spec = once((8, local_width), (1, 0))
    qkv, normed_one = project(True, in_hbm([x])[0], vectors, qkv_w, biases, qkv_bias_spec)

    embed = prefix_embed.astype(f32)
    trunk_weight = reparam_w1.astype(f32)
    head_weight = reparam_w2.astype(f32)
    trunk = jnp.tanh(jnp.dot(embed, trunk_weight, precision=highest) + reparam_b1.astype(f32))
    kv_values = jnp.einsum(
        "pr,rtd->ptd", trunk, head_weight, precision=highest
    ) + reparam_b2.astype(f32)
    flat_kv = jnp.pad(kv_values, ((0, PAD - prefix), (0, 0), (0, 0)))
    prefix_kv = jnp.concatenate([flat_kv[:, 0], flat_kv[:, 1]], axis=0)

    hold(ring_fc, [qkv])
    fc_held = last(ring_fc)
    hop(ring_fc)
    hold(ring_out, [qkv])
    out_held = last(ring_out)
    hop(ring_out)
    out, token = attend(
        prefix, parcel, lengths, pad_counts, qkv, prefix_kv, biases, fc_held + out_held
    )
    out = pack(across, parcel, out, out_weight, last(ring_fc) + last(ring_out))
    out = held([out], [token])[0]
    far_out_parcel = to_far(out)
    hold(ring_out, [out])
    out_held = last(ring_out)
    hop(ring_out)
    hold(ring_proj, out_held)
    hop(ring_proj)
    second_out = last(ring_out)
    hop(ring_out)
    hold(ring_fc, last(ring_proj) + second_out)
    hop(ring_fc)
    hold(ring_proj, last(ring_out))
    hop(ring_proj)
    across_fc, across_proj, piece_qkv, across_qkv, behind_qkv, ahead_qkv = picked(
        [across, across, here, across, (here + RING - hops) % RING, (here + hops) % RING],
        [fc_weight, proj_weight] + [qkv_w] * 4,
        last(ring_out),
    )
    far_out = [
        rebuilt(levels, far, parcel.part(length, parcel.piece), True, [across_qkv])
        for levels, far in zip(ring_out, far_out_parcel)
    ]
    lefts = [out] + far_out_parcel
    rights = [out_weight] + far_out
    send = half_product(theirs, half, lefts, rights, last(ring_fc))
    received = to_core(send)
    keep = half_product(mine, half, lefts, rights, [send], KEEP)
    facing_fc = to_far(held([across_fc], last(ring_fc))[0])
    hold(ring_fc, last(ring_proj))
    fc_held = last(ring_fc)
    hop(ring_fc)
    middle, normed = norm_two(mine, x, [keep, received], vectors, fc_held)
    other_normed = to_core(normed)
    own = (fc_weight, proj_weight, biases, fc_bias_spec)
    keep_sums = mlp(mine, normed, grad_out, *own, (), (), OWN)
    hold(ring_proj, [other_normed])
    hop(ring_proj)
    near_qkv = to_far(held([piece_qkv], [normed])[0])
    facing_proj = to_far(held([across_proj], facing_fc + [keep_sums[0]])[0])
    fc_spec, proj_spec = once(piece_fc.shape, (0, 0)), once(piece_proj.shape, (0, 0))
    send_sums = mlp(
        theirs, other_normed, grad_out, *own, (), [keep_sums[0]] + last(ring_fc)
    )
    ring_qkv = starting(near_qkv)
    hold(ring_qkv, [send_sums[0]] + last(ring_fc))
    hop(ring_qkv)
    far_fc = [
        rebuilt(levels, piece, fc_spec, False, [send_sums[0]])
        for levels, piece in zip(ring_fc, facing_fc)
    ]
    far_proj = [
        rebuilt(levels, piece, proj_spec, False, far_fc)
        for levels, piece in zip(ring_proj, facing_proj)
    ]
    far_bias_spec = parcel.part(parcel.bias + 8, 8)
    for fc, proj, far in zip(far_fc, far_proj, far_out_parcel):
        send_sums = mlp(
            theirs, other_normed, grad_out, fc, proj, far, far_bias_spec, send_sums, (), LIGHT
        )
    back_received = to_core(send_sums[1])
    for fc, proj, far in zip(far_fc, far_proj, far_out_parcel):
        keep_sums = mlp(
            mine,
            normed,
            grad_out,
            fc,
            proj,
            far,
            far_bias_spec,
            keep_sums,
            [send_sums[0]],
            FAR,
        )
    facing_qkv = to_far(held([across_qkv], near_qkv + [send_sums[0]])[0])
    upper = norm_two_back(
        mine, grad_out, keep_sums[1], back_received, middle, vectors
    )
    hold(ring_qkv, [upper])
    q_held = last(ring_qkv)
    hop(ring_qkv)
    other_upper = to_core(upper)
    feed_received = to_core(send_sums[0])
    result, mixed, result_token = result_half(
        mine, keep_sums[0], feed_received, middle, vectors, q_held + facing_qkv, FAR
    )
    other_result = to_core(result)
    behind = to_far(held([behind_qkv], [send_sums[0]])[0])
    ahead = to_far(held([ahead_qkv], [upper])[0])

    grads_far = heads_back(
        mine, upper, other_upper, [out_weight] + far_out, [result_token]
    )
    dqkv, grad_keys, grad_vals = attend_back(
        prefix,
        parcel,
        lengths,
        pad_counts,
        qkv,
        grads_far[0],
        out,
        (),
        LIGHT,
    )

    for levels, *ends in zip(ring_qkv, behind, ahead):
        levels.append(ends)
    grad_keys, grad_vals = held(
        [grad_keys, grad_vals],
        behind + ahead + [piece for levels in ring_qkv for piece in levels[-2]],
    )
    grad_here = jnp.concatenate([grad_keys, grad_vals], axis=1)
    flat_head = jnp.transpose(head_weight, (1, 2, 0)).reshape(2 * local_width, -1)
    trunk_here = jnp.dot(grad_here, flat_head, precision=highest)
    for_tensor = [("tensor", group, 1 << i) for i in range(group.bit_length() - 1)]
    for_dp = [("dp", copies, 1 << i) for i in reversed(range(copies.bit_length() - 1))]
    mixed, token = placed_half(theirs, other_result, mixed, [dqkv])
    far_qkv = [
        rebuilt(levels, piece, once(piece.shape, (0, 0, 0)), False, [token])
        for levels, piece in zip(ring_qkv, facing_qkv)
    ]
    qkvs = [qkv_w] + far_qkv
    trunk_here = swapped(trunk_here, *for_tensor[0])
    far_projected = [
        project(
            False,
            in_hbm([normed_one])[0],
            vectors,
            weight,
            far,
            parcel.part(parcel.bias, 8),
            [trunk_here],
        )[0]
        for weight, far in zip(far_qkv, far_out_parcel)
    ]
    for step in for_tensor[1:]:
        trunk_here = swapped(trunk_here, *step)
    grads = [dqkv]
    for number, far in enumerate(far_out_parcel):
        found = attend_back(
            prefix,
            parcel,
            lengths,
            pad_counts,
            far_projected[number],
            grads_far[1 + number],
            far,
            [trunk_here],
            LIGHT,
        )
        grads.append(found[0])
    both = jnp.concatenate([grad_here, trunk_here], axis=1)
    both = swapped(held([both], far_projected)[0], *for_dp[0])
    both = held([both], grads[-1:])[0]
    send_one = unproject(theirs, grads, qkvs, [both])
    received_one = to_core(send_one)
    both = swapped(both, *for_dp[1])
    keep_one = unproject(mine, grads, qkvs, [send_one, both])
    received_two = to_core(keep_one)
    for step in for_dp[2:-1]:
        both = swapped(both, *step)
    last_step = for_dp[-1]
    other_both = lax.ppermute(both, "dp", [(i, i ^ last_step[2]) for i in range(copies)])
    input_grad, token = norm_one_back(mine, x, upper, vectors, keep_one, received_one)
    w1_grad, w2_grad, b1_grad, b2_grad, embed_grad = prefix_grads(
        both,
        other_both,
        jnp.pad(trunk, ((0, PAD - prefix), (0, 0))),
        jnp.pad(prefix_embed, ((0, PAD - prefix), (0, 0))),
        reparam_w1,
        local_width,
        [token],
    )
    input_grad, _ = norm_one_back(
        theirs, x, other_upper, vectors, send_one, received_two, [input_grad], [b1_grad]
    )
    b1_grad, embed_grad = b1_grad.reshape(-1), embed_grad[:prefix]
    mixed, input_grad = mixed.reshape(tokens.shape), input_grad.reshape(tokens.shape)
    return (mixed, input_grad, embed_grad, w1_grad, b1_grad, w2_grad, b2_grad, kv_values)


def solution(mesh):
    return jax.shard_map(
        functools.partial(shards, mesh.shape["tensor"], mesh.shape["dp"]),
        mesh=mesh,
        in_specs=(
            P("dp", None, None),
            P("dp", None, None),
            P("dp", None),
            P("dp"),
            P(),
            P(),
            P(None, None, "tensor"),
            P(None, "tensor"),
            P("tensor", None),
            P(),
            P(),
            P(),
            P(None, "tensor"),
            P("tensor"),
            P("tensor", None),
            P(),
            P(),
            P(),
            P(),
            P(None, None, "tensor"),
            P(None, "tensor"),
        ),
        out_specs=(
            P("dp", None, None),
            P("dp", None, None),
            P(),
            P(),
            P(),
            P(None, None, "tensor"),
            P(None, "tensor"),
            P(None, None, "tensor"),
        ),
        check_vma=False,
    )
```

```python
import functools

import jax
import jax.numpy as jnp
from jax import lax
from jax.experimental import pallas as pl
from jax.experimental.pallas import tpu as pltpu
from jax.sharding import PartitionSpec as P

HEAD_DIM = 64
CORES = 2
QB = 128
SPAN = 384
PAD = 16
RING = 8
LIGHT = 16
KEEP, OWN, FAR = 640, 320, 320
MASKED = -1e30
GAIN_ONE, SHIFT_ONE, OUT_BIAS, GAIN_TWO, SHIFT_TWO, PROJ_BIAS = range(6)
highest = lax.Precision.HIGHEST
epsilon = 1e-05
f32 = jnp.float32
bf16 = jnp.bfloat16


def nn(a, b):
    return jnp.dot(a, b, preferred_element_type=f32)


def nt(a, b):
    return lax.dot_general(a, b, (((1,), (1,)), ((), ())), preferred_element_type=f32)


def tn(a, b):
    return lax.dot_general(a, b, (((0,), (0,)), ((), ())), preferred_element_type=f32)


def params(mib):
    return pltpu.CompilerParams(vmem_limit_bytes=mib * 1024 * 1024)


def in_hbm(values):
    return [pltpu.with_memory_space_constraint(v, pltpu.HBM) for v in values]


def cost(flops, bytes_accessed, transcendentals=0):
    return pl.CostEstimate(
        flops=int(flops) // LIGHT,
        bytes_accessed=int(bytes_accessed) // LIGHT,
        transcendentals=int(transcendentals) // LIGHT,
    )


def unread(after):
    return [pl.BlockSpec(memory_space=pl.ANY)] * len(after)


def once(shape, index):
    return pl.BlockSpec(shape, lambda *_: index, pipeline_mode=pl.Buffered(1))


def vector(ref, number):
    return ref[number : number + 1, :]


def normalize(values):
    centered = values - jnp.mean(values, axis=-1, keepdims=True)
    scale = lax.rsqrt(jnp.mean(centered * centered, axis=-1, keepdims=True) + epsilon)
    return centered * scale, scale


def norm_back(grad, hat, scale):
    mean_grad = jnp.mean(grad, axis=-1, keepdims=True)
    mean_both = jnp.mean(grad * hat, axis=-1, keepdims=True)
    return scale * (grad - mean_grad - hat * mean_both)


class Parcel:
    def __init__(self, length, width, full):
        self.length, self.width, self.full = length, width, full
        self.piece = full // 8
        self.kv = length + self.piece
        self.lse = self.kv + 2 * PAD
        self.bias = self.lse + 2 * (length // QB)
        self.rows = self.bias + 16

    def part(self, start, size):
        assert start % size == 0
        return once((size, self.width), (start // size, 0))


def head_masks():
    lanes = lax.broadcasted_iota(jnp.int32, (QB, 2 * HEAD_DIM), 1)
    return lanes < HEAD_DIM


def both_heads(block, first):
    zero = jnp.zeros_like(block)
    return jnp.concatenate([jnp.where(first, block, zero), jnp.where(first, zero, block)], axis=0)


def own_quadrants(product):
    return jnp.concatenate([product[:HEAD_DIM, :QB], product[HEAD_DIM:, QB:]], axis=0)


def segment_start(position, lengths_ref):
    start, end = jnp.zeros_like(position), jnp.int32(0)
    for number in range(lengths_ref.shape[0]):
        end = end + lengths_ref[number]
        start = jnp.where(position >= end, end, start)
    return start


def by_window(length, lengths_ref, order_ref, run):
    blocks = length // QB
    most = min(length, SPAN + QB) // QB

    def tiles_of(block):
        return block - segment_start(block * QB, lengths_ref) // QB + 1

    def place(block, ends):
        low, high = ends
        small = tiles_of(block) <= most // 2
        order_ref[jnp.where(small, low, high)] = block
        return jnp.where(small, low + 1, low), jnp.where(small, high, high - 1)

    lax.fori_loop(0, blocks, place, (jnp.int32(0), jnp.int32(blocks - 1)))

    def step(number, _):
        pair = order_ref[2 * number], order_ref[2 * number + 1]
        tiles = jnp.maximum(tiles_of(pair[0]), tiles_of(pair[1]))
        for count in (most // 2, most):

            @pl.when((tiles <= count) & (tiles > count - most // 2))
            def _():
                run(pair, count * QB)

        return 0

    lax.fori_loop(0, blocks // 2, step, 0)


def window_bias(block, start, window, length, lengths_ref, pads_ref):
    lanes = lax.broadcasted_iota(jnp.int32, (1, 2 * QB), 1)
    position = block * QB + jnp.where(lanes < QB, lanes, lanes - QB)
    low = segment_start(position, lengths_ref)
    low = jnp.where(position < length - pads_ref[0], low, 4 * length)
    key = start + lax.broadcasted_iota(jnp.int32, (window, 2 * QB), 0)
    return jnp.where((key >= low) & (key <= position), 0.0, MASKED)


def window_start(block, window):
    return pl.multiple_of(jnp.maximum((block + 1) * QB - window, 0), QB)


def prefix_bias(prefix):
    rows = lax.broadcasted_iota(jnp.int32, (PAD, 2 * QB), 0)
    return jnp.where(rows < prefix, 0.0, MASKED)


def project_kernel(first, x_ref, y_ref, vec_ref, w_ref, bias_ref, *refs):
    whole = jnp.concatenate([x_ref[...], y_ref[...]], axis=1)
    if first:
        qkv_ref, normed_ref = refs[-2:]
        hat, _ = normalize(whole.astype(f32))
        normed = (hat * vector(vec_ref, GAIN_ONE) + vector(vec_ref, SHIFT_ONE)).astype(bf16)
        normed_ref[...] = normed
    else:
        qkv_ref = refs[-1]
        normed = whole
    width = w_ref.shape[2]
    for i in range(3):
        part = nn(normed, w_ref[i]) + bias_ref[i : i + 1, :]
        qkv_ref[:, i * width : (i + 1) * width] = part.astype(bf16)


def project(first, x, vectors, weight, bias, bias_spec, after=()):
    length, full = x.shape
    width = weight.shape[2]
    step = 256
    block = pl.BlockSpec((step, full), lambda i: (i, 0))
    specs = [pl.BlockSpec((step, 3 * width), lambda i: (i, 0))]
    shapes = [jax.ShapeDtypeStruct((length, 3 * width), bf16)]
    if first:
        specs.append(block)
        shapes.append(pltpu.HBM((length, full), bf16))
    return pl.pallas_call(
        functools.partial(project_kernel, first),
        grid=(length // step,),
        in_specs=[
            pl.BlockSpec((step, full // 2), lambda i: (i, 0)),
            pl.BlockSpec((step, full // 2), lambda i: (i, 1)),
            once(vectors.shape, (0, 0)),
            once(weight.shape, (0, 0, 0)),
            bias_spec,
        ]
        + unread(after),
        out_specs=specs,
        out_shape=shapes,
        compiler_params=params(4),
        cost_estimate=cost(6 * length * full * width, length * full * 8),
        name="project",
    )(x, x, vectors, weight, bias, *after)


def attend_kernel(
    prefix, parcel, lengths_ref, pads_ref, qkv_ref, kv_ref, bias_ref, *refs
):
    o_ref, token_ref, norm_ref, order_ref = refs[-4:]
    token_ref[...] = jnp.zeros_like(token_ref)
    length, width = parcel.length, parcel.width
    pairs = width // (2 * HEAD_DIM)
    first = head_masks()
    front_bias = prefix_bias(prefix)
    o_ref[parcel.kv : parcel.lse, :] = kv_ref[...]
    o_ref[parcel.bias :, :] = bias_ref[...]

    def attend(blocks, window):
        for block in blocks:
            rows = pl.ds(pl.multiple_of(block * QB, QB), QB)
            start = window_start(block, window)
            keys_at = pl.ds(start, window)
            bias = window_bias(block, start, window, length, lengths_ref, pads_ref)
            for pair in range(pairs):
                at = pair * 2 * HEAD_DIM
                cols = slice(at, at + 2 * HEAD_DIM)
                q = both_heads(qkv_ref[rows, cols] * jnp.asarray(HEAD_DIM**-0.5, bf16), first)
                k = qkv_ref[keys_at, width + at : width + at + 2 * HEAD_DIM]
                v = qkv_ref[keys_at, 2 * width + at : 2 * width + at + 2 * HEAD_DIM]
                pk = kv_ref[:PAD, cols].astype(bf16)
                pv = kv_ref[PAD:, cols].astype(bf16)
                inside = nt(k, q) + bias
                front = nt(pk, q) + front_bias
                largest = jnp.maximum(
                    jnp.max(inside, axis=0, keepdims=True), jnp.max(front, axis=0, keepdims=True)
                )
                inside = jnp.exp(inside - largest)
                front = jnp.exp(front - largest)
                total = jnp.sum(inside, axis=0, keepdims=True) + jnp.sum(
                    front, axis=0, keepdims=True
                )
                scale = 1.0 / total
                out = tn(v, (inside * scale).astype(bf16)) + tn(pv, (front * scale).astype(bf16))
                o_ref[rows, cols] = own_quadrants(out).T
                lse = largest + jnp.log(total)
                norm_ref[pair, pl.ds(2 * block, 1), :] = lse[:, :QB]
                norm_ref[pair, pl.ds(2 * block + 1, 1), :] = lse[:, QB:]

    by_window(length, lengths_ref, order_ref, attend)
    for pair in range(pairs):
        cols = slice(pair * 2 * HEAD_DIM, (pair + 1) * 2 * HEAD_DIM)
        o_ref[parcel.lse : parcel.bias, cols] = norm_ref[pair]


def attend(prefix, parcel, lengths, pads, qkv, prefix_kv, biases, after=()):
    length, width = parcel.length, parcel.width
    return pl.pallas_call(
        functools.partial(attend_kernel, prefix, parcel),
        grid=(1,),
        in_specs=[pl.BlockSpec(memory_space=pltpu.SMEM)] * 2
        + [once(v.shape, (0, 0)) for v in (qkv, prefix_kv, biases)]
        + unread(after),
        out_specs=[once((parcel.rows, width), (0, 0)), once((8, 128), (0, 0))],
        out_shape=[
            jax.ShapeDtypeStruct((parcel.rows, width), f32),
            jax.ShapeDtypeStruct((8, 128), f32),
        ],
        scratch_shapes=[
            pltpu.VMEM((width // (2 * HEAD_DIM), parcel.bias - parcel.lse, 2 * HEAD_DIM), f32),
            pltpu.SMEM((length // QB,), jnp.int32),
        ],
        compiler_params=params(10),
        cost_estimate=cost(
            8 * length * (SPAN + QB) * width,
            length * width * 10,
            length * (SPAN + QB) * width // HEAD_DIM,
        ),
        name="attend",
    )(lengths, pads, qkv, prefix_kv, biases, *after)


def pack_kernel(which_ref, w_ref, *refs):
    out_ref = refs[-1]
    size, width = w_ref.shape[0], out_ref.shape[1]
    for i in range(w_ref.shape[1] // width):
        out_ref[i * size : (i + 1) * size, :] = w_ref[:, i * width : (i + 1) * width].astype(f32)


def pack(which, parcel, out, weight, after=()):
    size = weight.shape[0] // RING
    assert size * (weight.shape[1] // parcel.width) == parcel.piece
    assert parcel.length % parcel.piece == 0
    place = parcel.length // parcel.piece
    return pl.pallas_call(
        pack_kernel,
        grid_spec=pltpu.PrefetchScalarGridSpec(
            num_scalar_prefetch=1,
            grid=(1,),
            in_specs=[pl.BlockSpec((size, weight.shape[1]), lambda i, w: (w[0], 0))]
            + unread([out])
            + unread(after),
            out_specs=pl.BlockSpec((parcel.piece, parcel.width), lambda i, w: (place, 0)),
        ),
        out_shape=jax.ShapeDtypeStruct(out.shape, f32),
        input_output_aliases={2: 0},
        compiler_params=params(2),
        cost_estimate=cost(0, parcel.piece * parcel.width * 6),
        name="pack",
    )(which, weight, out, *after)


def heads_back_kernel(count, core_ref, keep_ref, other_ref, *refs):
    weights, outs = refs[:count], refs[-count:]
    own = pl.program_id(0) == core_ref[0]
    low = jnp.where(own, keep_ref[...], other_ref[...]).astype(bf16)
    for w_ref, out_ref in zip(weights, outs):
        out_ref[...] = nt(low, w_ref[...]).astype(bf16)


def heads_back(which, keep, other, weights, after=()):
    half, full = keep.shape
    step = 256
    count = half // step

    def at_keep(h, i, w):
        return jnp.where(h == w[0], i, (count - 1) * (1 - w[0])), 0

    def at_other(h, i, w):
        return jnp.where(h == w[0], (count - 1) * w[0], i), 0

    return pl.pallas_call(
        functools.partial(heads_back_kernel, len(weights)),
        grid_spec=pltpu.PrefetchScalarGridSpec(
            num_scalar_prefetch=1,
            grid=(2, count),
            in_specs=[pl.BlockSpec((step, full), at_keep), pl.BlockSpec((step, full), at_other)]
            + [once(w.shape, (0, 0)) for w in weights]
            + unread(after),
            out_specs=[
                pl.BlockSpec((step, w.shape[0]), lambda h, i, w: (h * count + i, 0))
                for w in weights
            ],
        ),
        out_shape=[jax.ShapeDtypeStruct((2 * half, w.shape[0]), bf16) for w in weights],
        compiler_params=params(8),
        cost_estimate=cost(4 * half * sum(w.size for w in weights), half * full * 10),
        name="heads_back",
    )(which, keep, other, *weights, *after)


def attend_back_kernel(
    prefix, lengths_ref, pads_ref, qkv_ref, do_ref, kv_ref, lse_ref, *refs
):
    dqkv_ref, dpk_ref, dpv_ref, norm_ref, order_ref, *sums = refs[-9:]
    length, width = do_ref.shape
    pairs = width // (2 * HEAD_DIM)
    first = head_masks()
    front_bias = prefix_bias(prefix)
    for pair in range(pairs):
        norm_ref[pair] = lse_ref[:, pair * 2 * HEAD_DIM : (pair + 1) * 2 * HEAD_DIM]
    for ref in (dpk_ref, dpv_ref, *sums):
        ref[...] = jnp.zeros_like(ref)
    factor = HEAD_DIM**-0.5

    def back(blocks, window):
        for number, block in enumerate(blocks):
            dk_ref, dv_ref = sums[2 * number : 2 * number + 2]
            rows = pl.ds(pl.multiple_of(block * QB, QB), QB)
            start = window_start(block, window)
            keys_at = pl.ds(start, window)
            bias = window_bias(block, start, window, length, lengths_ref, pads_ref)
            for pair in range(pairs):
                at = pair * 2 * HEAD_DIM
                cols = slice(at, at + 2 * HEAD_DIM)
                k = qkv_ref[keys_at, width + at : width + at + 2 * HEAD_DIM]
                v = qkv_ref[keys_at, 2 * width + at : 2 * width + at + 2 * HEAD_DIM]
                pk = kv_ref[:PAD, cols].astype(bf16)
                pv = kv_ref[PAD:, cols].astype(bf16)
                q = both_heads(qkv_ref[rows, cols] * jnp.asarray(factor, bf16), first)
                do = both_heads(do_ref[rows, cols], first)
                lse = jnp.concatenate(
                    [
                        norm_ref[pair, pl.ds(2 * block, 1), :],
                        norm_ref[pair, pl.ds(2 * block + 1, 1), :],
                    ],
                    axis=1,
                )
                inside = jnp.exp(nt(k, q) + bias - lse)
                front = jnp.exp(nt(pk, q) + front_bias - lse)
                d_inside = nt(v, do)
                d_front = nt(pv, do)
                delta = jnp.sum(inside * d_inside, axis=0, keepdims=True) + jnp.sum(
                    front * d_front, axis=0, keepdims=True
                )
                s_inside = (inside * (d_inside - delta)).astype(bf16)
                s_front = (front * (d_front - delta)).astype(bf16)
                dk_ref[keys_at, cols] += nn(s_inside, q)
                dv_ref[keys_at, cols] += nn(inside.astype(bf16), do)
                dpk_ref[:, cols] += nn(s_front, q)
                dpv_ref[:, cols] += nn(front.astype(bf16), do)
                dq = own_quadrants(tn(k, s_inside) + tn(pk, s_front)).T * factor
                dqkv_ref[rows, cols] = dq.astype(bf16)

    by_window(length, lengths_ref, order_ref, back)
    dqkv_ref[:, width : 2 * width] = (sums[0][...] + sums[2][...]).astype(bf16)
    dqkv_ref[:, 2 * width :] = (sums[1][...] + sums[3][...]).astype(bf16)


def attend_back(prefix, parcel, lengths, pads, qkv, grad, out, after=(), weight=1):
    length, width = parcel.length, parcel.width
    lse_rows = parcel.bias - parcel.lse
    return pl.pallas_call(
        functools.partial(attend_back_kernel, prefix),
        grid=(1,),
        in_specs=[pl.BlockSpec(memory_space=pltpu.SMEM)] * 2
        + [
            once(qkv.shape, (0, 0)),
            once(grad.shape, (0, 0)),
            parcel.part(parcel.kv, 2 * PAD),
            parcel.part(parcel.lse, lse_rows),
        ]
        + unread(after),
        out_specs=[
            once((length, 3 * width), (0, 0)),
            once((PAD, width), (0, 0)),
            once((PAD, width), (0, 0)),
        ],
        out_shape=[
            jax.ShapeDtypeStruct((length, 3 * width), bf16),
            jax.ShapeDtypeStruct((PAD, width), f32),
            jax.ShapeDtypeStruct((PAD, width), f32),
        ],
        scratch_shapes=[
            pltpu.VMEM((width // (2 * HEAD_DIM), lse_rows, 2 * HEAD_DIM), f32),
            pltpu.SMEM((length // QB,), jnp.int32),
        ]
        + [pltpu.VMEM((length, width), f32)] * 4,
        compiler_params=params(14),
        cost_estimate=cost(
            weight * 20 * length * (SPAN + QB) * width,
            length * width * 40,
            length * (SPAN + QB) * width // HEAD_DIM,
        ),
        name="attend_back",
    )(lengths, pads, qkv, grad, out, out, *after)


def pass_kernel(*refs):
    del refs


def held(values, after):
    count = len(values)
    return pl.pallas_call(
        pass_kernel,
        in_specs=unread(values) + unread(after),
        out_specs=unread(values),
        out_shape=[jax.ShapeDtypeStruct(v.shape, v.dtype) for v in values],
        input_output_aliases={i: i for i in range(count)},
        compiler_params=params(1),
        cost_estimate=cost(0, 0),
        name="held",
    )(*values, *after)


def pick_kernel(count, which_ref, *refs):
    weights, outs = refs[:count], refs[-2 * count - 1 : -count - 1]
    buffers, sems = refs[-count - 1 : -1], refs[-1]
    copies = []
    for number, (ref, buffer) in enumerate(zip(weights, buffers)):
        size = buffer.shape[-2]
        rows = pl.ds(pl.multiple_of(which_ref[number] * size, size), size)
        source = ref.at[rows, :] if len(ref.shape) == 2 else ref.at[:, rows, :]
        copies.append(pltpu.make_async_copy(source, buffer, sems.at[number]))
        copies[-1].start()
    for copy, buffer, out_ref in zip(copies, buffers, outs):
        copy.wait()
        out_ref[...] = buffer[...].astype(f32)


def joined_kernel(count, which_ref, w_ref, *refs):
    out_ref, buffer, sems = refs[-3:]
    lead, size = w_ref.shape[0], buffer.shape[-2]
    copies = []
    for number in range(count):
        rows = pl.ds(pl.multiple_of(which_ref[number] * size, size), size)
        part = buffer.at[number * lead : (number + 1) * lead]
        copies.append(pltpu.make_async_copy(w_ref.at[:, rows, :], part, sems.at[number]))
        copies[-1].start()
    for copy in copies:
        copy.wait()
    out_ref[...] = buffer[...].astype(f32)


def joined(whiches, weight, after=()):
    count, size = len(whiches), weight.shape[1] // RING
    whole = (count * weight.shape[0], size, weight.shape[2])
    return pl.pallas_call(
        functools.partial(joined_kernel, count),
        grid=(1,),
        in_specs=[
            pl.BlockSpec(memory_space=pltpu.SMEM),
            pl.BlockSpec(memory_space=pltpu.HBM),
        ]
        + unread(after),
        out_specs=once(whole, (0, 0, 0)),
        out_shape=jax.ShapeDtypeStruct(whole, f32),
        scratch_shapes=[pltpu.VMEM(whole, bf16), pltpu.SemaphoreType.DMA((count,))],
        compiler_params=params(4),
        cost_estimate=cost(0, whole[0] * size * whole[2] * 6),
        name="joined",
    )(jnp.concatenate(whiches), *in_hbm([weight]), *after)


def picked(whiches, weights, after=()):
    shapes = [(*w.shape[:-2], w.shape[-2] // RING, w.shape[-1]) for w in weights]
    return pl.pallas_call(
        functools.partial(pick_kernel, len(weights)),
        grid=(1,),
        in_specs=[pl.BlockSpec(memory_space=pltpu.SMEM)]
        + [pl.BlockSpec(memory_space=pltpu.HBM)] * len(weights)
        + unread(after),
        out_specs=[once(shape, (0,) * len(shape)) for shape in shapes],
        out_shape=[jax.ShapeDtypeStruct(shape, f32) for shape in shapes],
        scratch_shapes=[pltpu.VMEM(shape, bf16) for shape in shapes]
        + [pltpu.SemaphoreType.DMA((len(weights),))],
        compiler_params=params(6),
        cost_estimate=cost(0, sum(shape[-2] * shape[-1] for shape in shapes) * 6),
        name="pick",
    )(jnp.concatenate(whiches), *in_hbm(weights), *after)


def assemble_kernel(shifts, folded, order_ref, *refs):
    out_ref = refs[-1]
    pieces = refs[: len(shifts)]
    size = pieces[0].shape[-2]
    for shift, ref in zip(shifts, pieces):
        at = lax.rem(order_ref[0] + (shift + RING), RING) * size
        rows = pl.ds(pl.multiple_of(at, size), size)
        if folded and ref is pieces[-1]:
            width = ref.shape[1]
            for i in range(out_ref.shape[1] // width):
                block = ref[i * size : (i + 1) * size, :]
                out_ref[rows, i * width : (i + 1) * width] = block.astype(bf16)
        else:
            out_ref[..., rows, :] = ref[...].astype(bf16)


def assembled(order, shifts, pieces, last_specs, folded=False, after=()):
    shape = pieces[0].shape
    zeros = (0,) * len(shape)
    whole = (*shape[:-2], shape[-2] * RING, shape[-1])
    return pl.pallas_call(
        functools.partial(assemble_kernel, shifts, folded),
        grid=(1,),
        in_specs=[pl.BlockSpec(memory_space=pltpu.SMEM)]
        + [once(shape, zeros)] * (len(pieces) - len(last_specs))
        + last_specs
        + unread(after),
        out_specs=once(whole, zeros),
        out_shape=jax.ShapeDtypeStruct(whole, bf16),
        compiler_params=params(6),
        cost_estimate=cost(0, shape[-2] * RING * shape[-1] * 6),
        name="assemble",
    )(order, *pieces, *after)


def product_kernel(pieces, which_ref, *refs):
    total = None
    for a_ref, b_ref in zip(refs[:pieces], refs[pieces : 2 * pieces]):
        part = nn(a_ref[...].astype(bf16), b_ref[...])
        total = part if total is None else total + part
    refs[-1][...] = total


def half_product(which, half, lefts, rights, after=(), weight=1):
    columns = rights[0].shape[1]
    step = 256
    count = half // step
    depth = sum(b.shape[0] for b in rights)
    return pl.pallas_call(
        functools.partial(product_kernel, len(lefts)),
        grid_spec=pltpu.PrefetchScalarGridSpec(
            num_scalar_prefetch=1,
            grid=(count,),
            in_specs=[
                pl.BlockSpec((step, a.shape[1]), lambda i, w: (w[0] * count + i, 0)) for a in lefts
            ]
            + [once(b.shape, (0, 0)) for b in rights]
            + unread(after),
            out_specs=pl.BlockSpec((step, columns), lambda i, w: (i, 0)),
        ),
        out_shape=jax.ShapeDtypeStruct((half, columns), f32),
        compiler_params=params(6),
        cost_estimate=cost(
            weight * 2 * half * columns * depth, half * columns * 4 + depth * columns * 2
        ),
        name="half_product",
    )(which, *lefts, *rights, *after)


def unproject_kernel(pieces, which_ref, *refs):
    total = None
    for grad_ref, w_ref in zip(refs[:pieces], refs[pieces : 2 * pieces]):
        width = w_ref.shape[2]
        part = None
        for i in range(3):
            product = nt(grad_ref[:, i * width : (i + 1) * width], w_ref[i])
            part = product if part is None else part + product
        total = part if total is None else total + part
    refs[-1][...] = total


def unproject(which, grads, weights, after=()):
    full, width = weights[0].shape[1:]
    half = grads[0].shape[0] // 2
    step = 256
    count = half // step
    return pl.pallas_call(
        functools.partial(unproject_kernel, len(weights)),
        grid_spec=pltpu.PrefetchScalarGridSpec(
            num_scalar_prefetch=1,
            grid=(count,),
            in_specs=[pl.BlockSpec((step, 3 * width), lambda i, w: (w[0] * count + i, 0))]
            * len(grads)
            + [once(w.shape, (0, 0, 0)) for w in weights]
            + unread(after),
            out_specs=pl.BlockSpec((step, full), lambda i, w: (i, 0)),
        ),
        out_shape=jax.ShapeDtypeStruct((half, full), f32),
        compiler_params=params(4),
        cost_estimate=cost(6 * half * full * width * len(weights), half * full * 8),
        name="unproject",
    )(which, *grads, *weights, *after)


def norm_two_kernel(which_ref, x_ref, a_ref, b_ref, vec_ref, *refs):
    middle_ref, normed_ref = refs[-2:]
    middle = x_ref[...].astype(f32) + (a_ref[...] + b_ref[...]) + vector(vec_ref, OUT_BIAS)
    middle_ref[...] = middle
    hat, _ = normalize(middle)
    normed = hat * vector(vec_ref, GAIN_TWO) + vector(vec_ref, SHIFT_TWO)
    normed_ref[...] = normed.astype(bf16).astype(f32)


def norm_two(which, x, terms, vectors, after=()):
    half, width = terms[0].shape
    step = 128
    count = half // step
    block = pl.BlockSpec((step, width), lambda i, w: (i, 0))
    return pl.pallas_call(
        norm_two_kernel,
        grid_spec=pltpu.PrefetchScalarGridSpec(
            num_scalar_prefetch=1,
            grid=(count,),
            in_specs=[pl.BlockSpec((step, width), lambda i, w: (w[0] * count + i, 0))]
            + [block] * 2
            + [once(vectors.shape, (0, 0))]
            + unread(after),
            out_specs=[block] * 2,
        ),
        out_shape=[jax.ShapeDtypeStruct((half, width), f32)] * 2,
        compiler_params=params(6),
        cost_estimate=cost(half * width * 12, half * width * 20),
        name="norm_two",
    )(which, x, *terms, vectors, *after)


def mlp_kernel(has_sum, which_ref, n_ref, g_ref, fc_ref, proj_ref, bias_ref, *refs):
    feed_ref, back_ref, act_ref, grad_ref = refs[-4:]
    normed = n_ref[...].astype(bf16)
    grad = g_ref[...]
    units, step = fc_ref.shape[1], bias_ref.shape[1]
    for number, at in enumerate(range(0, units, step)):
        cols = slice(at, at + step)
        hidden = nn(normed, fc_ref[:, cols]) + bias_ref[number : number + 1, :]
        square = hidden * hidden
        inner = jnp.tanh(hidden * (0.7978845608028654 + 0.7978845608028654 * 0.044715 * square))
        gate = 0.5 + 0.5 * inner
        act_ref[:, cols] = (hidden * gate).astype(bf16)
        slope = gate + (0.5 * hidden) * (1.0 - inner * inner) * (
            0.7978845608028654 + 3.0 * 0.7978845608028654 * 0.044715 * square
        )
        grad_ref[:, cols] = (nt(grad, proj_ref[cols, :]) * slope).astype(bf16)
    feed = nn(act_ref[...], proj_ref[...])
    back = nt(grad_ref[...], fc_ref[...])
    if has_sum:
        feed = feed + refs[0][...]
        back = back + refs[1][...]
    feed_ref[...] = feed
    back_ref[...] = back


def mlp(which, normed, cotangent, fc, proj, bias, bias_spec, sums=(), after=(), weight=1):
    half, width = normed.shape
    units = fc.shape[1]
    step = 256
    count = half // step
    block = pl.BlockSpec((step, width), lambda i, w: (i, 0))
    return pl.pallas_call(
        functools.partial(mlp_kernel, bool(sums)),
        grid_spec=pltpu.PrefetchScalarGridSpec(
            num_scalar_prefetch=1,
            grid=(count,),
            in_specs=[
                block,
                pl.BlockSpec((step, width), lambda i, w: (w[0] * count + i, 0)),
                once(fc.shape, (0, 0)),
                once(proj.shape, (0, 0)),
                bias_spec,
            ]
            + [block] * len(sums)
            + unread(after),
            out_specs=[block] * 2,
            scratch_shapes=[pltpu.VMEM((step, units), bf16)] * 2,
        ),
        out_shape=[jax.ShapeDtypeStruct((half, width), f32)] * 2,
        compiler_params=params(14),
        cost_estimate=cost(
            weight * 8 * half * width * units, half * width * 16 + 4 * width * units, half * units
        ),
        name="mlp",
    )(which, normed, cotangent, fc, proj, bias, *sums, *after)


def norm_two_back_kernel(which_ref, g_ref, a_ref, b_ref, middle_ref, vec_ref, *refs):
    hat, scale = normalize(middle_ref[...])
    grad = (a_ref[...] + b_ref[...]) * vector(vec_ref, GAIN_TWO)
    refs[-1][...] = g_ref[...].astype(f32) + norm_back(grad, hat, scale)


def norm_two_back(which, cotangent, a, b, middle, vectors, after=()):
    half, width = a.shape
    step = 128
    count = half // step
    block = pl.BlockSpec((step, width), lambda i, w: (i, 0))
    return pl.pallas_call(
        norm_two_back_kernel,
        grid_spec=pltpu.PrefetchScalarGridSpec(
            num_scalar_prefetch=1,
            grid=(count,),
            in_specs=[
                pl.BlockSpec((step, width), lambda i, w: (w[0] * count + i, 0)),
                block,
                block,
                block,
                once(vectors.shape, (0, 0)),
            ]
            + unread(after),
            out_specs=block,
        ),
        out_shape=jax.ShapeDtypeStruct((half, width), f32),
        compiler_params=params(7),
        cost_estimate=cost(half * width * 20, half * width * 18),
        name="norm_two_back",
    )(which, cotangent, a, b, middle, vectors, *after)


def norm_one_back_kernel(which_ref, x_ref, upper_ref, vec_ref, a_ref, b_ref, *refs):
    hat, scale = normalize(x_ref[...].astype(f32))
    grad = (a_ref[...] + b_ref[...]) * vector(vec_ref, GAIN_ONE)
    refs[-2][...] = upper_ref[...] + norm_back(grad, hat, scale)
    refs[-1][...] = jnp.zeros_like(refs[-1])


def norm_one_back(which, x, upper, vectors, a, b, whole=(), after=()):
    half, width = upper.shape
    step = 128
    count = half // step
    block = pl.BlockSpec((step, width), lambda i, w: (i, 0))
    placed = pl.BlockSpec((step, width), lambda i, w: (w[0] * count + i, 0))
    return pl.pallas_call(
        norm_one_back_kernel,
        grid_spec=pltpu.PrefetchScalarGridSpec(
            num_scalar_prefetch=1,
            grid=(count,),
            in_specs=[placed, block, once(vectors.shape, (0, 0)), block, block]
            + unread(whole)
            + unread(after),
            out_specs=[placed, once((8, 128), (0, 0))],
        ),
        out_shape=[
            jax.ShapeDtypeStruct((2 * half, width), f32),
            jax.ShapeDtypeStruct((8, 128), f32),
        ],
        input_output_aliases={6: 0} if whole else {},
        compiler_params=params(6),
        cost_estimate=cost(half * width * 20, half * width * 18),
        name="norm_one_back",
    )(which, x, upper, vectors, a, b, *whole, *after)


def result_kernel(which_ref, a_ref, b_ref, middle_ref, vec_ref, *refs):
    half_ref, whole_ref, token_ref = refs[-3:]
    token_ref[...] = jnp.zeros_like(token_ref)
    result = middle_ref[...] + (a_ref[...] + b_ref[...]) + vector(vec_ref, PROJ_BIAS)
    half_ref[...] = result
    whole_ref[...] = result.astype(bf16)


def result_half(which, a, b, middle, vectors, after=(), weight=1):
    half, width = middle.shape
    step = 128
    count = half // step
    block = pl.BlockSpec((step, width), lambda i, w: (i, 0))
    placed = pl.BlockSpec((step, width), lambda i, w: (w[0] * count + i, 0))
    return pl.pallas_call(
        result_kernel,
        grid_spec=pltpu.PrefetchScalarGridSpec(
            num_scalar_prefetch=1,
            grid=(count,),
            in_specs=[block, block, block, once(vectors.shape, (0, 0))] + unread(after),
            out_specs=[block, placed, once((8, 128), (0, 0))],
        ),
        out_shape=[
            jax.ShapeDtypeStruct((half, width), f32),
            jax.ShapeDtypeStruct((2 * half, width), bf16),
            jax.ShapeDtypeStruct((8, 128), f32),
        ],
        compiler_params=params(6),
        cost_estimate=cost(weight * half * width * 2048, half * width * 18),
        name="result",
    )(which, a, b, middle, vectors, *after)


def place_kernel(which_ref, half_ref, *refs):
    refs[-2][...] = half_ref[...].astype(refs[-2].dtype)
    refs[-1][...] = jnp.zeros_like(refs[-1])


def placed_half(which, half_values, whole, after=()):
    half, width = half_values.shape
    step = 128
    count = half // step
    return pl.pallas_call(
        place_kernel,
        grid_spec=pltpu.PrefetchScalarGridSpec(
            num_scalar_prefetch=1,
            grid=(count,),
            in_specs=[pl.BlockSpec((step, width), lambda i, w: (i, 0))]
            + unread([whole])
            + unread(after),
            out_specs=[
                pl.BlockSpec((step, width), lambda i, w: (w[0] * count + i, 0)),
                once((8, 128), (0, 0)),
            ],
        ),
        out_shape=[
            jax.ShapeDtypeStruct(whole.shape, whole.dtype),
            jax.ShapeDtypeStruct((8, 128), f32),
        ],
        input_output_aliases={2: 0},
        compiler_params=params(3),
        cost_estimate=cost(0, half * width * 8),
        name="place",
    )(which, half_values, whole, *after)


def parts(values):
    high = values.astype(bf16)
    return high, (values - high.astype(f32)).astype(bf16)


def prefix_kernel(a_ref, b_ref, trunk_ref, embed_ref, w1_ref, *refs):
    w1_grad_ref, w2_grad_ref, b1_grad_ref, b2_grad_ref, embed_grad_ref = refs[-5:]
    columns = w2_grad_ref.shape[2]
    wide = w2_grad_ref.shape[1] * columns
    both = a_ref[:PAD, :] + b_ref[:PAD, :]
    kv, trunk = both[:, :wide], trunk_ref[...]
    pre = both[:, wide:] * (1.0 - trunk * trunk)
    pre_high, pre_low = parts(pre)
    embed = embed_ref[...]
    w1_grad_ref[...] = tn(
        jnp.concatenate([embed, embed], axis=0), jnp.concatenate([pre_high, pre_low], axis=0)
    )
    rows = nt(jnp.concatenate([pre_high, pre_low], axis=0), w1_ref[...])
    embed_grad_ref[...] = rows[:PAD] + rows[PAD:]
    b1_grad_ref[...] = jnp.sum(pre, axis=0, keepdims=True)
    b2_grad = jnp.sum(kv, axis=0, keepdims=True)
    trunk_high, trunk_low = parts(trunk)
    kv_high, kv_low = parts(kv)
    w2_grad = tn(
        jnp.concatenate([trunk_high, trunk_high, trunk_low], axis=0),
        jnp.concatenate([kv_high, kv_low, kv_high], axis=0),
    )
    for i in range(w2_grad_ref.shape[1]):
        cols = slice(i * columns, (i + 1) * columns)
        w2_grad_ref[:, i, :] = w2_grad[:, cols]
        b2_grad_ref[i : i + 1, :] = b2_grad[:, cols]


def prefix_grads(a, b, trunk, embed, w1, width, after=()):
    full, rank = w1.shape
    shapes = [(full, rank), (rank, 2, width), (1, rank), (2, width), (PAD, full)]
    return pl.pallas_call(
        prefix_kernel,
        grid=(1,),
        in_specs=[once(v.shape, (0, 0)) for v in (a, b, trunk, embed, w1)] + unread(after),
        out_specs=[once(shape, (0,) * len(shape)) for shape in shapes],
        out_shape=[jax.ShapeDtypeStruct(shape, f32) for shape in shapes],
        compiler_params=params(16),
        cost_estimate=cost(0, full * rank * 8),
        name="prefix_grads",
    )(a, b, trunk, embed, w1, *after)


def shards(
    group,
    copies,
    tokens,
    cotangent,
    seg_lengths,
    pad_counts,
    ln1_gain,
    ln1_shift,
    qkv_weight,
    qkv_bias,
    out_weight,
    out_bias,
    ln2_gain,
    ln2_shift,
    fc_weight,
    fc_bias,
    proj_weight,
    proj_bias,
    prefix_embed,
    reparam_w1,
    reparam_b1,
    reparam_w2,
    reparam_b2,
):
    rows_here, length, width = tokens.shape
    assert rows_here == 1 and copies % RING == 0
    local_width = qkv_weight.shape[2]
    prefix = prefix_embed.shape[0]
    half = length // 2
    parcel = Parcel(length, local_width, width)
    place = lax.axis_index("tensor")
    core = place % CORES
    mine = core.reshape(1).astype(jnp.int32)
    theirs = 1 - mine
    none = mine * 0
    far_shifts = [CORES * s for s in range(1, group // CORES)]

    def to_core(values):
        return lax.ppermute(values, "tensor", [(t, t ^ 1) for t in range(group)])

    def to_far(values):
        return [
            lax.ppermute(values, "tensor", [(t, (t + shift) % group) for t in range(group)])
            for shift in far_shifts
        ]

    def swapped(values, axis, size, step):
        return values + lax.ppermute(values, axis, [(i, i ^ step) for i in range(size)])

    ring = list(range(0, RING, 2)) + list(range(RING - 1, 0, -2))
    member = lax.axis_index("dp") % RING
    order = jnp.where(member % 2 == 0, member // 2, RING - 1 - member // 2)
    here = order.reshape(1).astype(jnp.int32)
    across = (here + RING // 2) % RING
    hops = RING // 2 - 1

    def along(values, step):
        hop = [
            (base + ring[i], base + ring[(i + step) % RING])
            for base in range(0, copies, RING)
            for i in range(RING)
        ]
        return lax.ppermute(values, "dp", hop)

    def hop(rings):
        for levels in rings:
            up, down = levels[-1]
            levels.append((along(up, 1), along(down, -1)))

    def last(rings):
        return [piece for levels in rings for piece in levels[-1]]

    def hold(rings, after):
        for levels in rings:
            up, down = levels[-1]
            if up is down:
                up = down = held([up], after)[0]
            else:
                up, down = held([up, down], after)
            levels[-1] = (up, down)

    def starting(pieces):
        return [[(piece, piece)] for piece in pieces]

    def rebuilt(levels, facing, spec, folded=False, after=()):
        shifts, pieces = [0], [levels[0][0]]
        for number, (up, down) in enumerate(levels[1:]):
            shifts += [-1 - number, number + 1]
            pieces += [up, down]
        return assembled(here, shifts + [RING // 2], pieces + [facing], [spec], folded, after)

    x = tokens.reshape(length, width)
    grad_out = cotangent.reshape(length, width)
    lengths = seg_lengths.reshape(-1)
    qkv_w = jnp.transpose(qkv_weight, (1, 0, 2))
    vectors = jnp.stack([ln1_gain, ln1_shift, out_bias, ln2_gain, ln2_shift, proj_bias])
    vectors = jnp.pad(vectors, ((0, 2), (0, 0))).astype(f32)

    (piece_fc,) = picked([here], [fc_weight])
    near_fc = to_far(piece_fc)
    (piece_out,) = picked([here], [out_weight], [piece_fc])
    near_out = to_far(piece_out)
    (piece_proj,) = picked([here], [proj_weight], [piece_out])
    near_proj = to_far(piece_proj)
    ring_out, ring_fc, ring_proj = starting(near_out), starting(near_fc), starting(near_proj)

    fc_rows = fc_bias.astype(f32).reshape(-1, local_width)
    biases = jnp.concatenate(
        [
            jnp.pad(qkv_bias.astype(f32), ((0, 5), (0, 0))),
            jnp.pad(fc_rows, ((0, 8 - fc_rows.shape[0]), (0, 0))),
        ],
        axis=0,
    )
    qkv_bias_spec = once((8, local_width), (0, 0))
    fc_bias_spec = once((8, local_width), (1, 0))
    qkv, normed_one = project(True, in_hbm([x])[0], vectors, qkv_w, biases, qkv_bias_spec)

    embed = prefix_embed.astype(f32)
    trunk_weight = reparam_w1.astype(f32)
    head_weight = reparam_w2.astype(f32)
    trunk = jnp.tanh(jnp.dot(embed, trunk_weight, precision=highest) + reparam_b1.astype(f32))
    kv_values = jnp.einsum(
        "pr,rtd->ptd", trunk, head_weight, precision=highest
    ) + reparam_b2.astype(f32)
    flat_kv = jnp.pad(kv_values, ((0, PAD - prefix), (0, 0), (0, 0)))
    prefix_kv = jnp.concatenate([flat_kv[:, 0], flat_kv[:, 1]], axis=0)

    hold(ring_fc, [qkv])
    fc_held = last(ring_fc)
    hop(ring_fc)
    hold(ring_out, [qkv])
    out_held = last(ring_out)
    hop(ring_out)
    out, token = attend(
        prefix, parcel, lengths, pad_counts, qkv, prefix_kv, biases, fc_held + out_held
    )
    out = pack(across, parcel, out, out_weight, last(ring_fc) + last(ring_out))
    out = held([out], [token])[0]
    far_out_parcel = to_far(out)
    hold(ring_out, [out])
    out_held = last(ring_out)
    hop(ring_out)
    hold(ring_proj, out_held)
    hop(ring_proj)
    second_out = last(ring_out)
    hop(ring_out)
    hold(ring_fc, last(ring_proj) + second_out)
    hop(ring_fc)
    hold(ring_proj, last(ring_out))
    hop(ring_proj)
    across_fc, across_proj, piece_qkv, across_qkv = picked(
        [across, across, here, across], [fc_weight, proj_weight, qkv_w, qkv_w], last(ring_out)
    )
    far_places = [-hops, hops]
    pieces_qkv = joined(
        [(here + place + RING) % RING for place in far_places], qkv_w, [piece_qkv]
    )
    far_out = [
        rebuilt(levels, far, parcel.part(length, parcel.piece), True, [pieces_qkv])
        for levels, far in zip(ring_out, far_out_parcel)
    ]
    lefts = [out] + far_out_parcel
    rights = [out_weight] + far_out
    send = half_product(theirs, half, lefts, rights, last(ring_fc))
    received = to_core(send)
    keep = half_product(mine, half, lefts, rights, [send], KEEP)
    facing_fc = to_far(held([across_fc], last(ring_fc))[0])
    hold(ring_fc, last(ring_proj))
    fc_held = last(ring_fc)
    hop(ring_fc)
    middle, normed = norm_two(mine, x, [keep, received], vectors, fc_held)
    other_normed = to_core(normed)
    own = (fc_weight, proj_weight, biases, fc_bias_spec)
    keep_sums = mlp(mine, normed, grad_out, *own, (), (), OWN)
    hold(ring_proj, [other_normed])
    hop(ring_proj)
    near_qkv = to_far(held([piece_qkv], [normed])[0])
    facing_proj = to_far(held([across_proj], facing_fc + [keep_sums[0]])[0])
    fc_spec, proj_spec = once(piece_fc.shape, (0, 0)), once(piece_proj.shape, (0, 0))
    send_sums = mlp(
        theirs, other_normed, grad_out, *own, (), [keep_sums[0]] + last(ring_fc)
    )
    ring_qkv = starting(near_qkv)
    hold(ring_qkv, [send_sums[0]] + last(ring_fc))
    hop(ring_qkv)
    far_fc = [
        rebuilt(levels, piece, fc_spec, False, [send_sums[0]])
        for levels, piece in zip(ring_fc, facing_fc)
    ]
    far_proj = [
        rebuilt(levels, piece, proj_spec, False, far_fc)
        for levels, piece in zip(ring_proj, facing_proj)
    ]
    far_bias_spec = parcel.part(parcel.bias + 8, 8)
    for fc, proj, far in zip(far_fc, far_proj, far_out_parcel):
        send_sums = mlp(
            theirs, other_normed, grad_out, fc, proj, far, far_bias_spec, send_sums, (), LIGHT
        )
    back_received = to_core(send_sums[1])
    for fc, proj, far in zip(far_fc, far_proj, far_out_parcel):
        keep_sums = mlp(
            mine,
            normed,
            grad_out,
            fc,
            proj,
            far,
            far_bias_spec,
            keep_sums,
            [send_sums[0]],
            FAR,
        )
    facing_qkv = to_far(held([across_qkv], near_qkv + [send_sums[0]])[0])
    upper = norm_two_back(
        mine, grad_out, keep_sums[1], back_received, middle, vectors
    )
    hold(ring_qkv, [upper])
    q_held = last(ring_qkv)
    hop(ring_qkv)
    other_upper = to_core(upper)
    feed_received = to_core(send_sums[0])
    result, mixed, result_token = result_half(
        mine, keep_sums[0], feed_received, middle, vectors, q_held + facing_qkv, FAR
    )
    other_result = to_core(result)
    ends_qkv = to_far(held([pieces_qkv], [upper])[0])

    grads_far = heads_back(
        mine, upper, other_upper, [out_weight] + far_out, [result_token]
    )
    dqkv, grad_keys, grad_vals = attend_back(
        prefix,
        parcel,
        lengths,
        pad_counts,
        qkv,
        grads_far[0],
        out,
        (),
        LIGHT,
    )

    grad_keys, grad_vals = held([grad_keys, grad_vals], last(ring_qkv))
    grad_here = jnp.concatenate([grad_keys, grad_vals], axis=1)
    flat_head = jnp.transpose(head_weight, (1, 2, 0)).reshape(2 * local_width, -1)
    trunk_here = jnp.dot(grad_here, flat_head, precision=highest)
    for_tensor = [("tensor", group, 1 << i) for i in range(group.bit_length() - 1)]
    for_dp = [("dp", copies, 1 << i) for i in reversed(range(copies.bit_length() - 1))]
    mixed, token = placed_half(theirs, other_result, mixed, [dqkv])
    far_qkv = []
    for levels, facing, pieces in zip(ring_qkv, facing_qkv, ends_qkv):
        shifts, found = [0], [levels[0][0]]
        for number, ends in enumerate(levels[1:]):
            shifts += [-1 - number, number + 1]
            found += list(ends)
        shifts, found = shifts + [RING // 2], found + [facing]
        specs = [once(piece_qkv.shape, (i, 0, 0)) for i in range(len(far_places))]
        far_qkv.append(
            assembled(here, shifts + far_places, found + [pieces] * len(far_places), specs, False, [token])
        )
    qkvs = [qkv_w] + far_qkv
    trunk_here = swapped(trunk_here, *for_tensor[0])
    far_projected = [
        project(
            False,
            in_hbm([normed_one])[0],
            vectors,
            weight,
            far,
            parcel.part(parcel.bias, 8),
            [trunk_here],
        )[0]
        for weight, far in zip(far_qkv, far_out_parcel)
    ]
    for step in for_tensor[1:]:
        trunk_here = swapped(trunk_here, *step)
    grads = [dqkv]
    for number, far in enumerate(far_out_parcel):
        found = attend_back(
            prefix,
            parcel,
            lengths,
            pad_counts,
            far_projected[number],
            grads_far[1 + number],
            far,
            [trunk_here],
            LIGHT,
        )
        grads.append(found[0])
    both = jnp.concatenate([grad_here, trunk_here], axis=1)
    both = swapped(held([both], far_projected)[0], *for_dp[0])
    both = held([both], grads[-1:])[0]
    send_one = unproject(theirs, grads, qkvs, [both])
    received_one = to_core(send_one)
    both = swapped(both, *for_dp[1])
    keep_one = unproject(mine, grads, qkvs, [send_one, both])
    received_two = to_core(keep_one)
    for step in for_dp[2:-1]:
        both = swapped(both, *step)
    last_step = for_dp[-1]
    other_both = lax.ppermute(both, "dp", [(i, i ^ last_step[2]) for i in range(copies)])
    input_grad, token = norm_one_back(mine, x, upper, vectors, keep_one, received_one)
    w1_grad, w2_grad, b1_grad, b2_grad, embed_grad = prefix_grads(
        both,
        other_both,
        jnp.pad(trunk, ((0, PAD - prefix), (0, 0))),
        jnp.pad(prefix_embed, ((0, PAD - prefix), (0, 0))),
        reparam_w1,
        local_width,
        [token],
    )
    input_grad, _ = norm_one_back(
        theirs, x, other_upper, vectors, send_one, received_two, [input_grad]
    )
    b1_grad, embed_grad = b1_grad.reshape(-1), embed_grad[:prefix]
    mixed, input_grad = mixed.reshape(tokens.shape), input_grad.reshape(tokens.shape)
    return (mixed, input_grad, embed_grad, w1_grad, b1_grad, w2_grad, b2_grad, kv_values)


def solution(mesh):
    return jax.shard_map(
        functools.partial(shards, mesh.shape["tensor"], mesh.shape["dp"]),
        mesh=mesh,
        in_specs=(
            P("dp", None, None),
            P("dp", None, None),
            P("dp", None),
            P("dp"),
            P(),
            P(),
            P(None, None, "tensor"),
            P(None, "tensor"),
            P("tensor", None),
            P(),
            P(),
            P(),
            P(None, "tensor"),
            P("tensor"),
            P("tensor", None),
            P(),
            P(),
            P(),
            P(),
            P(None, None, "tensor"),
            P(None, "tensor"),
        ),
        out_specs=(
            P("dp", None, None),
            P("dp", None, None),
            P(),
            P(),
            P(),
            P(None, None, "tensor"),
            P(None, "tensor"),
            P(None, None, "tensor"),
        ),
        check_vma=False,
    )
```

```python
import functools

import jax
import jax.numpy as jnp
from jax import lax
from jax.experimental import pallas as pl
from jax.experimental.pallas import tpu as pltpu
from jax.sharding import PartitionSpec as P

HEAD_DIM = 64
CORES = 2
QB = 128
SPAN = 384
PAD = 16
RING = 8
LIGHT = 16
KEEP, OWN, FAR = 640, 320, 320
MASKED = -1e30
GAIN_ONE, SHIFT_ONE, OUT_BIAS, GAIN_TWO, SHIFT_TWO, PROJ_BIAS = range(6)
highest = lax.Precision.HIGHEST
epsilon = 1e-05
f32 = jnp.float32
bf16 = jnp.bfloat16


def nn(a, b):
    return jnp.dot(a, b, preferred_element_type=f32)


def nt(a, b):
    return lax.dot_general(a, b, (((1,), (1,)), ((), ())), preferred_element_type=f32)


def tn(a, b):
    return lax.dot_general(a, b, (((0,), (0,)), ((), ())), preferred_element_type=f32)


def params(mib):
    return pltpu.CompilerParams(vmem_limit_bytes=mib * 1024 * 1024)


def in_hbm(values):
    return [pltpu.with_memory_space_constraint(v, pltpu.HBM) for v in values]


def cost(flops, bytes_accessed, transcendentals=0):
    return pl.CostEstimate(
        flops=int(flops) // LIGHT,
        bytes_accessed=int(bytes_accessed) // LIGHT,
        transcendentals=int(transcendentals) // LIGHT,
    )


def unread(after):
    return [pl.BlockSpec(memory_space=pl.ANY)] * len(after)


def once(shape, index):
    return pl.BlockSpec(shape, lambda *_: index, pipeline_mode=pl.Buffered(1))


def vector(ref, number):
    return ref[number : number + 1, :]


def normalize(values):
    centered = values - jnp.mean(values, axis=-1, keepdims=True)
    scale = lax.rsqrt(jnp.mean(centered * centered, axis=-1, keepdims=True) + epsilon)
    return centered * scale, scale


def norm_back(grad, hat, scale):
    mean_grad = jnp.mean(grad, axis=-1, keepdims=True)
    mean_both = jnp.mean(grad * hat, axis=-1, keepdims=True)
    return scale * (grad - mean_grad - hat * mean_both)


class Parcel:
    def __init__(self, length, width, full):
        self.length, self.width, self.full = length, width, full
        self.piece = full // 8
        self.kv = length + self.piece
        self.lse = self.kv + 2 * PAD
        self.bias = self.lse + 2 * (length // QB)
        self.rows = self.bias + 16

    def part(self, start, size):
        assert start % size == 0
        return once((size, self.width), (start // size, 0))


def head_masks():
    lanes = lax.broadcasted_iota(jnp.int32, (QB, 2 * HEAD_DIM), 1)
    return lanes < HEAD_DIM


def both_heads(block, first):
    zero = jnp.zeros_like(block)
    return jnp.concatenate([jnp.where(first, block, zero), jnp.where(first, zero, block)], axis=0)


def own_quadrants(product):
    return jnp.concatenate([product[:HEAD_DIM, :QB], product[HEAD_DIM:, QB:]], axis=0)


def segment_start(position, lengths_ref):
    start, end = jnp.zeros_like(position), jnp.int32(0)
    for number in range(lengths_ref.shape[0]):
        end = end + lengths_ref[number]
        start = jnp.where(position >= end, end, start)
    return start


def by_window(length, lengths_ref, order_ref, run):
    blocks = length // QB
    most = min(length, SPAN + QB) // QB

    def tiles_of(block):
        return block - segment_start(block * QB, lengths_ref) // QB + 1

    def place(block, ends):
        low, high = ends
        small = tiles_of(block) <= most // 2
        order_ref[jnp.where(small, low, high)] = block
        return jnp.where(small, low + 1, low), jnp.where(small, high, high - 1)

    lax.fori_loop(0, blocks, place, (jnp.int32(0), jnp.int32(blocks - 1)))

    def step(number, _):
        pair = order_ref[2 * number], order_ref[2 * number + 1]
        tiles = jnp.maximum(tiles_of(pair[0]), tiles_of(pair[1]))
        for count in (most // 2, most):

            @pl.when((tiles <= count) & (tiles > count - most // 2))
            def _():
                run(pair, count * QB)

        return 0

    lax.fori_loop(0, blocks // 2, step, 0)


def window_bias(block, start, window, length, lengths_ref, pads_ref):
    lanes = lax.broadcasted_iota(jnp.int32, (1, 2 * QB), 1)
    position = block * QB + jnp.where(lanes < QB, lanes, lanes - QB)
    low = segment_start(position, lengths_ref)
    low = jnp.where(position < length - pads_ref[0], low, 4 * length)
    key = start + lax.broadcasted_iota(jnp.int32, (window, 2 * QB), 0)
    return jnp.where((key >= low) & (key <= position), 0.0, MASKED)


def window_start(block, window):
    return pl.multiple_of(jnp.maximum((block + 1) * QB - window, 0), QB)


def prefix_bias(prefix):
    rows = lax.broadcasted_iota(jnp.int32, (PAD, 2 * QB), 0)
    return jnp.where(rows < prefix, 0.0, MASKED)


def project_kernel(first, x_ref, y_ref, vec_ref, w_ref, bias_ref, *refs):
    whole = jnp.concatenate([x_ref[...], y_ref[...]], axis=1)
    if first:
        qkv_ref, normed_ref = refs[-2:]
        hat, _ = normalize(whole.astype(f32))
        normed = (hat * vector(vec_ref, GAIN_ONE) + vector(vec_ref, SHIFT_ONE)).astype(bf16)
        normed_ref[...] = normed
    else:
        qkv_ref = refs[-1]
        normed = whole
    width = w_ref.shape[2]
    for i in range(3):
        part = nn(normed, w_ref[i]) + bias_ref[i : i + 1, :]
        qkv_ref[:, i * width : (i + 1) * width] = part.astype(bf16)


def project(first, x, vectors, weight, bias, bias_spec, after=()):
    length, full = x.shape
    width = weight.shape[2]
    step = 256
    block = pl.BlockSpec((step, full), lambda i: (i, 0))
    specs = [pl.BlockSpec((step, 3 * width), lambda i: (i, 0))]
    shapes = [jax.ShapeDtypeStruct((length, 3 * width), bf16)]
    if first:
        specs.append(block)
        shapes.append(pltpu.HBM((length, full), bf16))
    return pl.pallas_call(
        functools.partial(project_kernel, first),
        grid=(length // step,),
        in_specs=[
            pl.BlockSpec((step, full // 2), lambda i: (i, 0)),
            pl.BlockSpec((step, full // 2), lambda i: (i, 1)),
            once(vectors.shape, (0, 0)),
            once(weight.shape, (0, 0, 0)),
            bias_spec,
        ]
        + unread(after),
        out_specs=specs,
        out_shape=shapes,
        compiler_params=params(4),
        cost_estimate=cost(6 * length * full * width, length * full * 8),
        name="project",
    )(x, x, vectors, weight, bias, *after)


def attend_kernel(
    prefix, parcel, lengths_ref, pads_ref, qkv_ref, kv_ref, bias_ref, *refs
):
    o_ref, token_ref, norm_ref, order_ref = refs[-4:]
    token_ref[...] = jnp.zeros_like(token_ref)
    length, width = parcel.length, parcel.width
    pairs = width // (2 * HEAD_DIM)
    first = head_masks()
    front_bias = prefix_bias(prefix)
    o_ref[parcel.kv : parcel.lse, :] = kv_ref[...]
    o_ref[parcel.bias :, :] = bias_ref[...]

    def attend(blocks, window):
        for block in blocks:
            rows = pl.ds(pl.multiple_of(block * QB, QB), QB)
            start = window_start(block, window)
            keys_at = pl.ds(start, window)
            bias = window_bias(block, start, window, length, lengths_ref, pads_ref)
            for pair in range(pairs):
                at = pair * 2 * HEAD_DIM
                cols = slice(at, at + 2 * HEAD_DIM)
                q = both_heads(qkv_ref[rows, cols] * jnp.asarray(HEAD_DIM**-0.5, bf16), first)
                k = qkv_ref[keys_at, width + at : width + at + 2 * HEAD_DIM]
                v = qkv_ref[keys_at, 2 * width + at : 2 * width + at + 2 * HEAD_DIM]
                pk = kv_ref[:PAD, cols].astype(bf16)
                pv = kv_ref[PAD:, cols].astype(bf16)
                inside = nt(k, q) + bias
                front = nt(pk, q) + front_bias
                largest = jnp.maximum(
                    jnp.max(inside, axis=0, keepdims=True), jnp.max(front, axis=0, keepdims=True)
                )
                inside = jnp.exp(inside - largest)
                front = jnp.exp(front - largest)
                total = jnp.sum(inside, axis=0, keepdims=True) + jnp.sum(
                    front, axis=0, keepdims=True
                )
                scale = 1.0 / total
                out = tn(v, (inside * scale).astype(bf16)) + tn(pv, (front * scale).astype(bf16))
                o_ref[rows, cols] = own_quadrants(out).T
                lse = largest + jnp.log(total)
                norm_ref[pair, pl.ds(2 * block, 1), :] = lse[:, :QB]
                norm_ref[pair, pl.ds(2 * block + 1, 1), :] = lse[:, QB:]

    by_window(length, lengths_ref, order_ref, attend)
    for pair in range(pairs):
        cols = slice(pair * 2 * HEAD_DIM, (pair + 1) * 2 * HEAD_DIM)
        o_ref[parcel.lse : parcel.bias, cols] = norm_ref[pair]


def attend(prefix, parcel, lengths, pads, qkv, prefix_kv, biases, after=()):
    length, width = parcel.length, parcel.width
    return pl.pallas_call(
        functools.partial(attend_kernel, prefix, parcel),
        grid=(1,),
        in_specs=[pl.BlockSpec(memory_space=pltpu.SMEM)] * 2
        + [once(v.shape, (0, 0)) for v in (qkv, prefix_kv, biases)]
        + unread(after),
        out_specs=[once((parcel.rows, width), (0, 0)), once((8, 128), (0, 0))],
        out_shape=[
            jax.ShapeDtypeStruct((parcel.rows, width), f32),
            jax.ShapeDtypeStruct((8, 128), f32),
        ],
        scratch_shapes=[
            pltpu.VMEM((width // (2 * HEAD_DIM), parcel.bias - parcel.lse, 2 * HEAD_DIM), f32),
            pltpu.SMEM((length // QB,), jnp.int32),
        ],
        compiler_params=params(10),
        cost_estimate=cost(
            8 * length * (SPAN + QB) * width,
            length * width * 10,
            length * (SPAN + QB) * width // HEAD_DIM,
        ),
        name="attend",
    )(lengths, pads, qkv, prefix_kv, biases, *after)


def pack_kernel(which_ref, w_ref, *refs):
    out_ref = refs[-1]
    size, width = w_ref.shape[0], out_ref.shape[1]
    for i in range(w_ref.shape[1] // width):
        out_ref[i * size : (i + 1) * size, :] = w_ref[:, i * width : (i + 1) * width].astype(f32)


def pack(which, parcel, out, weight, after=()):
    size = weight.shape[0] // RING
    assert size * (weight.shape[1] // parcel.width) == parcel.piece
    assert parcel.length % parcel.piece == 0
    place = parcel.length // parcel.piece
    return pl.pallas_call(
        pack_kernel,
        grid_spec=pltpu.PrefetchScalarGridSpec(
            num_scalar_prefetch=1,
            grid=(1,),
            in_specs=[pl.BlockSpec((size, weight.shape[1]), lambda i, w: (w[0], 0))]
            + unread([out])
            + unread(after),
            out_specs=pl.BlockSpec((parcel.piece, parcel.width), lambda i, w: (place, 0)),
        ),
        out_shape=jax.ShapeDtypeStruct(out.shape, f32),
        input_output_aliases={2: 0},
        compiler_params=params(2),
        cost_estimate=cost(0, parcel.piece * parcel.width * 6),
        name="pack",
    )(which, weight, out, *after)


def heads_back_kernel(count, core_ref, keep_ref, other_ref, *refs):
    weights, outs = refs[:count], refs[-count:]
    own = pl.program_id(0) == core_ref[0]
    low = jnp.where(own, keep_ref[...], other_ref[...]).astype(bf16)
    for w_ref, out_ref in zip(weights, outs):
        out_ref[...] = nt(low, w_ref[...]).astype(bf16)


def heads_back(which, keep, other, weights, after=()):
    half, full = keep.shape
    step = 256
    count = half // step

    def at_keep(h, i, w):
        return jnp.where(h == w[0], i, (count - 1) * (1 - w[0])), 0

    def at_other(h, i, w):
        return jnp.where(h == w[0], (count - 1) * w[0], i), 0

    return pl.pallas_call(
        functools.partial(heads_back_kernel, len(weights)),
        grid_spec=pltpu.PrefetchScalarGridSpec(
            num_scalar_prefetch=1,
            grid=(2, count),
            in_specs=[pl.BlockSpec((step, full), at_keep), pl.BlockSpec((step, full), at_other)]
            + [once(w.shape, (0, 0)) for w in weights]
            + unread(after),
            out_specs=[
                pl.BlockSpec((step, w.shape[0]), lambda h, i, w: (h * count + i, 0))
                for w in weights
            ],
        ),
        out_shape=[jax.ShapeDtypeStruct((2 * half, w.shape[0]), bf16) for w in weights],
        compiler_params=params(8),
        cost_estimate=cost(4 * half * sum(w.size for w in weights), half * full * 10),
        name="heads_back",
    )(which, keep, other, *weights, *after)


def attend_back_kernel(
    prefix, lengths_ref, pads_ref, qkv_ref, do_ref, kv_ref, lse_ref, *refs
):
    dqkv_ref, dpk_ref, dpv_ref, norm_ref, order_ref, *sums = refs[-9:]
    length, width = do_ref.shape
    pairs = width // (2 * HEAD_DIM)
    first = head_masks()
    front_bias = prefix_bias(prefix)
    for pair in range(pairs):
        norm_ref[pair] = lse_ref[:, pair * 2 * HEAD_DIM : (pair + 1) * 2 * HEAD_DIM]
    for ref in (dpk_ref, dpv_ref, *sums):
        ref[...] = jnp.zeros_like(ref)
    factor = HEAD_DIM**-0.5

    def back(blocks, window):
        for number, block in enumerate(blocks):
            dk_ref, dv_ref = sums[2 * number : 2 * number + 2]
            rows = pl.ds(pl.multiple_of(block * QB, QB), QB)
            start = window_start(block, window)
            keys_at = pl.ds(start, window)
            bias = window_bias(block, start, window, length, lengths_ref, pads_ref)
            for pair in range(pairs):
                at = pair * 2 * HEAD_DIM
                cols = slice(at, at + 2 * HEAD_DIM)
                k = qkv_ref[keys_at, width + at : width + at + 2 * HEAD_DIM]
                v = qkv_ref[keys_at, 2 * width + at : 2 * width + at + 2 * HEAD_DIM]
                pk = kv_ref[:PAD, cols].astype(bf16)
                pv = kv_ref[PAD:, cols].astype(bf16)
                q = both_heads(qkv_ref[rows, cols] * jnp.asarray(factor, bf16), first)
                do = both_heads(do_ref[rows, cols], first)
                lse = jnp.concatenate(
                    [
                        norm_ref[pair, pl.ds(2 * block, 1), :],
                        norm_ref[pair, pl.ds(2 * block + 1, 1), :],
                    ],
                    axis=1,
                )
                inside = jnp.exp(nt(k, q) + bias - lse)
                front = jnp.exp(nt(pk, q) + front_bias - lse)
                d_inside = nt(v, do)
                d_front = nt(pv, do)
                delta = jnp.sum(inside * d_inside, axis=0, keepdims=True) + jnp.sum(
                    front * d_front, axis=0, keepdims=True
                )
                s_inside = (inside * (d_inside - delta)).astype(bf16)
                s_front = (front * (d_front - delta)).astype(bf16)
                dk_ref[keys_at, cols] += nn(s_inside, q)
                dv_ref[keys_at, cols] += nn(inside.astype(bf16), do)
                dpk_ref[:, cols] += nn(s_front, q)
                dpv_ref[:, cols] += nn(front.astype(bf16), do)
                dq = own_quadrants(tn(k, s_inside) + tn(pk, s_front)).T * factor
                dqkv_ref[rows, cols] = dq.astype(bf16)

    by_window(length, lengths_ref, order_ref, back)
    dqkv_ref[:, width : 2 * width] = (sums[0][...] + sums[2][...]).astype(bf16)
    dqkv_ref[:, 2 * width :] = (sums[1][...] + sums[3][...]).astype(bf16)


def attend_back(prefix, parcel, lengths, pads, qkv, grad, out, after=(), weight=1):
    length, width = parcel.length, parcel.width
    lse_rows = parcel.bias - parcel.lse
    return pl.pallas_call(
        functools.partial(attend_back_kernel, prefix),
        grid=(1,),
        in_specs=[pl.BlockSpec(memory_space=pltpu.SMEM)] * 2
        + [
            once(qkv.shape, (0, 0)),
            once(grad.shape, (0, 0)),
            parcel.part(parcel.kv, 2 * PAD),
            parcel.part(parcel.lse, lse_rows),
        ]
        + unread(after),
        out_specs=[
            once((length, 3 * width), (0, 0)),
            once((PAD, width), (0, 0)),
            once((PAD, width), (0, 0)),
        ],
        out_shape=[
            jax.ShapeDtypeStruct((length, 3 * width), bf16),
            jax.ShapeDtypeStruct((PAD, width), f32),
            jax.ShapeDtypeStruct((PAD, width), f32),
        ],
        scratch_shapes=[
            pltpu.VMEM((width // (2 * HEAD_DIM), lse_rows, 2 * HEAD_DIM), f32),
            pltpu.SMEM((length // QB,), jnp.int32),
        ]
        + [pltpu.VMEM((length, width), f32)] * 4,
        compiler_params=params(14),
        cost_estimate=cost(
            weight * 20 * length * (SPAN + QB) * width,
            length * width * 40,
            length * (SPAN + QB) * width // HEAD_DIM,
        ),
        name="attend_back",
    )(lengths, pads, qkv, grad, out, out, *after)


def pass_kernel(*refs):
    del refs


def held(values, after):
    count = len(values)
    return pl.pallas_call(
        pass_kernel,
        in_specs=unread(values) + unread(after),
        out_specs=unread(values),
        out_shape=[jax.ShapeDtypeStruct(v.shape, v.dtype) for v in values],
        input_output_aliases={i: i for i in range(count)},
        compiler_params=params(1),
        cost_estimate=cost(0, 0),
        name="held",
    )(*values, *after)


def pick_kernel(count, which_ref, *refs):
    weights, outs = refs[:count], refs[-2 * count - 1 : -count - 1]
    buffers, sems = refs[-count - 1 : -1], refs[-1]
    copies = []
    for number, (ref, buffer) in enumerate(zip(weights, buffers)):
        size = buffer.shape[-2]
        rows = pl.ds(pl.multiple_of(which_ref[number] * size, size), size)
        source = ref.at[rows, :] if len(ref.shape) == 2 else ref.at[:, rows, :]
        copies.append(pltpu.make_async_copy(source, buffer, sems.at[number]))
        copies[-1].start()
    for copy, buffer, out_ref in zip(copies, buffers, outs):
        copy.wait()
        out_ref[...] = buffer[...].astype(f32)


def joined_kernel(count, which_ref, w_ref, *refs):
    out_ref, buffer, sems = refs[-3:]
    lead, size = w_ref.shape[0], buffer.shape[-2]
    copies = []
    for number in range(count):
        rows = pl.ds(pl.multiple_of(which_ref[number] * size, size), size)
        part = buffer.at[number * lead : (number + 1) * lead]
        copies.append(pltpu.make_async_copy(w_ref.at[:, rows, :], part, sems.at[number]))
        copies[-1].start()
    for copy in copies:
        copy.wait()
    out_ref[...] = buffer[...].astype(f32)


def joined(whiches, weight, after=()):
    count, size = len(whiches), weight.shape[1] // RING
    whole = (count * weight.shape[0], size, weight.shape[2])
    return pl.pallas_call(
        functools.partial(joined_kernel, count),
        grid=(1,),
        in_specs=[
            pl.BlockSpec(memory_space=pltpu.SMEM),
            pl.BlockSpec(memory_space=pltpu.HBM),
        ]
        + unread(after),
        out_specs=once(whole, (0, 0, 0)),
        out_shape=jax.ShapeDtypeStruct(whole, f32),
        scratch_shapes=[pltpu.VMEM(whole, bf16), pltpu.SemaphoreType.DMA((count,))],
        compiler_params=params(4),
        cost_estimate=cost(0, whole[0] * size * whole[2] * 6),
        name="joined",
    )(jnp.concatenate(whiches), *in_hbm([weight]), *after)


def picked(whiches, weights, after=()):
    shapes = [(*w.shape[:-2], w.shape[-2] // RING, w.shape[-1]) for w in weights]
    return pl.pallas_call(
        functools.partial(pick_kernel, len(weights)),
        grid=(1,),
        in_specs=[pl.BlockSpec(memory_space=pltpu.SMEM)]
        + [pl.BlockSpec(memory_space=pltpu.HBM)] * len(weights)
        + unread(after),
        out_specs=[once(shape, (0,) * len(shape)) for shape in shapes],
        out_shape=[jax.ShapeDtypeStruct(shape, f32) for shape in shapes],
        scratch_shapes=[pltpu.VMEM(shape, bf16) for shape in shapes]
        + [pltpu.SemaphoreType.DMA((len(weights),))],
        compiler_params=params(6),
        cost_estimate=cost(0, sum(shape[-2] * shape[-1] for shape in shapes) * 6),
        name="pick",
    )(jnp.concatenate(whiches), *in_hbm(weights), *after)


def assemble_kernel(shifts, folded, order_ref, *refs):
    out_ref = refs[-1]
    pieces = refs[: len(shifts)]
    size = pieces[0].shape[-2]
    for shift, ref in zip(shifts, pieces):
        at = lax.rem(order_ref[0] + (shift + RING), RING) * size
        rows = pl.ds(pl.multiple_of(at, size), size)
        if folded and ref is pieces[-1]:
            width = ref.shape[1]
            for i in range(out_ref.shape[1] // width):
                block = ref[i * size : (i + 1) * size, :]
                out_ref[rows, i * width : (i + 1) * width] = block.astype(bf16)
        else:
            out_ref[..., rows, :] = ref[...].astype(bf16)


def assembled(order, shifts, pieces, last_specs, folded=False, after=()):
    shape = pieces[0].shape
    zeros = (0,) * len(shape)
    whole = (*shape[:-2], shape[-2] * RING, shape[-1])
    return pl.pallas_call(
        functools.partial(assemble_kernel, shifts, folded),
        grid=(1,),
        in_specs=[pl.BlockSpec(memory_space=pltpu.SMEM)]
        + [once(shape, zeros)] * (len(pieces) - len(last_specs))
        + last_specs
        + unread(after),
        out_specs=once(whole, zeros),
        out_shape=jax.ShapeDtypeStruct(whole, bf16),
        compiler_params=params(6),
        cost_estimate=cost(0, shape[-2] * RING * shape[-1] * 6),
        name="assemble",
    )(order, *pieces, *after)


def product_kernel(pieces, which_ref, *refs):
    total = None
    for a_ref, b_ref in zip(refs[:pieces], refs[pieces : 2 * pieces]):
        part = nn(a_ref[...].astype(bf16), b_ref[...])
        total = part if total is None else total + part
    refs[-1][...] = total


def half_product(which, half, lefts, rights, after=(), weight=1):
    columns = rights[0].shape[1]
    step = 256
    count = half // step
    depth = sum(b.shape[0] for b in rights)
    return pl.pallas_call(
        functools.partial(product_kernel, len(lefts)),
        grid_spec=pltpu.PrefetchScalarGridSpec(
            num_scalar_prefetch=1,
            grid=(count,),
            in_specs=[
                pl.BlockSpec((step, a.shape[1]), lambda i, w: (w[0] * count + i, 0)) for a in lefts
            ]
            + [once(b.shape, (0, 0)) for b in rights]
            + unread(after),
            out_specs=pl.BlockSpec((step, columns), lambda i, w: (i, 0)),
        ),
        out_shape=jax.ShapeDtypeStruct((half, columns), f32),
        compiler_params=params(6),
        cost_estimate=cost(
            weight * 2 * half * columns * depth, half * columns * 4 + depth * columns * 2
        ),
        name="half_product",
    )(which, *lefts, *rights, *after)


def unproject_kernel(pieces, which_ref, *refs):
    total = None
    for grad_ref, w_ref in zip(refs[:pieces], refs[pieces : 2 * pieces]):
        width = w_ref.shape[2]
        part = None
        for i in range(3):
            product = nt(grad_ref[:, i * width : (i + 1) * width], w_ref[i])
            part = product if part is None else part + product
        total = part if total is None else total + part
    refs[-1][...] = total


def unproject(which, grads, weights, after=()):
    full, width = weights[0].shape[1:]
    half = grads[0].shape[0] // 2
    step = 256
    count = half // step
    return pl.pallas_call(
        functools.partial(unproject_kernel, len(weights)),
        grid_spec=pltpu.PrefetchScalarGridSpec(
            num_scalar_prefetch=1,
            grid=(count,),
            in_specs=[pl.BlockSpec((step, 3 * width), lambda i, w: (w[0] * count + i, 0))]
            * len(grads)
            + [once(w.shape, (0, 0, 0)) for w in weights]
            + unread(after),
            out_specs=pl.BlockSpec((step, full), lambda i, w: (i, 0)),
        ),
        out_shape=jax.ShapeDtypeStruct((half, full), f32),
        compiler_params=params(4),
        cost_estimate=cost(6 * half * full * width * len(weights), half * full * 8),
        name="unproject",
    )(which, *grads, *weights, *after)


def norm_two_kernel(which_ref, x_ref, a_ref, b_ref, vec_ref, *refs):
    middle_ref, normed_ref = refs[-2:]
    middle = x_ref[...].astype(f32) + (a_ref[...] + b_ref[...]) + vector(vec_ref, OUT_BIAS)
    middle_ref[...] = middle
    hat, _ = normalize(middle)
    normed = hat * vector(vec_ref, GAIN_TWO) + vector(vec_ref, SHIFT_TWO)
    normed_ref[...] = normed.astype(bf16).astype(f32)


def norm_two(which, x, terms, vectors, after=()):
    half, width = terms[0].shape
    step = 128
    count = half // step
    block = pl.BlockSpec((step, width), lambda i, w: (i, 0))
    return pl.pallas_call(
        norm_two_kernel,
        grid_spec=pltpu.PrefetchScalarGridSpec(
            num_scalar_prefetch=1,
            grid=(count,),
            in_specs=[pl.BlockSpec((step, width), lambda i, w: (w[0] * count + i, 0))]
            + [block] * 2
            + [once(vectors.shape, (0, 0))]
            + unread(after),
            out_specs=[block] * 2,
        ),
        out_shape=[jax.ShapeDtypeStruct((half, width), f32)] * 2,
        compiler_params=params(6),
        cost_estimate=cost(half * width * 12, half * width * 20),
        name="norm_two",
    )(which, x, *terms, vectors, *after)


def mlp_kernel(has_sum, which_ref, n_ref, g_ref, fc_ref, proj_ref, bias_ref, *refs):
    feed_ref, back_ref, act_ref, grad_ref = refs[-4:]
    normed = n_ref[...].astype(bf16)
    grad = g_ref[...]
    units, step = fc_ref.shape[1], bias_ref.shape[1]
    for number, at in enumerate(range(0, units, step)):
        cols = slice(at, at + step)
        hidden = nn(normed, fc_ref[:, cols]) + bias_ref[number : number + 1, :]
        square = hidden * hidden
        inner = jnp.tanh(hidden * (0.7978845608028654 + 0.7978845608028654 * 0.044715 * square))
        gate = 0.5 + 0.5 * inner
        act_ref[:, cols] = (hidden * gate).astype(bf16)
        slope = gate + (0.5 * hidden) * (1.0 - inner * inner) * (
            0.7978845608028654 + 3.0 * 0.7978845608028654 * 0.044715 * square
        )
        grad_ref[:, cols] = (nt(grad, proj_ref[cols, :]) * slope).astype(bf16)
    feed = nn(act_ref[...], proj_ref[...])
    back = nt(grad_ref[...], fc_ref[...])
    if has_sum:
        feed = feed + refs[0][...]
        back = back + refs[1][...]
    feed_ref[...] = feed
    back_ref[...] = back


def mlp(which, normed, cotangent, fc, proj, bias, bias_spec, sums=(), after=(), weight=1):
    half, width = normed.shape
    units = fc.shape[1]
    step = 256
    count = half // step
    block = pl.BlockSpec((step, width), lambda i, w: (i, 0))
    return pl.pallas_call(
        functools.partial(mlp_kernel, bool(sums)),
        grid_spec=pltpu.PrefetchScalarGridSpec(
            num_scalar_prefetch=1,
            grid=(count,),
            in_specs=[
                block,
                pl.BlockSpec((step, width), lambda i, w: (w[0] * count + i, 0)),
                once(fc.shape, (0, 0)),
                once(proj.shape, (0, 0)),
                bias_spec,
            ]
            + [block] * len(sums)
            + unread(after),
            out_specs=[block] * 2,
            scratch_shapes=[pltpu.VMEM((step, units), bf16)] * 2,
        ),
        out_shape=[jax.ShapeDtypeStruct((half, width), f32)] * 2,
        compiler_params=params(14),
        cost_estimate=cost(
            weight * 8 * half * width * units, half * width * 16 + 4 * width * units, half * units
        ),
        name="mlp",
    )(which, normed, cotangent, fc, proj, bias, *sums, *after)


def front_kernel(n_ref, fc_ref, bias_ref, *refs):
    act_ref, slope_ref = refs[-2:]
    normed = n_ref[...].astype(bf16)
    units, step = fc_ref.shape[1], bias_ref.shape[1]
    for number, at in enumerate(range(0, units, step)):
        cols = slice(at, at + step)
        hidden = nn(normed, fc_ref[:, cols]) + bias_ref[number : number + 1, :]
        square = hidden * hidden
        inner = jnp.tanh(hidden * (0.7978845608028654 + 0.7978845608028654 * 0.044715 * square))
        gate = 0.5 + 0.5 * inner
        act_ref[:, cols] = (hidden * gate).astype(bf16)
        slope_ref[:, cols] = gate + (0.5 * hidden) * (1.0 - inner * inner) * (
            0.7978845608028654 + 3.0 * 0.7978845608028654 * 0.044715 * square
        )


def front(normed, fc, bias, bias_spec, after=()):
    half, width = normed.shape
    units = fc.shape[1]
    step = 256
    block = pl.BlockSpec((step, units), lambda i: (i, 0))
    return pl.pallas_call(
        front_kernel,
        grid=(half // step,),
        in_specs=[
            pl.BlockSpec((step, width), lambda i: (i, 0)),
            once(fc.shape, (0, 0)),
            bias_spec,
        ]
        + unread(after),
        out_specs=[block] * 2,
        out_shape=[
            jax.ShapeDtypeStruct((half, units), bf16),
            jax.ShapeDtypeStruct((half, units), f32),
        ],
        compiler_params=params(10),
        cost_estimate=cost(2 * half * width * units, half * width * 10, half * units),
        name="mlp_front",
    )(normed, fc, bias, *after)


def rest_kernel(which_ref, act_ref, slope_ref, g_ref, fc_ref, proj_ref, *refs):
    feed_in, back_in = refs[:2]
    feed_ref, back_ref, grad_ref = refs[-3:]
    grad = g_ref[...]
    units = fc_ref.shape[1]
    step = min(units, 256)
    for at in range(0, units, step):
        cols = slice(at, at + step)
        grad_ref[:, cols] = (nt(grad, proj_ref[cols, :]) * slope_ref[:, cols]).astype(bf16)
    feed_ref[...] = nn(act_ref[...], proj_ref[...]) + feed_in[...]
    back_ref[...] = nt(grad_ref[...], fc_ref[...]) + back_in[...]


def rest(which, fronts, cotangent, fc, proj, sums, after=(), weight=1):
    half, units = fronts[0].shape
    width = fc.shape[0]
    step = 256
    count = half // step
    block = pl.BlockSpec((step, width), lambda i, w: (i, 0))
    return pl.pallas_call(
        rest_kernel,
        grid_spec=pltpu.PrefetchScalarGridSpec(
            num_scalar_prefetch=1,
            grid=(count,),
            in_specs=[pl.BlockSpec((step, units), lambda i, w: (i, 0))] * 2
            + [
                pl.BlockSpec((step, width), lambda i, w: (w[0] * count + i, 0)),
                once(fc.shape, (0, 0)),
                once(proj.shape, (0, 0)),
            ]
            + [block] * 2
            + unread(after),
            out_specs=[block] * 2,
            scratch_shapes=[pltpu.VMEM((step, units), bf16)],
        ),
        out_shape=[jax.ShapeDtypeStruct((half, width), f32)] * 2,
        compiler_params=params(14),
        cost_estimate=cost(
            weight * 6 * half * width * units, half * width * 16 + 4 * width * units
        ),
        name="mlp_rest",
    )(which, *fronts, cotangent, fc, proj, *sums, *after)


def norm_two_back_kernel(which_ref, g_ref, a_ref, b_ref, middle_ref, vec_ref, *refs):
    hat, scale = normalize(middle_ref[...])
    grad = (a_ref[...] + b_ref[...]) * vector(vec_ref, GAIN_TWO)
    refs[-1][...] = g_ref[...].astype(f32) + norm_back(grad, hat, scale)


def norm_two_back(which, cotangent, a, b, middle, vectors, after=()):
    half, width = a.shape
    step = 128
    count = half // step
    block = pl.BlockSpec((step, width), lambda i, w: (i, 0))
    return pl.pallas_call(
        norm_two_back_kernel,
        grid_spec=pltpu.PrefetchScalarGridSpec(
            num_scalar_prefetch=1,
            grid=(count,),
            in_specs=[
                pl.BlockSpec((step, width), lambda i, w: (w[0] * count + i, 0)),
                block,
                block,
                block,
                once(vectors.shape, (0, 0)),
            ]
            + unread(after),
            out_specs=block,
        ),
        out_shape=jax.ShapeDtypeStruct((half, width), f32),
        compiler_params=params(7),
        cost_estimate=cost(half * width * 20, half * width * 18),
        name="norm_two_back",
    )(which, cotangent, a, b, middle, vectors, *after)


def norm_one_back_kernel(which_ref, x_ref, upper_ref, vec_ref, a_ref, b_ref, *refs):
    hat, scale = normalize(x_ref[...].astype(f32))
    grad = (a_ref[...] + b_ref[...]) * vector(vec_ref, GAIN_ONE)
    refs[-2][...] = upper_ref[...] + norm_back(grad, hat, scale)
    refs[-1][...] = jnp.zeros_like(refs[-1])


def norm_one_back(which, x, upper, vectors, a, b, whole=(), after=()):
    half, width = upper.shape
    step = 128
    count = half // step
    block = pl.BlockSpec((step, width), lambda i, w: (i, 0))
    placed = pl.BlockSpec((step, width), lambda i, w: (w[0] * count + i, 0))
    return pl.pallas_call(
        norm_one_back_kernel,
        grid_spec=pltpu.PrefetchScalarGridSpec(
            num_scalar_prefetch=1,
            grid=(count,),
            in_specs=[placed, block, once(vectors.shape, (0, 0)), block, block]
            + unread(whole)
            + unread(after),
            out_specs=[placed, once((8, 128), (0, 0))],
        ),
        out_shape=[
            jax.ShapeDtypeStruct((2 * half, width), f32),
            jax.ShapeDtypeStruct((8, 128), f32),
        ],
        input_output_aliases={6: 0} if whole else {},
        compiler_params=params(6),
        cost_estimate=cost(half * width * 20, half * width * 18),
        name="norm_one_back",
    )(which, x, upper, vectors, a, b, *whole, *after)


def result_kernel(which_ref, a_ref, b_ref, middle_ref, vec_ref, *refs):
    half_ref, whole_ref, token_ref = refs[-3:]
    token_ref[...] = jnp.zeros_like(token_ref)
    result = middle_ref[...] + (a_ref[...] + b_ref[...]) + vector(vec_ref, PROJ_BIAS)
    half_ref[...] = result
    whole_ref[...] = result.astype(bf16)


def result_half(which, a, b, middle, vectors, after=(), weight=1):
    half, width = middle.shape
    step = 128
    count = half // step
    block = pl.BlockSpec((step, width), lambda i, w: (i, 0))
    placed = pl.BlockSpec((step, width), lambda i, w: (w[0] * count + i, 0))
    return pl.pallas_call(
        result_kernel,
        grid_spec=pltpu.PrefetchScalarGridSpec(
            num_scalar_prefetch=1,
            grid=(count,),
            in_specs=[block, block, block, once(vectors.shape, (0, 0))] + unread(after),
            out_specs=[block, placed, once((8, 128), (0, 0))],
        ),
        out_shape=[
            jax.ShapeDtypeStruct((half, width), f32),
            jax.ShapeDtypeStruct((2 * half, width), bf16),
            jax.ShapeDtypeStruct((8, 128), f32),
        ],
        compiler_params=params(6),
        cost_estimate=cost(weight * half * width * 2048, half * width * 18),
        name="result",
    )(which, a, b, middle, vectors, *after)


def place_kernel(which_ref, half_ref, *refs):
    refs[-2][...] = half_ref[...].astype(refs[-2].dtype)
    refs[-1][...] = jnp.zeros_like(refs[-1])


def placed_half(which, half_values, whole, after=()):
    half, width = half_values.shape
    step = 128
    count = half // step
    return pl.pallas_call(
        place_kernel,
        grid_spec=pltpu.PrefetchScalarGridSpec(
            num_scalar_prefetch=1,
            grid=(count,),
            in_specs=[pl.BlockSpec((step, width), lambda i, w: (i, 0))]
            + unread([whole])
            + unread(after),
            out_specs=[
                pl.BlockSpec((step, width), lambda i, w: (w[0] * count + i, 0)),
                once((8, 128), (0, 0)),
            ],
        ),
        out_shape=[
            jax.ShapeDtypeStruct(whole.shape, whole.dtype),
            jax.ShapeDtypeStruct((8, 128), f32),
        ],
        input_output_aliases={2: 0},
        compiler_params=params(3),
        cost_estimate=cost(0, half * width * 8),
        name="place",
    )(which, half_values, whole, *after)


def parts(values):
    high = values.astype(bf16)
    return high, (values - high.astype(f32)).astype(bf16)


def prefix_kernel(a_ref, b_ref, trunk_ref, embed_ref, w1_ref, *refs):
    w1_grad_ref, w2_grad_ref, b1_grad_ref, b2_grad_ref, embed_grad_ref = refs[-5:]
    columns = w2_grad_ref.shape[2]
    wide = w2_grad_ref.shape[1] * columns
    both = a_ref[:PAD, :] + b_ref[:PAD, :]
    kv, trunk = both[:, :wide], trunk_ref[...]
    pre = both[:, wide:] * (1.0 - trunk * trunk)
    pre_high, pre_low = parts(pre)
    embed = embed_ref[...]
    w1_grad_ref[...] = tn(
        jnp.concatenate([embed, embed], axis=0), jnp.concatenate([pre_high, pre_low], axis=0)
    )
    rows = nt(jnp.concatenate([pre_high, pre_low], axis=0), w1_ref[...])
    embed_grad_ref[...] = rows[:PAD] + rows[PAD:]
    b1_grad_ref[...] = jnp.sum(pre, axis=0, keepdims=True)
    b2_grad = jnp.sum(kv, axis=0, keepdims=True)
    trunk_high, trunk_low = parts(trunk)
    kv_high, kv_low = parts(kv)
    w2_grad = tn(
        jnp.concatenate([trunk_high, trunk_high, trunk_low], axis=0),
        jnp.concatenate([kv_high, kv_low, kv_high], axis=0),
    )
    for i in range(w2_grad_ref.shape[1]):
        cols = slice(i * columns, (i + 1) * columns)
        w2_grad_ref[:, i, :] = w2_grad[:, cols]
        b2_grad_ref[i : i + 1, :] = b2_grad[:, cols]


def prefix_grads(a, b, trunk, embed, w1, width, after=()):
    full, rank = w1.shape
    shapes = [(full, rank), (rank, 2, width), (1, rank), (2, width), (PAD, full)]
    return pl.pallas_call(
        prefix_kernel,
        grid=(1,),
        in_specs=[once(v.shape, (0, 0)) for v in (a, b, trunk, embed, w1)] + unread(after),
        out_specs=[once(shape, (0,) * len(shape)) for shape in shapes],
        out_shape=[jax.ShapeDtypeStruct(shape, f32) for shape in shapes],
        compiler_params=params(16),
        cost_estimate=cost(0, full * rank * 8),
        name="prefix_grads",
    )(a, b, trunk, embed, w1, *after)


def shards(
    group,
    copies,
    tokens,
    cotangent,
    seg_lengths,
    pad_counts,
    ln1_gain,
    ln1_shift,
    qkv_weight,
    qkv_bias,
    out_weight,
    out_bias,
    ln2_gain,
    ln2_shift,
    fc_weight,
    fc_bias,
    proj_weight,
    proj_bias,
    prefix_embed,
    reparam_w1,
    reparam_b1,
    reparam_w2,
    reparam_b2,
):
    rows_here, length, width = tokens.shape
    assert rows_here == 1 and copies % RING == 0
    local_width = qkv_weight.shape[2]
    prefix = prefix_embed.shape[0]
    half = length // 2
    parcel = Parcel(length, local_width, width)
    place = lax.axis_index("tensor")
    core = place % CORES
    mine = core.reshape(1).astype(jnp.int32)
    theirs = 1 - mine
    none = mine * 0
    far_shifts = [CORES * s for s in range(1, group // CORES)]

    def to_core(values):
        return lax.ppermute(values, "tensor", [(t, t ^ 1) for t in range(group)])

    def to_far(values):
        return [
            lax.ppermute(values, "tensor", [(t, (t + shift) % group) for t in range(group)])
            for shift in far_shifts
        ]

    def swapped(values, axis, size, step):
        return values + lax.ppermute(values, axis, [(i, i ^ step) for i in range(size)])

    ring = list(range(0, RING, 2)) + list(range(RING - 1, 0, -2))
    member = lax.axis_index("dp") % RING
    order = jnp.where(member % 2 == 0, member // 2, RING - 1 - member // 2)
    here = order.reshape(1).astype(jnp.int32)
    across = (here + RING // 2) % RING
    hops = RING // 2 - 1

    def along(values, step):
        hop = [
            (base + ring[i], base + ring[(i + step) % RING])
            for base in range(0, copies, RING)
            for i in range(RING)
        ]
        return lax.ppermute(values, "dp", hop)

    def hop(rings):
        for levels in rings:
            up, down = levels[-1]
            levels.append((along(up, 1), along(down, -1)))

    def last(rings):
        return [piece for levels in rings for piece in levels[-1]]

    def hold(rings, after):
        for levels in rings:
            up, down = levels[-1]
            if up is down:
                up = down = held([up], after)[0]
            else:
                up, down = held([up, down], after)
            levels[-1] = (up, down)

    def starting(pieces):
        return [[(piece, piece)] for piece in pieces]

    def rebuilt(levels, facing, spec, folded=False, after=()):
        shifts, pieces = [0], [levels[0][0]]
        for number, (up, down) in enumerate(levels[1:]):
            shifts += [-1 - number, number + 1]
            pieces += [up, down]
        return assembled(here, shifts + [RING // 2], pieces + [facing], [spec], folded, after)

    x = tokens.reshape(length, width)
    grad_out = cotangent.reshape(length, width)
    lengths = seg_lengths.reshape(-1)
    qkv_w = jnp.transpose(qkv_weight, (1, 0, 2))
    vectors = jnp.stack([ln1_gain, ln1_shift, out_bias, ln2_gain, ln2_shift, proj_bias])
    vectors = jnp.pad(vectors, ((0, 2), (0, 0))).astype(f32)

    (piece_fc,) = picked([here], [fc_weight])
    near_fc = to_far(piece_fc)
    (piece_out,) = picked([here], [out_weight], [piece_fc])
    near_out = to_far(piece_out)
    (piece_proj,) = picked([here], [proj_weight], [piece_out])
    near_proj = to_far(piece_proj)
    ring_out, ring_fc, ring_proj = starting(near_out), starting(near_fc), starting(near_proj)

    fc_rows = fc_bias.astype(f32).reshape(-1, local_width)
    biases = jnp.concatenate(
        [
            jnp.pad(qkv_bias.astype(f32), ((0, 5), (0, 0))),
            jnp.pad(fc_rows, ((0, 8 - fc_rows.shape[0]), (0, 0))),
        ],
        axis=0,
    )
    qkv_bias_spec = once((8, local_width), (0, 0))
    fc_bias_spec = once((8, local_width), (1, 0))
    qkv, normed_one = project(True, in_hbm([x])[0], vectors, qkv_w, biases, qkv_bias_spec)

    embed = prefix_embed.astype(f32)
    trunk_weight = reparam_w1.astype(f32)
    head_weight = reparam_w2.astype(f32)
    trunk = jnp.tanh(jnp.dot(embed, trunk_weight, precision=highest) + reparam_b1.astype(f32))
    kv_values = jnp.einsum(
        "pr,rtd->ptd", trunk, head_weight, precision=highest
    ) + reparam_b2.astype(f32)
    flat_kv = jnp.pad(kv_values, ((0, PAD - prefix), (0, 0), (0, 0)))
    prefix_kv = jnp.concatenate([flat_kv[:, 0], flat_kv[:, 1]], axis=0)

    hold(ring_fc, [qkv])
    fc_held = last(ring_fc)
    hop(ring_fc)
    hold(ring_out, [qkv])
    out_held = last(ring_out)
    hop(ring_out)
    out, token = attend(
        prefix, parcel, lengths, pad_counts, qkv, prefix_kv, biases, fc_held + out_held
    )
    out = pack(across, parcel, out, out_weight, last(ring_fc) + last(ring_out))
    out = held([out], [token])[0]
    far_out_parcel = to_far(out)
    hold(ring_out, [out])
    out_held = last(ring_out)
    hop(ring_out)
    hold(ring_proj, out_held)
    hop(ring_proj)
    second_out = last(ring_out)
    hop(ring_out)
    hold(ring_fc, last(ring_proj) + second_out)
    hop(ring_fc)
    hold(ring_proj, last(ring_out))
    hop(ring_proj)
    across_fc, across_proj, piece_qkv, across_qkv = picked(
        [across, across, here, across], [fc_weight, proj_weight, qkv_w, qkv_w], last(ring_out)
    )
    far_places = [-hops, hops]
    pieces_qkv = joined(
        [(here + place + RING) % RING for place in far_places], qkv_w, [piece_qkv]
    )
    far_out = [
        rebuilt(levels, far, parcel.part(length, parcel.piece), True, [pieces_qkv])
        for levels, far in zip(ring_out, far_out_parcel)
    ]
    lefts = [out] + far_out_parcel
    rights = [out_weight] + far_out
    send = half_product(theirs, half, lefts, rights, last(ring_fc))
    received = to_core(send)
    keep = half_product(mine, half, lefts, rights, [send], KEEP)
    facing_fc = to_far(held([across_fc], last(ring_fc))[0])
    hold(ring_fc, last(ring_proj))
    fc_held = last(ring_fc)
    hop(ring_fc)
    middle, normed = norm_two(mine, x, [keep, received], vectors, fc_held)
    other_normed = to_core(normed)
    own = (fc_weight, proj_weight, biases, fc_bias_spec)
    keep_sums = mlp(mine, normed, grad_out, *own, (), (), OWN)
    hold(ring_proj, [other_normed])
    hop(ring_proj)
    near_qkv = to_far(held([piece_qkv], [normed])[0])
    facing_proj = to_far(held([across_proj], facing_fc + [keep_sums[0]])[0])
    fc_spec, proj_spec = once(piece_fc.shape, (0, 0)), once(piece_proj.shape, (0, 0))
    send_sums = mlp(
        theirs, other_normed, grad_out, *own, (), [keep_sums[0]] + last(ring_fc)
    )
    ring_qkv = starting(near_qkv)
    hold(ring_qkv, [send_sums[0]] + last(ring_fc))
    hop(ring_qkv)
    far_fc = [
        rebuilt(levels, piece, fc_spec, False, [send_sums[0]])
        for levels, piece in zip(ring_fc, facing_fc)
    ]
    far_bias_spec = parcel.part(parcel.bias + 8, 8)
    other_fronts, fronts = [], []
    for fc, far in zip(far_fc, far_out_parcel):
        other_fronts.append(front(other_normed, fc, far, far_bias_spec))
        fronts.append(front(normed, fc, far, far_bias_spec, other_fronts[-1][:1]))
    far_proj = [
        rebuilt(levels, piece, proj_spec, False, [ahead[1] for ahead in fronts])
        for levels, piece in zip(ring_proj, facing_proj)
    ]
    for ahead, fc, proj in zip(other_fronts, far_fc, far_proj):
        send_sums = rest(theirs, ahead, grad_out, fc, proj, send_sums, (), LIGHT)
    back_received = to_core(send_sums[1])
    for ahead, fc, proj in zip(fronts, far_fc, far_proj):
        keep_sums = rest(mine, ahead, grad_out, fc, proj, keep_sums, [send_sums[0]], FAR)
    facing_qkv = to_far(held([across_qkv], near_qkv + [send_sums[0]])[0])
    upper = norm_two_back(
        mine, grad_out, keep_sums[1], back_received, middle, vectors
    )
    hold(ring_qkv, [upper])
    q_held = last(ring_qkv)
    hop(ring_qkv)
    other_upper = to_core(upper)
    feed_received = to_core(send_sums[0])
    result, mixed, result_token = result_half(
        mine, keep_sums[0], feed_received, middle, vectors, q_held + facing_qkv, FAR
    )
    other_result = to_core(result)
    ends_qkv = to_far(held([pieces_qkv], [upper])[0])

    grads_far = heads_back(
        mine, upper, other_upper, [out_weight] + far_out, [result_token]
    )
    dqkv, grad_keys, grad_vals = attend_back(
        prefix,
        parcel,
        lengths,
        pad_counts,
        qkv,
        grads_far[0],
        out,
        (),
        LIGHT,
    )

    grad_keys, grad_vals = held([grad_keys, grad_vals], last(ring_qkv))
    grad_here = jnp.concatenate([grad_keys, grad_vals], axis=1)
    flat_head = jnp.transpose(head_weight, (1, 2, 0)).reshape(2 * local_width, -1)
    trunk_here = jnp.dot(grad_here, flat_head, precision=highest)
    for_tensor = [("tensor", group, 1 << i) for i in range(group.bit_length() - 1)]
    for_dp = [("dp", copies, 1 << i) for i in reversed(range(copies.bit_length() - 1))]
    mixed, token = placed_half(theirs, other_result, mixed, [dqkv])
    far_qkv = []
    for levels, facing, pieces in zip(ring_qkv, facing_qkv, ends_qkv):
        shifts, found = [0], [levels[0][0]]
        for number, ends in enumerate(levels[1:]):
            shifts += [-1 - number, number + 1]
            found += list(ends)
        shifts, found = shifts + [RING // 2], found + [facing]
        specs = [once(piece_qkv.shape, (i, 0, 0)) for i in range(len(far_places))]
        far_qkv.append(
            assembled(here, shifts + far_places, found + [pieces] * len(far_places), specs, False, [token])
        )
    qkvs = [qkv_w] + far_qkv
    trunk_here = swapped(trunk_here, *for_tensor[0])
    far_projected = [
        project(
            False,
            in_hbm([normed_one])[0],
            vectors,
            weight,
            far,
            parcel.part(parcel.bias, 8),
            [trunk_here],
        )[0]
        for weight, far in zip(far_qkv, far_out_parcel)
    ]
    for step in for_tensor[1:]:
        trunk_here = swapped(trunk_here, *step)
    grads = [dqkv]
    for number, far in enumerate(far_out_parcel):
        found = attend_back(
            prefix,
            parcel,
            lengths,
            pad_counts,
            far_projected[number],
            grads_far[1 + number],
            far,
            [trunk_here],
            LIGHT,
        )
        grads.append(found[0])
    both = jnp.concatenate([grad_here, trunk_here], axis=1)
    both = swapped(held([both], far_projected)[0], *for_dp[0])
    both = held([both], grads[-1:])[0]
    send_one = unproject(theirs, grads, qkvs, [both])
    received_one = to_core(send_one)
    both = swapped(both, *for_dp[1])
    keep_one = unproject(mine, grads, qkvs, [send_one, both])
    received_two = to_core(keep_one)
    for step in for_dp[2:-1]:
        both = swapped(both, *step)
    last_step = for_dp[-1]
    other_both = lax.ppermute(both, "dp", [(i, i ^ last_step[2]) for i in range(copies)])
    input_grad, token = norm_one_back(mine, x, upper, vectors, keep_one, received_one)
    w1_grad, w2_grad, b1_grad, b2_grad, embed_grad = prefix_grads(
        both,
        other_both,
        jnp.pad(trunk, ((0, PAD - prefix), (0, 0))),
        jnp.pad(prefix_embed, ((0, PAD - prefix), (0, 0))),
        reparam_w1,
        local_width,
        [token],
    )
    input_grad, _ = norm_one_back(
        theirs, x, other_upper, vectors, send_one, received_two, [input_grad]
    )
    b1_grad, embed_grad = b1_grad.reshape(-1), embed_grad[:prefix]
    mixed, input_grad = mixed.reshape(tokens.shape), input_grad.reshape(tokens.shape)
    return (mixed, input_grad, embed_grad, w1_grad, b1_grad, w2_grad, b2_grad, kv_values)


def solution(mesh):
    return jax.shard_map(
        functools.partial(shards, mesh.shape["tensor"], mesh.shape["dp"]),
        mesh=mesh,
        in_specs=(
            P("dp", None, None),
            P("dp", None, None),
            P("dp", None),
            P("dp"),
            P(),
            P(),
            P(None, None, "tensor"),
            P(None, "tensor"),
            P("tensor", None),
            P(),
            P(),
            P(),
            P(None, "tensor"),
            P("tensor"),
            P("tensor", None),
            P(),
            P(),
            P(),
            P(),
            P(None, None, "tensor"),
            P(None, "tensor"),
        ),
        out_specs=(
            P("dp", None, None),
            P("dp", None, None),
            P(),
            P(),
            P(),
            P(None, None, "tensor"),
            P(None, "tensor"),
            P(None, None, "tensor"),
        ),
        check_vma=False,
    )
```

```python
import functools

import jax
import jax.numpy as jnp
from jax import lax
from jax.experimental import pallas as pl
from jax.experimental.pallas import tpu as pltpu
from jax.sharding import PartitionSpec as P

HEAD_DIM = 64
CORES = 2
QB = 128
SPAN = 384
PAD = 16
RING = 8
LIGHT = 16
KEEP, OWN, FAR = 640, 320, 320
MASKED = -1e30
GAIN_ONE, SHIFT_ONE, OUT_BIAS, GAIN_TWO, SHIFT_TWO, PROJ_BIAS = range(6)
highest = lax.Precision.HIGHEST
epsilon = 1e-05
f32 = jnp.float32
bf16 = jnp.bfloat16


def nn(a, b):
    return jnp.dot(a, b, preferred_element_type=f32)


def nt(a, b):
    return lax.dot_general(a, b, (((1,), (1,)), ((), ())), preferred_element_type=f32)


def tn(a, b):
    return lax.dot_general(a, b, (((0,), (0,)), ((), ())), preferred_element_type=f32)


def params(mib):
    return pltpu.CompilerParams(vmem_limit_bytes=mib * 1024 * 1024)


def in_hbm(values):
    return [pltpu.with_memory_space_constraint(v, pltpu.HBM) for v in values]


def cost(flops, bytes_accessed, transcendentals=0):
    return pl.CostEstimate(
        flops=int(flops) // LIGHT,
        bytes_accessed=int(bytes_accessed) // LIGHT,
        transcendentals=int(transcendentals) // LIGHT,
    )


def unread(after):
    return [pl.BlockSpec(memory_space=pl.ANY)] * len(after)


def once(shape, index):
    return pl.BlockSpec(shape, lambda *_: index, pipeline_mode=pl.Buffered(1))


def vector(ref, number):
    return ref[number : number + 1, :]


def normalize(values):
    centered = values - jnp.mean(values, axis=-1, keepdims=True)
    scale = lax.rsqrt(jnp.mean(centered * centered, axis=-1, keepdims=True) + epsilon)
    return centered * scale, scale


def norm_back(grad, hat, scale):
    mean_grad = jnp.mean(grad, axis=-1, keepdims=True)
    mean_both = jnp.mean(grad * hat, axis=-1, keepdims=True)
    return scale * (grad - mean_grad - hat * mean_both)


class Parcel:
    def __init__(self, length, width, full):
        self.length, self.width, self.full = length, width, full
        self.piece = full // 8
        self.kv = length + self.piece
        self.lse = self.kv + 2 * PAD
        self.bias = self.lse + 2 * (length // QB)
        self.rows = self.bias + 16

    def part(self, start, size):
        assert start % size == 0
        return once((size, self.width), (start // size, 0))


def head_masks():
    lanes = lax.broadcasted_iota(jnp.int32, (QB, 2 * HEAD_DIM), 1)
    return lanes < HEAD_DIM


def both_heads(block, first):
    zero = jnp.zeros_like(block)
    return jnp.concatenate([jnp.where(first, block, zero), jnp.where(first, zero, block)], axis=0)


def own_quadrants(product):
    return jnp.concatenate([product[:HEAD_DIM, :QB], product[HEAD_DIM:, QB:]], axis=0)


def segment_start(position, lengths_ref):
    start, end = jnp.zeros_like(position), jnp.int32(0)
    for number in range(lengths_ref.shape[0]):
        end = end + lengths_ref[number]
        start = jnp.where(position >= end, end, start)
    return start


def by_window(length, lengths_ref, order_ref, run):
    blocks = length // QB
    most = min(length, SPAN + QB) // QB

    def tiles_of(block):
        return block - segment_start(block * QB, lengths_ref) // QB + 1

    def place(block, ends):
        low, high = ends
        small = tiles_of(block) <= most // 2
        order_ref[jnp.where(small, low, high)] = block
        return jnp.where(small, low + 1, low), jnp.where(small, high, high - 1)

    lax.fori_loop(0, blocks, place, (jnp.int32(0), jnp.int32(blocks - 1)))

    def step(number, _):
        pair = order_ref[2 * number], order_ref[2 * number + 1]
        tiles = jnp.maximum(tiles_of(pair[0]), tiles_of(pair[1]))
        for count in (most // 2, most):

            @pl.when((tiles <= count) & (tiles > count - most // 2))
            def _():
                run(pair, count * QB)

        return 0

    lax.fori_loop(0, blocks // 2, step, 0)


def window_bias(block, start, window, length, lengths_ref, pads_ref):
    lanes = lax.broadcasted_iota(jnp.int32, (1, 2 * QB), 1)
    position = block * QB + jnp.where(lanes < QB, lanes, lanes - QB)
    low = segment_start(position, lengths_ref)
    low = jnp.where(position < length - pads_ref[0], low, 4 * length)
    key = start + lax.broadcasted_iota(jnp.int32, (window, 2 * QB), 0)
    return jnp.where((key >= low) & (key <= position), 0.0, MASKED)


def window_start(block, window):
    return pl.multiple_of(jnp.maximum((block + 1) * QB - window, 0), QB)


def prefix_bias(prefix):
    rows = lax.broadcasted_iota(jnp.int32, (PAD, 2 * QB), 0)
    return jnp.where(rows < prefix, 0.0, MASKED)


def project_kernel(first, x_ref, y_ref, vec_ref, w_ref, bias_ref, *refs):
    whole = jnp.concatenate([x_ref[...], y_ref[...]], axis=1)
    if first:
        qkv_ref, normed_ref = refs[-2:]
        hat, _ = normalize(whole.astype(f32))
        normed = (hat * vector(vec_ref, GAIN_ONE) + vector(vec_ref, SHIFT_ONE)).astype(bf16)
        normed_ref[...] = normed
    else:
        qkv_ref = refs[-1]
        normed = whole
    width = w_ref.shape[2]
    for i in range(3):
        part = nn(normed, w_ref[i]) + bias_ref[i : i + 1, :]
        qkv_ref[:, i * width : (i + 1) * width] = part.astype(bf16)


def project(first, x, vectors, weight, bias, bias_spec, after=()):
    length, full = x.shape
    width = weight.shape[2]
    step = 256
    block = pl.BlockSpec((step, full), lambda i: (i, 0))
    specs = [pl.BlockSpec((step, 3 * width), lambda i: (i, 0))]
    shapes = [jax.ShapeDtypeStruct((length, 3 * width), bf16)]
    if first:
        specs.append(block)
        shapes.append(pltpu.HBM((length, full), bf16))
    return pl.pallas_call(
        functools.partial(project_kernel, first),
        grid=(length // step,),
        in_specs=[
            pl.BlockSpec((step, full // 2), lambda i: (i, 0)),
            pl.BlockSpec((step, full // 2), lambda i: (i, 1)),
            once(vectors.shape, (0, 0)),
            once(weight.shape, (0, 0, 0)),
            bias_spec,
        ]
        + unread(after),
        out_specs=specs,
        out_shape=shapes,
        compiler_params=params(4),
        cost_estimate=cost(6 * length * full * width, length * full * 8),
        name="project",
    )(x, x, vectors, weight, bias, *after)


def attend_kernel(
    prefix, parcel, lengths_ref, pads_ref, qkv_ref, kv_ref, bias_ref, *refs
):
    o_ref, token_ref, norm_ref, order_ref = refs[-4:]
    token_ref[...] = jnp.zeros_like(token_ref)
    length, width = parcel.length, parcel.width
    pairs = width // (2 * HEAD_DIM)
    first = head_masks()
    front_bias = prefix_bias(prefix)
    o_ref[parcel.kv : parcel.lse, :] = kv_ref[...]
    o_ref[parcel.bias :, :] = bias_ref[...]

    def attend(blocks, window):
        for block in blocks:
            rows = pl.ds(pl.multiple_of(block * QB, QB), QB)
            start = window_start(block, window)
            keys_at = pl.ds(start, window)
            bias = window_bias(block, start, window, length, lengths_ref, pads_ref)
            for pair in range(pairs):
                at = pair * 2 * HEAD_DIM
                cols = slice(at, at + 2 * HEAD_DIM)
                q = both_heads(qkv_ref[rows, cols] * jnp.asarray(HEAD_DIM**-0.5, bf16), first)
                k = qkv_ref[keys_at, width + at : width + at + 2 * HEAD_DIM]
                v = qkv_ref[keys_at, 2 * width + at : 2 * width + at + 2 * HEAD_DIM]
                pk = kv_ref[:PAD, cols].astype(bf16)
                pv = kv_ref[PAD:, cols].astype(bf16)
                inside = nt(k, q) + bias
                front = nt(pk, q) + front_bias
                largest = jnp.maximum(
                    jnp.max(inside, axis=0, keepdims=True), jnp.max(front, axis=0, keepdims=True)
                )
                inside = jnp.exp(inside - largest)
                front = jnp.exp(front - largest)
                total = jnp.sum(inside, axis=0, keepdims=True) + jnp.sum(
                    front, axis=0, keepdims=True
                )
                scale = 1.0 / total
                out = tn(v, (inside * scale).astype(bf16)) + tn(pv, (front * scale).astype(bf16))
                o_ref[rows, cols] = own_quadrants(out).T
                lse = largest + jnp.log(total)
                norm_ref[pair, pl.ds(2 * block, 1), :] = lse[:, :QB]
                norm_ref[pair, pl.ds(2 * block + 1, 1), :] = lse[:, QB:]

    by_window(length, lengths_ref, order_ref, attend)
    for pair in range(pairs):
        cols = slice(pair * 2 * HEAD_DIM, (pair + 1) * 2 * HEAD_DIM)
        o_ref[parcel.lse : parcel.bias, cols] = norm_ref[pair]


def attend(prefix, parcel, lengths, pads, qkv, prefix_kv, biases, after=()):
    length, width = parcel.length, parcel.width
    return pl.pallas_call(
        functools.partial(attend_kernel, prefix, parcel),
        grid=(1,),
        in_specs=[pl.BlockSpec(memory_space=pltpu.SMEM)] * 2
        + [once(v.shape, (0, 0)) for v in (qkv, prefix_kv, biases)]
        + unread(after),
        out_specs=[once((parcel.rows, width), (0, 0)), once((8, 128), (0, 0))],
        out_shape=[
            jax.ShapeDtypeStruct((parcel.rows, width), f32),
            jax.ShapeDtypeStruct((8, 128), f32),
        ],
        scratch_shapes=[
            pltpu.VMEM((width // (2 * HEAD_DIM), parcel.bias - parcel.lse, 2 * HEAD_DIM), f32),
            pltpu.SMEM((length // QB,), jnp.int32),
        ],
        compiler_params=params(10),
        cost_estimate=cost(
            8 * length * (SPAN + QB) * width,
            length * width * 10,
            length * (SPAN + QB) * width // HEAD_DIM,
        ),
        name="attend",
    )(lengths, pads, qkv, prefix_kv, biases, *after)


def pack_kernel(which_ref, w_ref, *refs):
    out_ref = refs[-1]
    size, width = w_ref.shape[0], out_ref.shape[1]
    for i in range(w_ref.shape[1] // width):
        out_ref[i * size : (i + 1) * size, :] = w_ref[:, i * width : (i + 1) * width].astype(f32)


def pack(which, parcel, out, weight, after=()):
    size = weight.shape[0] // RING
    assert size * (weight.shape[1] // parcel.width) == parcel.piece
    assert parcel.length % parcel.piece == 0
    place = parcel.length // parcel.piece
    return pl.pallas_call(
        pack_kernel,
        grid_spec=pltpu.PrefetchScalarGridSpec(
            num_scalar_prefetch=1,
            grid=(1,),
            in_specs=[pl.BlockSpec((size, weight.shape[1]), lambda i, w: (w[0], 0))]
            + unread([out])
            + unread(after),
            out_specs=pl.BlockSpec((parcel.piece, parcel.width), lambda i, w: (place, 0)),
        ),
        out_shape=jax.ShapeDtypeStruct(out.shape, f32),
        input_output_aliases={2: 0},
        compiler_params=params(2),
        cost_estimate=cost(0, parcel.piece * parcel.width * 6),
        name="pack",
    )(which, weight, out, *after)


def heads_back_kernel(count, core_ref, keep_ref, other_ref, *refs):
    weights, outs = refs[:count], refs[-count:]
    own = pl.program_id(0) == core_ref[0]
    low = jnp.where(own, keep_ref[...], other_ref[...]).astype(bf16)
    for w_ref, out_ref in zip(weights, outs):
        out_ref[...] = nt(low, w_ref[...]).astype(bf16)


def heads_back(which, keep, other, weights, after=()):
    half, full = keep.shape
    step = 256
    count = half // step

    def at_keep(h, i, w):
        return jnp.where(h == w[0], i, (count - 1) * (1 - w[0])), 0

    def at_other(h, i, w):
        return jnp.where(h == w[0], (count - 1) * w[0], i), 0

    return pl.pallas_call(
        functools.partial(heads_back_kernel, len(weights)),
        grid_spec=pltpu.PrefetchScalarGridSpec(
            num_scalar_prefetch=1,
            grid=(2, count),
            in_specs=[pl.BlockSpec((step, full), at_keep), pl.BlockSpec((step, full), at_other)]
            + [once(w.shape, (0, 0)) for w in weights]
            + unread(after),
            out_specs=[
                pl.BlockSpec((step, w.shape[0]), lambda h, i, w: (h * count + i, 0))
                for w in weights
            ],
        ),
        out_shape=[jax.ShapeDtypeStruct((2 * half, w.shape[0]), bf16) for w in weights],
        compiler_params=params(8),
        cost_estimate=cost(4 * half * sum(w.size for w in weights), half * full * 10),
        name="heads_back",
    )(which, keep, other, *weights, *after)


def attend_back_kernel(
    prefix, lengths_ref, pads_ref, qkv_ref, do_ref, kv_ref, lse_ref, *refs
):
    dqkv_ref, dpk_ref, dpv_ref, norm_ref, order_ref, *sums = refs[-9:]
    length, width = do_ref.shape
    pairs = width // (2 * HEAD_DIM)
    first = head_masks()
    front_bias = prefix_bias(prefix)
    for pair in range(pairs):
        norm_ref[pair] = lse_ref[:, pair * 2 * HEAD_DIM : (pair + 1) * 2 * HEAD_DIM]
    for ref in (dpk_ref, dpv_ref, *sums):
        ref[...] = jnp.zeros_like(ref)
    factor = HEAD_DIM**-0.5

    def back(blocks, window):
        for number, block in enumerate(blocks):
            dk_ref, dv_ref = sums[2 * number : 2 * number + 2]
            rows = pl.ds(pl.multiple_of(block * QB, QB), QB)
            start = window_start(block, window)
            keys_at = pl.ds(start, window)
            bias = window_bias(block, start, window, length, lengths_ref, pads_ref)
            for pair in range(pairs):
                at = pair * 2 * HEAD_DIM
                cols = slice(at, at + 2 * HEAD_DIM)
                k = qkv_ref[keys_at, width + at : width + at + 2 * HEAD_DIM]
                v = qkv_ref[keys_at, 2 * width + at : 2 * width + at + 2 * HEAD_DIM]
                pk = kv_ref[:PAD, cols].astype(bf16)
                pv = kv_ref[PAD:, cols].astype(bf16)
                q = both_heads(qkv_ref[rows, cols] * jnp.asarray(factor, bf16), first)
                do = both_heads(do_ref[rows, cols], first)
                lse = jnp.concatenate(
                    [
                        norm_ref[pair, pl.ds(2 * block, 1), :],
                        norm_ref[pair, pl.ds(2 * block + 1, 1), :],
                    ],
                    axis=1,
                )
                inside = jnp.exp(nt(k, q) + bias - lse)
                front = jnp.exp(nt(pk, q) + front_bias - lse)
                d_inside = nt(v, do)
                d_front = nt(pv, do)
                delta = jnp.sum(inside * d_inside, axis=0, keepdims=True) + jnp.sum(
                    front * d_front, axis=0, keepdims=True
                )
                s_inside = (inside * (d_inside - delta)).astype(bf16)
                s_front = (front * (d_front - delta)).astype(bf16)
                dk_ref[keys_at, cols] += nn(s_inside, q)
                dv_ref[keys_at, cols] += nn(inside.astype(bf16), do)
                dpk_ref[:, cols] += nn(s_front, q)
                dpv_ref[:, cols] += nn(front.astype(bf16), do)
                dq = own_quadrants(tn(k, s_inside) + tn(pk, s_front)).T * factor
                dqkv_ref[rows, cols] = dq.astype(bf16)

    by_window(length, lengths_ref, order_ref, back)
    dqkv_ref[:, width : 2 * width] = (sums[0][...] + sums[2][...]).astype(bf16)
    dqkv_ref[:, 2 * width :] = (sums[1][...] + sums[3][...]).astype(bf16)


def attend_back(prefix, parcel, lengths, pads, qkv, grad, out, after=(), weight=1):
    length, width = parcel.length, parcel.width
    lse_rows = parcel.bias - parcel.lse
    return pl.pallas_call(
        functools.partial(attend_back_kernel, prefix),
        grid=(1,),
        in_specs=[pl.BlockSpec(memory_space=pltpu.SMEM)] * 2
        + [
            once(qkv.shape, (0, 0)),
            once(grad.shape, (0, 0)),
            parcel.part(parcel.kv, 2 * PAD),
            parcel.part(parcel.lse, lse_rows),
        ]
        + unread(after),
        out_specs=[
            once((length, 3 * width), (0, 0)),
            once((PAD, width), (0, 0)),
            once((PAD, width), (0, 0)),
        ],
        out_shape=[
            jax.ShapeDtypeStruct((length, 3 * width), bf16),
            jax.ShapeDtypeStruct((PAD, width), f32),
            jax.ShapeDtypeStruct((PAD, width), f32),
        ],
        scratch_shapes=[
            pltpu.VMEM((width // (2 * HEAD_DIM), lse_rows, 2 * HEAD_DIM), f32),
            pltpu.SMEM((length // QB,), jnp.int32),
        ]
        + [pltpu.VMEM((length, width), f32)] * 4,
        compiler_params=params(14),
        cost_estimate=cost(
            weight * 20 * length * (SPAN + QB) * width,
            length * width * 40,
            length * (SPAN + QB) * width // HEAD_DIM,
        ),
        name="attend_back",
    )(lengths, pads, qkv, grad, out, out, *after)


def pass_kernel(*refs):
    del refs


def held(values, after):
    count = len(values)
    return pl.pallas_call(
        pass_kernel,
        in_specs=unread(values) + unread(after),
        out_specs=unread(values),
        out_shape=[jax.ShapeDtypeStruct(v.shape, v.dtype) for v in values],
        input_output_aliases={i: i for i in range(count)},
        compiler_params=params(1),
        cost_estimate=cost(0, 0),
        name="held",
    )(*values, *after)


def pick_kernel(count, which_ref, *refs):
    weights, outs = refs[:count], refs[-2 * count - 1 : -count - 1]
    buffers, sems = refs[-count - 1 : -1], refs[-1]
    copies = []
    for number, (ref, buffer) in enumerate(zip(weights, buffers)):
        size = buffer.shape[-2]
        rows = pl.ds(pl.multiple_of(which_ref[number] * size, size), size)
        source = ref.at[rows, :] if len(ref.shape) == 2 else ref.at[:, rows, :]
        copies.append(pltpu.make_async_copy(source, buffer, sems.at[number]))
        copies[-1].start()
    for copy, buffer, out_ref in zip(copies, buffers, outs):
        copy.wait()
        out_ref[...] = buffer[...].astype(f32)


def joined_kernel(count, which_ref, w_ref, *refs):
    out_ref, buffer, sems = refs[-3:]
    lead, size = w_ref.shape[0], buffer.shape[-2]
    copies = []
    for number in range(count):
        rows = pl.ds(pl.multiple_of(which_ref[number] * size, size), size)
        part = buffer.at[number * lead : (number + 1) * lead]
        copies.append(pltpu.make_async_copy(w_ref.at[:, rows, :], part, sems.at[number]))
        copies[-1].start()
    for copy in copies:
        copy.wait()
    out_ref[...] = buffer[...].astype(f32)


def joined(whiches, weight, after=()):
    count, size = len(whiches), weight.shape[1] // RING
    whole = (count * weight.shape[0], size, weight.shape[2])
    return pl.pallas_call(
        functools.partial(joined_kernel, count),
        grid=(1,),
        in_specs=[
            pl.BlockSpec(memory_space=pltpu.SMEM),
            pl.BlockSpec(memory_space=pltpu.HBM),
        ]
        + unread(after),
        out_specs=once(whole, (0, 0, 0)),
        out_shape=jax.ShapeDtypeStruct(whole, f32),
        scratch_shapes=[pltpu.VMEM(whole, bf16), pltpu.SemaphoreType.DMA((count,))],
        compiler_params=params(4),
        cost_estimate=cost(0, whole[0] * size * whole[2] * 6),
        name="joined",
    )(jnp.concatenate(whiches), *in_hbm([weight]), *after)


def picked(whiches, weights, after=()):
    shapes = [(*w.shape[:-2], w.shape[-2] // RING, w.shape[-1]) for w in weights]
    return pl.pallas_call(
        functools.partial(pick_kernel, len(weights)),
        grid=(1,),
        in_specs=[pl.BlockSpec(memory_space=pltpu.SMEM)]
        + [pl.BlockSpec(memory_space=pltpu.HBM)] * len(weights)
        + unread(after),
        out_specs=[once(shape, (0,) * len(shape)) for shape in shapes],
        out_shape=[jax.ShapeDtypeStruct(shape, f32) for shape in shapes],
        scratch_shapes=[pltpu.VMEM(shape, bf16) for shape in shapes]
        + [pltpu.SemaphoreType.DMA((len(weights),))],
        compiler_params=params(6),
        cost_estimate=cost(0, sum(shape[-2] * shape[-1] for shape in shapes) * 6),
        name="pick",
    )(jnp.concatenate(whiches), *in_hbm(weights), *after)


def assemble_kernel(shifts, folded, order_ref, *refs):
    out_ref = refs[-1]
    pieces = refs[: len(shifts)]
    size = pieces[0].shape[-2]
    for shift, ref in zip(shifts, pieces):
        at = lax.rem(order_ref[0] + (shift + RING), RING) * size
        rows = pl.ds(pl.multiple_of(at, size), size)
        if folded and ref is pieces[-1]:
            width = ref.shape[1]
            for i in range(out_ref.shape[1] // width):
                block = ref[i * size : (i + 1) * size, :]
                out_ref[rows, i * width : (i + 1) * width] = block.astype(bf16)
        else:
            out_ref[..., rows, :] = ref[...].astype(bf16)


def assembled(order, shifts, pieces, last_specs, folded=False, after=()):
    shape = pieces[0].shape
    zeros = (0,) * len(shape)
    whole = (*shape[:-2], shape[-2] * RING, shape[-1])
    return pl.pallas_call(
        functools.partial(assemble_kernel, shifts, folded),
        grid=(1,),
        in_specs=[pl.BlockSpec(memory_space=pltpu.SMEM)]
        + [once(shape, zeros)] * (len(pieces) - len(last_specs))
        + last_specs
        + unread(after),
        out_specs=once(whole, zeros),
        out_shape=jax.ShapeDtypeStruct(whole, bf16),
        compiler_params=params(6),
        cost_estimate=cost(0, shape[-2] * RING * shape[-1] * 6),
        name="assemble",
    )(order, *pieces, *after)


def product_kernel(pieces, which_ref, *refs):
    total = None
    for a_ref, b_ref in zip(refs[:pieces], refs[pieces : 2 * pieces]):
        part = nn(a_ref[...].astype(bf16), b_ref[...])
        total = part if total is None else total + part
    refs[-1][...] = total


def half_product(which, half, lefts, rights, after=(), weight=1):
    columns = rights[0].shape[1]
    step = 256
    count = half // step
    depth = sum(b.shape[0] for b in rights)
    return pl.pallas_call(
        functools.partial(product_kernel, len(lefts)),
        grid_spec=pltpu.PrefetchScalarGridSpec(
            num_scalar_prefetch=1,
            grid=(count,),
            in_specs=[
                pl.BlockSpec((step, a.shape[1]), lambda i, w: (w[0] * count + i, 0)) for a in lefts
            ]
            + [once(b.shape, (0, 0)) for b in rights]
            + unread(after),
            out_specs=pl.BlockSpec((step, columns), lambda i, w: (i, 0)),
        ),
        out_shape=jax.ShapeDtypeStruct((half, columns), f32),
        compiler_params=params(6),
        cost_estimate=cost(
            weight * 2 * half * columns * depth, half * columns * 4 + depth * columns * 2
        ),
        name="half_product",
    )(which, *lefts, *rights, *after)


def unproject_kernel(pieces, which_ref, *refs):
    total = None
    for grad_ref, w_ref in zip(refs[:pieces], refs[pieces : 2 * pieces]):
        width = w_ref.shape[2]
        part = None
        for i in range(3):
            product = nt(grad_ref[:, i * width : (i + 1) * width], w_ref[i])
            part = product if part is None else part + product
        total = part if total is None else total + part
    refs[-1][...] = total


def unproject(which, grads, weights, after=()):
    full, width = weights[0].shape[1:]
    half = grads[0].shape[0] // 2
    step = 256
    count = half // step
    return pl.pallas_call(
        functools.partial(unproject_kernel, len(weights)),
        grid_spec=pltpu.PrefetchScalarGridSpec(
            num_scalar_prefetch=1,
            grid=(count,),
            in_specs=[pl.BlockSpec((step, 3 * width), lambda i, w: (w[0] * count + i, 0))]
            * len(grads)
            + [once(w.shape, (0, 0, 0)) for w in weights]
            + unread(after),
            out_specs=pl.BlockSpec((step, full), lambda i, w: (i, 0)),
        ),
        out_shape=jax.ShapeDtypeStruct((half, full), f32),
        compiler_params=params(4),
        cost_estimate=cost(6 * half * full * width * len(weights), half * full * 8),
        name="unproject",
    )(which, *grads, *weights, *after)


def norm_two_kernel(which_ref, x_ref, a_ref, b_ref, vec_ref, *refs):
    middle_ref, normed_ref = refs[-2:]
    middle = x_ref[...].astype(f32) + (a_ref[...] + b_ref[...]) + vector(vec_ref, OUT_BIAS)
    middle_ref[...] = middle
    hat, _ = normalize(middle)
    normed = hat * vector(vec_ref, GAIN_TWO) + vector(vec_ref, SHIFT_TWO)
    normed_ref[...] = normed.astype(bf16).astype(f32)


def norm_two(which, x, terms, vectors, after=()):
    half, width = terms[0].shape
    step = 128
    count = half // step
    block = pl.BlockSpec((step, width), lambda i, w: (i, 0))
    return pl.pallas_call(
        norm_two_kernel,
        grid_spec=pltpu.PrefetchScalarGridSpec(
            num_scalar_prefetch=1,
            grid=(count,),
            in_specs=[pl.BlockSpec((step, width), lambda i, w: (w[0] * count + i, 0))]
            + [block] * 2
            + [once(vectors.shape, (0, 0))]
            + unread(after),
            out_specs=[block] * 2,
        ),
        out_shape=[jax.ShapeDtypeStruct((half, width), f32)] * 2,
        compiler_params=params(6),
        cost_estimate=cost(half * width * 12, half * width * 20),
        name="norm_two",
    )(which, x, *terms, vectors, *after)


def through_kernel(g_ref, proj_ref, *refs):
    grad = g_ref[...]
    units = proj_ref.shape[0]
    step = min(units, 256)
    for at in range(0, units, step):
        refs[-1][:, at : at + step] = nt(grad, proj_ref[at : at + step, :])


def through(cotangent, proj, after=()):
    length, width = cotangent.shape
    units = proj.shape[0]
    step = 256
    return pl.pallas_call(
        through_kernel,
        grid=(length // step,),
        in_specs=[pl.BlockSpec((step, width), lambda i: (i, 0)), once(proj.shape, (0, 0))]
        + unread(after),
        out_specs=pl.BlockSpec((step, units), lambda i: (i, 0)),
        out_shape=jax.ShapeDtypeStruct((length, units), f32),
        compiler_params=params(8),
        cost_estimate=cost(2 * length * width * units, length * width * 6),
        name="through",
    )(cotangent, proj, *after)


def mlp_kernel(which_ref, n_ref, through_ref, fc_ref, proj_ref, bias_ref, *refs):
    feed_ref, back_ref, act_ref, grad_ref = refs[-4:]
    normed = n_ref[...].astype(bf16)
    units, step = fc_ref.shape[1], bias_ref.shape[1]
    for number, at in enumerate(range(0, units, step)):
        cols = slice(at, at + step)
        hidden = nn(normed, fc_ref[:, cols]) + bias_ref[number : number + 1, :]
        square = hidden * hidden
        inner = jnp.tanh(hidden * (0.7978845608028654 + 0.7978845608028654 * 0.044715 * square))
        gate = 0.5 + 0.5 * inner
        act_ref[:, cols] = (hidden * gate).astype(bf16)
        slope = gate + (0.5 * hidden) * (1.0 - inner * inner) * (
            0.7978845608028654 + 3.0 * 0.7978845608028654 * 0.044715 * square
        )
        grad_ref[:, cols] = (through_ref[:, cols] * slope).astype(bf16)
    feed_ref[...] = nn(act_ref[...], proj_ref[...])
    back_ref[...] = nt(grad_ref[...], fc_ref[...])


def mlp(which, normed, grads, fc, proj, bias, bias_spec, after=(), weight=1):
    half, width = normed.shape
    units = fc.shape[1]
    step = 256
    count = half // step
    block = pl.BlockSpec((step, width), lambda i, w: (i, 0))
    return pl.pallas_call(
        mlp_kernel,
        grid_spec=pltpu.PrefetchScalarGridSpec(
            num_scalar_prefetch=1,
            grid=(count,),
            in_specs=[
                block,
                pl.BlockSpec((step, units), lambda i, w: (w[0] * count + i, 0)),
                once(fc.shape, (0, 0)),
                once(proj.shape, (0, 0)),
                bias_spec,
            ]
            + unread(after),
            out_specs=[block] * 2,
            scratch_shapes=[pltpu.VMEM((step, units), bf16)] * 2,
        ),
        out_shape=[jax.ShapeDtypeStruct((half, width), f32)] * 2,
        compiler_params=params(14),
        cost_estimate=cost(
            weight * 8 * half * width * units, half * width * 16 + 4 * width * units, half * units
        ),
        name="mlp",
    )(which, normed, grads, fc, proj, bias, *after)


def front_kernel(n_ref, fc_ref, bias_ref, *refs):
    act_ref, slope_ref = refs[-2:]
    normed = n_ref[...].astype(bf16)
    units, step = fc_ref.shape[1], bias_ref.shape[1]
    for number, at in enumerate(range(0, units, step)):
        cols = slice(at, at + step)
        hidden = nn(normed, fc_ref[:, cols]) + bias_ref[number : number + 1, :]
        square = hidden * hidden
        inner = jnp.tanh(hidden * (0.7978845608028654 + 0.7978845608028654 * 0.044715 * square))
        gate = 0.5 + 0.5 * inner
        act_ref[:, cols] = (hidden * gate).astype(bf16)
        slope_ref[:, cols] = gate + (0.5 * hidden) * (1.0 - inner * inner) * (
            0.7978845608028654 + 3.0 * 0.7978845608028654 * 0.044715 * square
        )


def front(normed, fc, bias, bias_spec, after=()):
    half, width = normed.shape
    units = fc.shape[1]
    step = 256
    block = pl.BlockSpec((step, units), lambda i: (i, 0))
    return pl.pallas_call(
        front_kernel,
        grid=(half // step,),
        in_specs=[
            pl.BlockSpec((step, width), lambda i: (i, 0)),
            once(fc.shape, (0, 0)),
            bias_spec,
        ]
        + unread(after),
        out_specs=[block] * 2,
        out_shape=[
            jax.ShapeDtypeStruct((half, units), bf16),
            jax.ShapeDtypeStruct((half, units), f32),
        ],
        compiler_params=params(10),
        cost_estimate=cost(2 * half * width * units, half * width * 10, half * units),
        name="mlp_front",
    )(normed, fc, bias, *after)


def rest_kernel(which_ref, act_ref, slope_ref, g_ref, fc_ref, proj_ref, *refs):
    feed_in, back_in = refs[:2]
    feed_ref, back_ref, grad_ref = refs[-3:]
    grad = g_ref[...]
    units = fc_ref.shape[1]
    step = min(units, 256)
    for at in range(0, units, step):
        cols = slice(at, at + step)
        grad_ref[:, cols] = (nt(grad, proj_ref[cols, :]) * slope_ref[:, cols]).astype(bf16)
    feed_ref[...] = nn(act_ref[...], proj_ref[...]) + feed_in[...]
    back_ref[...] = nt(grad_ref[...], fc_ref[...]) + back_in[...]


def rest(which, fronts, cotangent, fc, proj, sums, after=(), weight=1):
    half, units = fronts[0].shape
    width = fc.shape[0]
    step = 256
    count = half // step
    block = pl.BlockSpec((step, width), lambda i, w: (i, 0))
    return pl.pallas_call(
        rest_kernel,
        grid_spec=pltpu.PrefetchScalarGridSpec(
            num_scalar_prefetch=1,
            grid=(count,),
            in_specs=[pl.BlockSpec((step, units), lambda i, w: (i, 0))] * 2
            + [
                pl.BlockSpec((step, width), lambda i, w: (w[0] * count + i, 0)),
                once(fc.shape, (0, 0)),
                once(proj.shape, (0, 0)),
            ]
            + [block] * 2
            + unread(after),
            out_specs=[block] * 2,
            scratch_shapes=[pltpu.VMEM((step, units), bf16)],
        ),
        out_shape=[jax.ShapeDtypeStruct((half, width), f32)] * 2,
        compiler_params=params(14),
        cost_estimate=cost(
            weight * 6 * half * width * units, half * width * 16 + 4 * width * units
        ),
        name="mlp_rest",
    )(which, *fronts, cotangent, fc, proj, *sums, *after)


def norm_two_back_kernel(which_ref, g_ref, a_ref, b_ref, middle_ref, vec_ref, *refs):
    hat, scale = normalize(middle_ref[...])
    grad = (a_ref[...] + b_ref[...]) * vector(vec_ref, GAIN_TWO)
    refs[-1][...] = g_ref[...].astype(f32) + norm_back(grad, hat, scale)


def norm_two_back(which, cotangent, a, b, middle, vectors, after=()):
    half, width = a.shape
    step = 128
    count = half // step
    block = pl.BlockSpec((step, width), lambda i, w: (i, 0))
    return pl.pallas_call(
        norm_two_back_kernel,
        grid_spec=pltpu.PrefetchScalarGridSpec(
            num_scalar_prefetch=1,
            grid=(count,),
            in_specs=[
                pl.BlockSpec((step, width), lambda i, w: (w[0] * count + i, 0)),
                block,
                block,
                block,
                once(vectors.shape, (0, 0)),
            ]
            + unread(after),
            out_specs=block,
        ),
        out_shape=jax.ShapeDtypeStruct((half, width), f32),
        compiler_params=params(7),
        cost_estimate=cost(half * width * 20, half * width * 18),
        name="norm_two_back",
    )(which, cotangent, a, b, middle, vectors, *after)


def norm_one_back_kernel(which_ref, x_ref, upper_ref, vec_ref, a_ref, b_ref, *refs):
    hat, scale = normalize(x_ref[...].astype(f32))
    grad = (a_ref[...] + b_ref[...]) * vector(vec_ref, GAIN_ONE)
    refs[-2][...] = upper_ref[...] + norm_back(grad, hat, scale)
    refs[-1][...] = jnp.zeros_like(refs[-1])


def norm_one_back(which, x, upper, vectors, a, b, whole=(), after=()):
    half, width = upper.shape
    step = 128
    count = half // step
    block = pl.BlockSpec((step, width), lambda i, w: (i, 0))
    placed = pl.BlockSpec((step, width), lambda i, w: (w[0] * count + i, 0))
    return pl.pallas_call(
        norm_one_back_kernel,
        grid_spec=pltpu.PrefetchScalarGridSpec(
            num_scalar_prefetch=1,
            grid=(count,),
            in_specs=[placed, block, once(vectors.shape, (0, 0)), block, block]
            + unread(whole)
            + unread(after),
            out_specs=[placed, once((8, 128), (0, 0))],
        ),
        out_shape=[
            jax.ShapeDtypeStruct((2 * half, width), f32),
            jax.ShapeDtypeStruct((8, 128), f32),
        ],
        input_output_aliases={6: 0} if whole else {},
        compiler_params=params(6),
        cost_estimate=cost(half * width * 20, half * width * 18),
        name="norm_one_back",
    )(which, x, upper, vectors, a, b, *whole, *after)


def result_kernel(which_ref, a_ref, b_ref, middle_ref, vec_ref, *refs):
    half_ref, whole_ref, token_ref = refs[-3:]
    token_ref[...] = jnp.zeros_like(token_ref)
    result = middle_ref[...] + (a_ref[...] + b_ref[...]) + vector(vec_ref, PROJ_BIAS)
    half_ref[...] = result
    whole_ref[...] = result.astype(bf16)


def result_half(which, a, b, middle, vectors, after=(), weight=1):
    half, width = middle.shape
    step = 128
    count = half // step
    block = pl.BlockSpec((step, width), lambda i, w: (i, 0))
    placed = pl.BlockSpec((step, width), lambda i, w: (w[0] * count + i, 0))
    return pl.pallas_call(
        result_kernel,
        grid_spec=pltpu.PrefetchScalarGridSpec(
            num_scalar_prefetch=1,
            grid=(count,),
            in_specs=[block, block, block, once(vectors.shape, (0, 0))] + unread(after),
            out_specs=[block, placed, once((8, 128), (0, 0))],
        ),
        out_shape=[
            jax.ShapeDtypeStruct((half, width), f32),
            jax.ShapeDtypeStruct((2 * half, width), bf16),
            jax.ShapeDtypeStruct((8, 128), f32),
        ],
        compiler_params=params(6),
        cost_estimate=cost(weight * half * width * 2048, half * width * 18),
        name="result",
    )(which, a, b, middle, vectors, *after)


def place_kernel(which_ref, half_ref, *refs):
    refs[-2][...] = half_ref[...].astype(refs[-2].dtype)
    refs[-1][...] = jnp.zeros_like(refs[-1])


def placed_half(which, half_values, whole, after=()):
    half, width = half_values.shape
    step = 128
    count = half // step
    return pl.pallas_call(
        place_kernel,
        grid_spec=pltpu.PrefetchScalarGridSpec(
            num_scalar_prefetch=1,
            grid=(count,),
            in_specs=[pl.BlockSpec((step, width), lambda i, w: (i, 0))]
            + unread([whole])
            + unread(after),
            out_specs=[
                pl.BlockSpec((step, width), lambda i, w: (w[0] * count + i, 0)),
                once((8, 128), (0, 0)),
            ],
        ),
        out_shape=[
            jax.ShapeDtypeStruct(whole.shape, whole.dtype),
            jax.ShapeDtypeStruct((8, 128), f32),
        ],
        input_output_aliases={2: 0},
        compiler_params=params(3),
        cost_estimate=cost(0, half * width * 8),
        name="place",
    )(which, half_values, whole, *after)


def parts(values):
    high = values.astype(bf16)
    return high, (values - high.astype(f32)).astype(bf16)


def prefix_kernel(a_ref, b_ref, trunk_ref, embed_ref, w1_ref, *refs):
    w1_grad_ref, w2_grad_ref, b1_grad_ref, b2_grad_ref, embed_grad_ref = refs[-5:]
    columns = w2_grad_ref.shape[2]
    wide = w2_grad_ref.shape[1] * columns
    both = a_ref[:PAD, :] + b_ref[:PAD, :]
    kv, trunk = both[:, :wide], trunk_ref[...]
    pre = both[:, wide:] * (1.0 - trunk * trunk)
    pre_high, pre_low = parts(pre)
    embed = embed_ref[...]
    w1_grad_ref[...] = tn(
        jnp.concatenate([embed, embed], axis=0), jnp.concatenate([pre_high, pre_low], axis=0)
    )
    rows = nt(jnp.concatenate([pre_high, pre_low], axis=0), w1_ref[...])
    embed_grad_ref[...] = rows[:PAD] + rows[PAD:]
    b1_grad_ref[...] = jnp.sum(pre, axis=0, keepdims=True)
    b2_grad = jnp.sum(kv, axis=0, keepdims=True)
    trunk_high, trunk_low = parts(trunk)
    kv_high, kv_low = parts(kv)
    w2_grad = tn(
        jnp.concatenate([trunk_high, trunk_high, trunk_low], axis=0),
        jnp.concatenate([kv_high, kv_low, kv_high], axis=0),
    )
    for i in range(w2_grad_ref.shape[1]):
        cols = slice(i * columns, (i + 1) * columns)
        w2_grad_ref[:, i, :] = w2_grad[:, cols]
        b2_grad_ref[i : i + 1, :] = b2_grad[:, cols]


def prefix_grads(a, b, trunk, embed, w1, width, after=()):
    full, rank = w1.shape
    shapes = [(full, rank), (rank, 2, width), (1, rank), (2, width), (PAD, full)]
    return pl.pallas_call(
        prefix_kernel,
        grid=(1,),
        in_specs=[once(v.shape, (0, 0)) for v in (a, b, trunk, embed, w1)] + unread(after),
        out_specs=[once(shape, (0,) * len(shape)) for shape in shapes],
        out_shape=[jax.ShapeDtypeStruct(shape, f32) for shape in shapes],
        compiler_params=params(16),
        cost_estimate=cost(0, full * rank * 8),
        name="prefix_grads",
    )(a, b, trunk, embed, w1, *after)


def shards(
    group,
    copies,
    tokens,
    cotangent,
    seg_lengths,
    pad_counts,
    ln1_gain,
    ln1_shift,
    qkv_weight,
    qkv_bias,
    out_weight,
    out_bias,
    ln2_gain,
    ln2_shift,
    fc_weight,
    fc_bias,
    proj_weight,
    proj_bias,
    prefix_embed,
    reparam_w1,
    reparam_b1,
    reparam_w2,
    reparam_b2,
):
    rows_here, length, width = tokens.shape
    assert rows_here == 1 and copies % RING == 0
    local_width = qkv_weight.shape[2]
    prefix = prefix_embed.shape[0]
    half = length // 2
    parcel = Parcel(length, local_width, width)
    place = lax.axis_index("tensor")
    core = place % CORES
    mine = core.reshape(1).astype(jnp.int32)
    theirs = 1 - mine
    none = mine * 0
    far_shifts = [CORES * s for s in range(1, group // CORES)]

    def to_core(values):
        return lax.ppermute(values, "tensor", [(t, t ^ 1) for t in range(group)])

    def to_far(values):
        return [
            lax.ppermute(values, "tensor", [(t, (t + shift) % group) for t in range(group)])
            for shift in far_shifts
        ]

    def swapped(values, axis, size, step):
        return values + lax.ppermute(values, axis, [(i, i ^ step) for i in range(size)])

    ring = list(range(0, RING, 2)) + list(range(RING - 1, 0, -2))
    member = lax.axis_index("dp") % RING
    order = jnp.where(member % 2 == 0, member // 2, RING - 1 - member // 2)
    here = order.reshape(1).astype(jnp.int32)
    across = (here + RING // 2) % RING
    hops = RING // 2 - 1

    def along(values, step):
        hop = [
            (base + ring[i], base + ring[(i + step) % RING])
            for base in range(0, copies, RING)
            for i in range(RING)
        ]
        return lax.ppermute(values, "dp", hop)

    def hop(rings):
        for levels in rings:
            up, down = levels[-1]
            levels.append((along(up, 1), along(down, -1)))

    def last(rings):
        return [piece for levels in rings for piece in levels[-1]]

    def hold(rings, after):
        for levels in rings:
            up, down = levels[-1]
            if up is down:
                up = down = held([up], after)[0]
            else:
                up, down = held([up, down], after)
            levels[-1] = (up, down)

    def starting(pieces):
        return [[(piece, piece)] for piece in pieces]

    def rebuilt(levels, facing, spec, folded=False, after=()):
        shifts, pieces = [0], [levels[0][0]]
        for number, (up, down) in enumerate(levels[1:]):
            shifts += [-1 - number, number + 1]
            pieces += [up, down]
        return assembled(here, shifts + [RING // 2], pieces + [facing], [spec], folded, after)

    x = tokens.reshape(length, width)
    grad_out = cotangent.reshape(length, width)
    lengths = seg_lengths.reshape(-1)
    qkv_w = jnp.transpose(qkv_weight, (1, 0, 2))
    vectors = jnp.stack([ln1_gain, ln1_shift, out_bias, ln2_gain, ln2_shift, proj_bias])
    vectors = jnp.pad(vectors, ((0, 2), (0, 0))).astype(f32)

    (piece_fc,) = picked([here], [fc_weight])
    near_fc = to_far(piece_fc)
    (piece_out,) = picked([here], [out_weight], [piece_fc])
    near_out = to_far(piece_out)
    (piece_proj,) = picked([here], [proj_weight], [piece_out])
    near_proj = to_far(piece_proj)
    ring_out, ring_fc, ring_proj = starting(near_out), starting(near_fc), starting(near_proj)

    fc_rows = fc_bias.astype(f32).reshape(-1, local_width)
    biases = jnp.concatenate(
        [
            jnp.pad(qkv_bias.astype(f32), ((0, 5), (0, 0))),
            jnp.pad(fc_rows, ((0, 8 - fc_rows.shape[0]), (0, 0))),
        ],
        axis=0,
    )
    qkv_bias_spec = once((8, local_width), (0, 0))
    fc_bias_spec = once((8, local_width), (1, 0))
    qkv, normed_one = project(True, in_hbm([x])[0], vectors, qkv_w, biases, qkv_bias_spec)

    embed = prefix_embed.astype(f32)
    trunk_weight = reparam_w1.astype(f32)
    head_weight = reparam_w2.astype(f32)
    trunk = jnp.tanh(jnp.dot(embed, trunk_weight, precision=highest) + reparam_b1.astype(f32))
    kv_values = jnp.einsum(
        "pr,rtd->ptd", trunk, head_weight, precision=highest
    ) + reparam_b2.astype(f32)
    flat_kv = jnp.pad(kv_values, ((0, PAD - prefix), (0, 0), (0, 0)))
    prefix_kv = jnp.concatenate([flat_kv[:, 0], flat_kv[:, 1]], axis=0)

    hold(ring_fc, [qkv])
    fc_held = last(ring_fc)
    hop(ring_fc)
    hold(ring_out, [qkv])
    out_held = last(ring_out)
    hop(ring_out)
    out, token = attend(
        prefix, parcel, lengths, pad_counts, qkv, prefix_kv, biases, fc_held + out_held
    )
    out = pack(across, parcel, out, out_weight, last(ring_fc) + last(ring_out))
    out = held([out], [token])[0]
    far_out_parcel = to_far(out)
    hold(ring_out, [out])
    out_held = last(ring_out)
    hop(ring_out)
    hold(ring_proj, out_held)
    hop(ring_proj)
    second_out = last(ring_out)
    hop(ring_out)
    hold(ring_fc, last(ring_proj) + second_out)
    hop(ring_fc)
    hold(ring_proj, last(ring_out))
    hop(ring_proj)
    across_fc, across_proj, piece_qkv, across_qkv = picked(
        [across, across, here, across], [fc_weight, proj_weight, qkv_w, qkv_w], last(ring_out)
    )
    far_places = [-hops, hops]
    pieces_qkv = joined(
        [(here + place + RING) % RING for place in far_places], qkv_w, [piece_qkv]
    )
    own_grads = through(grad_out, proj_weight, [piece_qkv])
    own_token = own_grads
    far_out = [
        rebuilt(levels, far, parcel.part(length, parcel.piece), True, [pieces_qkv, own_token])
        for levels, far in zip(ring_out, far_out_parcel)
    ]
    lefts = [out] + far_out_parcel
    rights = [out_weight] + far_out
    send = half_product(theirs, half, lefts, rights, last(ring_fc))
    received = to_core(send)
    keep = half_product(mine, half, lefts, rights, [send], KEEP)
    facing_fc = to_far(held([across_fc], last(ring_fc))[0])
    hold(ring_fc, last(ring_proj))
    fc_held = last(ring_fc)
    hop(ring_fc)
    middle, normed = norm_two(mine, x, [keep, received], vectors, fc_held)
    other_normed = to_core(normed)
    own = (fc_weight, proj_weight, biases, fc_bias_spec)
    keep_sums = mlp(mine, normed, own_grads, *own, (), OWN)
    hold(ring_proj, [other_normed])
    hop(ring_proj)
    near_qkv = to_far(held([piece_qkv], [normed])[0])
    facing_proj = to_far(held([across_proj], facing_fc + [keep_sums[0]])[0])
    fc_spec, proj_spec = once(piece_fc.shape, (0, 0)), once(piece_proj.shape, (0, 0))
    send_sums = mlp(
        theirs, other_normed, own_grads, *own, [keep_sums[0]] + last(ring_fc)
    )
    ring_qkv = starting(near_qkv)
    hold(ring_qkv, [send_sums[0]] + last(ring_fc))
    hop(ring_qkv)
    far_fc = [
        rebuilt(levels, piece, fc_spec, False, [send_sums[0]])
        for levels, piece in zip(ring_fc, facing_fc)
    ]
    far_bias_spec = parcel.part(parcel.bias + 8, 8)
    other_fronts, fronts = [], []
    for fc, far in zip(far_fc, far_out_parcel):
        other_fronts.append(front(other_normed, fc, far, far_bias_spec))
        fronts.append(front(normed, fc, far, far_bias_spec, other_fronts[-1][:1]))
    far_proj = [
        rebuilt(levels, piece, proj_spec, False, [ahead[1] for ahead in fronts])
        for levels, piece in zip(ring_proj, facing_proj)
    ]
    for ahead, fc, proj in zip(other_fronts, far_fc, far_proj):
        send_sums = rest(theirs, ahead, grad_out, fc, proj, send_sums, (), LIGHT)
    back_received = to_core(send_sums[1])
    for ahead, fc, proj in zip(fronts, far_fc, far_proj):
        keep_sums = rest(mine, ahead, grad_out, fc, proj, keep_sums, [send_sums[0]], FAR)
    facing_qkv = to_far(held([across_qkv], near_qkv + [send_sums[0]])[0])
    upper = norm_two_back(
        mine, grad_out, keep_sums[1], back_received, middle, vectors
    )
    hold(ring_qkv, [upper])
    q_held = last(ring_qkv)
    hop(ring_qkv)
    other_upper = to_core(upper)
    feed_received = to_core(send_sums[0])
    result, mixed, result_token = result_half(
        mine, keep_sums[0], feed_received, middle, vectors, q_held + facing_qkv, FAR
    )
    other_result = to_core(result)
    ends_qkv = to_far(held([pieces_qkv], [upper])[0])

    grads_far = heads_back(
        mine, upper, other_upper, [out_weight] + far_out, [result_token]
    )
    dqkv, grad_keys, grad_vals = attend_back(
        prefix,
        parcel,
        lengths,
        pad_counts,
        qkv,
        grads_far[0],
        out,
        (),
        LIGHT,
    )

    grad_keys, grad_vals = held([grad_keys, grad_vals], last(ring_qkv))
    grad_here = jnp.concatenate([grad_keys, grad_vals], axis=1)
    flat_head = jnp.transpose(head_weight, (1, 2, 0)).reshape(2 * local_width, -1)
    trunk_here = jnp.dot(grad_here, flat_head, precision=highest)
    for_tensor = [("tensor", group, 1 << i) for i in range(group.bit_length() - 1)]
    for_dp = [("dp", copies, 1 << i) for i in reversed(range(copies.bit_length() - 1))]
    mixed, token = placed_half(theirs, other_result, mixed, [dqkv])
    far_qkv = []
    for levels, facing, pieces in zip(ring_qkv, facing_qkv, ends_qkv):
        shifts, found = [0], [levels[0][0]]
        for number, ends in enumerate(levels[1:]):
            shifts += [-1 - number, number + 1]
            found += list(ends)
        shifts, found = shifts + [RING // 2], found + [facing]
        specs = [once(piece_qkv.shape, (i, 0, 0)) for i in range(len(far_places))]
        far_qkv.append(
            assembled(here, shifts + far_places, found + [pieces] * len(far_places), specs, False, [token])
        )
    qkvs = [qkv_w] + far_qkv
    trunk_here = swapped(trunk_here, *for_tensor[0])
    far_projected = [
        project(
            False,
            in_hbm([normed_one])[0],
            vectors,
            weight,
            far,
            parcel.part(parcel.bias, 8),
            [trunk_here],
        )[0]
        for weight, far in zip(far_qkv, far_out_parcel)
    ]
    for step in for_tensor[1:]:
        trunk_here = swapped(trunk_here, *step)
    grads = [dqkv]
    for number, far in enumerate(far_out_parcel):
        found = attend_back(
            prefix,
            parcel,
            lengths,
            pad_counts,
            far_projected[number],
            grads_far[1 + number],
            far,
            [trunk_here],
            LIGHT,
        )
        grads.append(found[0])
    both = jnp.concatenate([grad_here, trunk_here], axis=1)
    both = swapped(held([both], far_projected)[0], *for_dp[0])
    both = held([both], grads[-1:])[0]
    send_one = unproject(theirs, grads, qkvs, [both])
    received_one = to_core(send_one)
    both = swapped(both, *for_dp[1])
    keep_one = unproject(mine, grads, qkvs, [send_one, both])
    received_two = to_core(keep_one)
    for step in for_dp[2:-1]:
        both = swapped(both, *step)
    last_step = for_dp[-1]
    other_both = lax.ppermute(both, "dp", [(i, i ^ last_step[2]) for i in range(copies)])
    input_grad, token = norm_one_back(mine, x, upper, vectors, keep_one, received_one)
    w1_grad, w2_grad, b1_grad, b2_grad, embed_grad = prefix_grads(
        both,
        other_both,
        jnp.pad(trunk, ((0, PAD - prefix), (0, 0))),
        jnp.pad(prefix_embed, ((0, PAD - prefix), (0, 0))),
        reparam_w1,
        local_width,
        [token],
    )
    input_grad, _ = norm_one_back(
        theirs, x, other_upper, vectors, send_one, received_two, [input_grad]
    )
    b1_grad, embed_grad = b1_grad.reshape(-1), embed_grad[:prefix]
    mixed, input_grad = mixed.reshape(tokens.shape), input_grad.reshape(tokens.shape)
    return (mixed, input_grad, embed_grad, w1_grad, b1_grad, w2_grad, b2_grad, kv_values)


def solution(mesh):
    return jax.shard_map(
        functools.partial(shards, mesh.shape["tensor"], mesh.shape["dp"]),
        mesh=mesh,
        in_specs=(
            P("dp", None, None),
            P("dp", None, None),
            P("dp", None),
            P("dp"),
            P(),
            P(),
            P(None, None, "tensor"),
            P(None, "tensor"),
            P("tensor", None),
            P(),
            P(),
            P(),
            P(None, "tensor"),
            P("tensor"),
            P("tensor", None),
            P(),
            P(),
            P(),
            P(),
            P(None, None, "tensor"),
            P(None, "tensor"),
        ),
        out_specs=(
            P("dp", None, None),
            P("dp", None, None),
            P(),
            P(),
            P(),
            P(None, None, "tensor"),
            P(None, "tensor"),
            P(None, None, "tensor"),
        ),
        check_vma=False,
    )
```
